32 devices in a mesh: table: 8 (over z, y), ctx: 4 (over x, core).
Axes of the slice: x: 2, y: 2, z: 4, core: 2. Of those that a mesh axis runs over, the one named last changes fastest.
Arguments:
- table: bfloat16 [16384, 512], P(('table', 'ctx')), may hold values from -6 to 6
- item_owner: int32 [8192, 2], P(('table', 'ctx')), may hold values from 0 to 31, as said below
- item_row: int32 [8192, 2], P(('table', 'ctx')), may hold values from 0 to 511
- segment_ids: int32 [8, 1024], P('table', 'ctx'), may hold values from 0 to 1, never falling along the last dimension, each value on 1 to 896 neighbouring positions
- w_in: bfloat16 [512, 2048], replicated, may hold values from -0.5 to 0.5
- w_out: bfloat16 [512, 512], replicated, may hold values from -0.25 to 0.25
- cotangent: bfloat16 [8192, 512], P(('table', 'ctx')), may hold values from -6 to 6
Outputs:
- layer_out: bfloat16 [8192, 512], P(('table', 'ctx'))
- row_grad: float32 [16384, 512], P(('table', 'ctx'))
The draws below stay inside these ranges and needn't reach their ends.
Inputs may be any that keep to these rules, and one draw needn't show every extreme that they name: `item_owner`: among the 512 ids of one device's events no owner is named more than 32 times; one owner, the same for every device, is named exactly 32 times by every device.
All inputs are finite; a program needn't handle non-finite values.
Results may differ from the reference program's by a relative error of at most 0.0095.
Values may be sent and summed in bfloat16 or wider, within the bound.
No kernel may reach another device: no remote copies, remote signals or barrier semaphores. Data moves between devices by JAX's collectives and lax.ppermute only.
A program may use at most 64 MiB of HBM per device.

```python
import math
import jax
import jax.numpy as jnp
import numpy as np
from jax import lax

D = 512
HEADS = 4
HEAD_DIM = 128
NIDS = 2
NSEQ = 2
TAB_DEV = 512
GROUPS = 8
CTX_LEN = 1024
MAXLEN = 896
TOKENS = 8192
OWNERS = 32
ROWS = 16384
NID_DEV = 512
CAP = 32


def draw_item_owner(key, part):
    busiest = jax.random.randint(jax.random.fold_in(key, 7), (), 0, OWNERS).astype(jnp.int32)
    spread = jnp.arange(NID_DEV - CAP, dtype=jnp.int32)
    others = (busiest + 1 + spread % (OWNERS - 1)) % OWNERS
    listed = jnp.concatenate([jnp.full((CAP,), busiest, jnp.int32), others.astype(jnp.int32)])

    def shuffle(device_key):
        return jax.random.permutation(device_key, listed)
    key_list = jax.random.split(jax.random.fold_in(key, 11), OWNERS)
    return jax.vmap(shuffle)(key_list).reshape(TOKENS, NIDS)


def draw_w_in(key, part):
    noise_key = jax.random.fold_in(key, 3)
    shift_key = jax.random.fold_in(key, 5)
    weight_scale = D ** (-0.5)
    base_noise = jnp.clip(jax.random.normal(noise_key, (D, 4 * D), jnp.float32), -5.0, 5.0) * weight_scale
    column_lift = jnp.full((1, 4 * D), 0.6, jnp.float32)
    shift_dir = jnp.clip(jax.random.normal(shift_key, (D, 1), jnp.float32), -4.0, 4.0) * weight_scale
    return jnp.clip(base_noise + shift_dir * column_lift, -0.5, 0.5).astype(jnp.bfloat16)


def touch_ends(values, key, smallest, largest):
    dims = values.shape
    index_at = [jax.random.randint(jax.random.fold_in(key, axis), (), 0, dims[axis]) for axis in range(len(dims))]
    values = values.at[tuple(index_at)].set(smallest)
    longest = dims.index(max(dims))
    index_at[longest] = (index_at[longest] + 1) % dims[longest]
    return values.at[tuple(index_at)].set(largest)


def block_levels(rng, dims, pieces, smallest, largest):
    factor_of = 1.0
    for position, blocks in pieces:
        draws = jax.random.uniform(jax.random.fold_in(jax.random.fold_in(rng, 6), position), (blocks,), jnp.float32, smallest / len(pieces), largest / len(pieces))
        factor_of = factor_of * jnp.repeat(jnp.exp(draws), dims[position] // blocks).reshape((-1,) + (1,) * (len(dims) - 1 - position))
    return factor_of


def split_up(number_of, total, most, slope):
    portions = [(1 << 20) // math.isqrt(standing ** slope) + 1 for standing in range(2, number_of + 1)]
    rest, counts = total - most - (number_of - 1), [1] * (number_of - 1)
    while rest > 0:
        movable = [i for i in range(number_of - 1) if counts[i] < most]
        mass, budget = sum([portions[i] for i in movable]), rest
        for i in movable:
            more = min(most - counts[i], max(1, budget * portions[i] // mass), rest)
            counts[i] = counts[i] + more
            rest = rest - more
    return np.array([most] + counts)


def ragged(rng, number_of, total, most, slope):
    if number_of == 2:
        one = jax.random.randint(rng, (), max(1, total - most), min(most, total - 1) + 1)
        return jnp.stack([one, total - one])
    tallies = jnp.asarray(split_up(number_of, total, most, slope), jnp.int32)
    couples = (number_of - 1) // 2
    donor, receiver = tallies[1:1 + 2 * couples:2], tallies[2:2 + 2 * couples:2]
    slack = jnp.minimum(donor - 1, most - receiver)
    moved = jax.random.randint(jax.random.fold_in(rng, 1), (couples,), 0, 1 << 20) % (slack + 1)
    tallies = tallies.at[1:1 + 2 * couples:2].set(donor - moved).at[2:2 + 2 * couples:2].set(receiver + moved)
    return tallies[jax.random.permutation(jax.random.fold_in(rng, 2), number_of)]


def gaussian(own_key, dims, width, limit, pieces=(), held_as=jnp.bfloat16):
    drawn = jax.random.normal(own_key, dims, jnp.float32) * width
    if len(pieces) > 0:
        drawn = block_levels(own_key, dims, pieces, -0.22, 0.18) * drawn
    return jnp.clip(drawn, min=-limit, max=limit).astype(held_as)


def setup_inputs(seed: int = 0) -> dict:
    keys = jax.random.split(jax.random.key(seed), 8)
    table = gaussian(keys[0], (ROWS, D), 1.0, 6.0, ((0, 32),))
    item_owner = draw_item_owner(jax.random.fold_in(keys[7], 71), 0)
    item_row = touch_ends(jax.random.randint(keys[2], (TOKENS, NIDS), 0, TAB_DEV), jax.random.fold_in(keys[2], 1), 0, TAB_DEV - 1).astype(jnp.int32)
    segment_ids = jax.vmap(lambda own: jnp.searchsorted(jnp.cumsum(ragged(own, NSEQ, CTX_LEN, MAXLEN, 0)), jnp.arange(CTX_LEN), side="right"))(jax.random.split(keys[3], GROUPS)).reshape((GROUPS, CTX_LEN)).astype(jnp.int32)
    w_in = draw_w_in(jax.random.fold_in(keys[7], 71), 0)
    w_out = gaussian(keys[5], (D, D), D ** -0.5, 0.25)
    cotangent = gaussian(keys[6], (TOKENS, D), 1.0, 6.0, ((0, 32),))
    return dict(table=table, item_owner=item_owner, item_row=item_row, segment_ids=segment_ids, w_in=w_in, w_out=w_out, cotangent=cotangent)


EPS = 1e-06

def silu_grad(values):
    sigma = jax.nn.sigmoid(values)
    return sigma * (1.0 + values * (1.0 - sigma))

def normalize(values):
    centred = values - lax.optimization_barrier(jnp.mean(values, -1, keepdims=True))
    inverse = lax.rsqrt(lax.optimization_barrier(jnp.mean(centred * centred, -1, keepdims=True)) + EPS)
    return (centred * inverse, inverse)

def norm_back(grad_norm, normed, inverse):
    mean_grad = lax.optimization_barrier(jnp.mean(grad_norm, -1, keepdims=True))
    mean_cross = lax.optimization_barrier(jnp.mean(grad_norm * normed, -1, keepdims=True))
    return (grad_norm - mean_grad - normed * mean_cross) * inverse

def split_heads(values):
    return values.astype(jnp.float32).reshape(values.shape[0], HEADS, HEAD_DIM)

def visible(query_pos, query_seg, key_pos, key_seg):
    return (query_seg[:, None] == key_seg[None, :]) & (key_pos[None, :] <= query_pos[:, None])

def layer_group(embedded, segments, cotangent, w_in, w_out):
    length = embedded.shape[0]
    scale = HEAD_DIM ** (-0.5)
    positions = jnp.arange(length, dtype=jnp.int32)
    normed, inverse = normalize(embedded.astype(jnp.float32))
    before = jnp.dot(normed.astype(jnp.bfloat16), w_in, preferred_element_type=jnp.float32)
    proj = jax.nn.silu(before).astype(jnp.bfloat16)
    gate = proj[:, :D]
    values = proj[:, D:2 * D]
    queries = proj[:, 2 * D:3 * D]
    keys_in = proj[:, 3 * D:]
    mask = visible(positions, segments, positions, segments)[None]
    raw = jnp.einsum('qhd,khd->hqk', split_heads(queries), split_heads(keys_in)) * scale
    weights = jnp.where(mask, jax.nn.silu(raw), 0.0).astype(jnp.bfloat16)
    attended = jnp.einsum('hqk,khd->qhd', weights.astype(jnp.float32), split_heads(values)).reshape(length, D)
    att_norm, att_inverse = normalize(attended)
    mixed = (att_norm * gate.astype(jnp.float32)).astype(jnp.bfloat16)
    output = (embedded.astype(jnp.float32) + jnp.dot(mixed, w_out, preferred_element_type=jnp.float32)).astype(jnp.bfloat16)
    grad_mixed = jnp.dot(cotangent, w_out.T, preferred_element_type=jnp.float32)
    grad_gate = grad_mixed * att_norm
    grad_norm = grad_mixed * gate.astype(jnp.float32)
    grad_att = norm_back(grad_norm, att_norm, att_inverse).astype(jnp.bfloat16)
    grad_weights = jnp.einsum('qhd,khd->hqk', split_heads(grad_att), split_heads(values))
    grad_raw = (jnp.where(mask, grad_weights * silu_grad(raw), 0.0) * scale).astype(jnp.bfloat16)
    grad_queries = jnp.einsum('hqk,khd->qhd', grad_raw.astype(jnp.float32), split_heads(keys_in)).reshape(length, D)
    grad_keys = jnp.einsum('hqk,qhd->khd', grad_raw.astype(jnp.float32), split_heads(queries)).reshape(length, D)
    grad_values = jnp.einsum('hqk,qhd->khd', weights.astype(jnp.float32), split_heads(grad_att)).reshape(length, D)
    joined = jnp.concatenate([grad_gate, grad_values, grad_queries, grad_keys], 1)
    grad_proj = (joined * silu_grad(before)).astype(jnp.bfloat16)
    grad_normed = jnp.dot(grad_proj, w_in.T, preferred_element_type=jnp.float32)
    grad_embedded = norm_back(grad_normed, normed, inverse) + cotangent.astype(jnp.float32)
    return (output, grad_embedded)

def reference(table, item_owner, item_row, segment_ids, w_in, w_out, cotangent):
    flat_ids = (item_owner * TAB_DEV + item_row).reshape(-1).astype(jnp.int32)
    rows = table[flat_ids].astype(jnp.float32).reshape(TOKENS, NIDS, D)
    embedded = lax.optimization_barrier(jnp.sum(rows, 1)).astype(jnp.bfloat16)

    def one_group(operands):
        return layer_group(operands[0], operands[1], operands[2], w_in, w_out)
    outputs, grads = lax.map(one_group, (embedded.reshape(GROUPS, CTX_LEN, D), segment_ids, cotangent.reshape(GROUPS, CTX_LEN, D)))
    spread = jnp.broadcast_to(grads.reshape(TOKENS, 1, D), (TOKENS, NIDS, D)).reshape(TOKENS * NIDS, D)
    row_grad = jax.ops.segment_sum(spread, flat_ids, num_segments=ROWS)
    return (outputs.reshape(TOKENS, D), row_grad)
```

```python
import functools

import jax
import jax.numpy as jnp
from jax import lax
from jax.experimental import pallas as pl
from jax.experimental.pallas import tpu as pltpu
from jax.sharding import PartitionSpec as P

HEADS = 4
HEAD_DIM = 128
NIDS = 2
EPS = 1e-06
VMEM_LIMIT = 50 * 1024 * 1024

F32 = jnp.float32
BF16 = jnp.bfloat16


def dot(a, b):
    return jnp.dot(a, b, preferred_element_type=F32)


def dot_nt(a, b):
    return lax.dot_general(a, b, (((1,), (1,)), ((), ())), preferred_element_type=F32)


def iota(shape, dim):
    return lax.broadcasted_iota(jnp.int32, shape, dim)


def normalize(values):
    centred = values - jnp.mean(values, -1, keepdims=True)
    inverse = lax.rsqrt(jnp.mean(centred * centred, -1, keepdims=True) + EPS)
    return centred * inverse, inverse


def norm_back(grad_norm, normed, inverse):
    mean_grad = jnp.mean(grad_norm, -1, keepdims=True)
    mean_cross = jnp.mean(grad_norm * normed, -1, keepdims=True)
    return (grad_norm - mean_grad - normed * mean_cross) * inverse


def split_exact(values):
    return (values >> 4).astype(F32).astype(BF16), (values & 15).astype(F32).astype(BF16)


def slots_kernel(capacity, owner_ref, row_ref, slots_ref, wanted_ref):
    events = owner_ref.shape[1]
    owners = wanted_ref.shape[0]
    owner = jnp.concatenate([owner_ref[k : k + 1, :] for k in range(NIDS)], 1)
    row = jnp.concatenate([row_ref[k : k + 1, :] for k in range(NIDS)], 1)
    ids = owner.shape[1]
    named = iota((owners, ids), 0) == owner
    named_f = jnp.where(named, 1.0, 0.0)
    before = jnp.where(iota((ids, ids), 0) < iota((ids, ids), 1), 1.0, 0.0).astype(BF16)
    earlier = dot(named_f.astype(BF16), before)
    rank = jnp.sum(earlier * named_f, 0, keepdims=True).astype(jnp.int32)
    slot = owner * capacity + rank
    slots_ref[...] = jnp.full(slots_ref.shape, -1, jnp.int32)
    for k in range(NIDS):
        slots_ref[k : k + 1, :] = slot[:, k * events : (k + 1) * events]
    ranked = jnp.where(iota((capacity, ids), 0) == rank, 1.0, 0.0).astype(BF16)
    high, low = (row >> 4).astype(F32), (row & 15).astype(F32)
    wanted = 16.0 * dot_nt((named_f * high).astype(BF16), ranked) + dot_nt(
        (named_f * low).astype(BF16), ranked
    )
    wanted_ref[...] = wanted.astype(jnp.int32)


def select_kernel(asked_ref, table_ref, out_ref):
    owners, capacity = asked_ref.shape
    rows = table_ref.shape[0]
    slots = owners * capacity
    high, low = split_exact(asked_ref[...])
    source = jnp.where(
        iota((slots, owners), 0) // capacity == iota((slots, owners), 1), 1.0, 0.0
    ).astype(BF16)
    spread = 16.0 * dot(source, high) + dot(source, low)
    mine = iota((slots, capacity), 0) % capacity == iota((slots, capacity), 1)
    asked = jnp.sum(jnp.where(mine, spread, 0.0), 1, keepdims=True).astype(jnp.int32)
    chosen = jnp.where(iota((slots, rows), 1) == asked, 1.0, 0.0).astype(BF16)
    out_ref[...] = dot(chosen, table_ref[...]).astype(BF16)


def embed_kernel(slots_ref, fetched_ref, out_ref):
    events = out_ref.shape[0]
    slots = fetched_ref.shape[0]
    column = jnp.transpose(slots_ref[...])
    lane = iota((events, slots), 1)
    hit = lane == column[:, 0:1]
    for k in range(1, NIDS):
        hit = hit | (lane == column[:, k : k + 1])
    picked = jnp.where(hit, 1.0, 0.0).astype(BF16)
    out_ref[...] = dot(picked, fetched_ref[...]).astype(BF16)


def collect_kernel(asked_ref, returned_ref, out_ref):
    owners, capacity = asked_ref.shape
    rows = out_ref.shape[0]
    slots = owners * capacity
    high, low = split_exact(asked_ref[...])
    place = jnp.where(
        iota((capacity, slots), 1) % capacity == iota((capacity, slots), 0), 1.0, 0.0
    ).astype(BF16)
    spread = 16.0 * dot(high, place) + dot(low, place)
    mine = iota((owners, slots), 1) // capacity == iota((owners, slots), 0)
    asked = jnp.sum(jnp.where(mine, spread, 0.0), 0, keepdims=True).astype(jnp.int32)
    chosen = jnp.where(iota((rows, slots), 0) == asked, 1.0, 0.0).astype(BF16)
    out_ref[...] = dot(chosen, returned_ref[...])


def layer_kernel(count, *refs):
    index_ref = refs[0]
    slots_ref = refs[1]
    emb_refs = refs[2 : 2 + count]
    cot_refs = refs[2 + count : 2 + 2 * count]
    seg_refs = refs[2 + 2 * count : 2 + 3 * count]
    w_in_ref, w_out_ref = refs[2 + 3 * count : 4 + 3 * count]
    out_ref, grad_ref = refs[4 + 3 * count : 6 + 3 * count]
    (
        proj_ref,
        slope_ref,
        cot_ref,
        segc_ref,
        segr_ref,
        att_ref,
        gatt_ref,
        join_ref,
    ) = refs[6 + 3 * count :]
    events, width = out_ref.shape
    half_scale = 0.5 * HEAD_DIM ** (-0.5)
    scale = HEAD_DIM ** (-0.5)
    own = index_ref[0]

    for t in range(count):
        place = index_ref[t]
        normed, _ = normalize(emb_refs[t][...].astype(F32))
        normed = normed.astype(BF16)
        for block in range(4):
            columns = slice(block * width, (block + 1) * width)
            before = dot(normed, w_in_ref[:, columns])
            half = 0.5 * before
            bend = jnp.tanh(half)
            value = half + half * bend
            proj_ref[place, :, columns] = value.astype(BF16)
            if t == 0:
                sigma = 0.5 + 0.5 * bend
                slope_ref[:, columns] = sigma + value - value * sigma
        cot_ref[place] = cot_refs[t][...]
        seg = jnp.broadcast_to(seg_refs[t][...], (8, events))
        segr_ref[place] = seg
        segc_ref[place] = jnp.broadcast_to(jnp.transpose(seg)[:, 0:1], segc_ref.shape[1:])

    def head(part, h):
        return slice(part * width + h * HEAD_DIM, part * width + (h + 1) * HEAD_DIM)

    def forward(i, _):
        att_ref[...] = jnp.zeros_like(att_ref)

        def pair(j, _):
            mask = (segc_ref[i][:, 0:1] == segr_ref[j][0:1, :]) & (
                iota((events, events), 0) + (i - j) * events >= iota((events, events), 1)
            )
            for h in range(HEADS):
                raw = dot_nt(proj_ref[i, :, head(2, h)], proj_ref[j, :, head(3, h)])
                half = raw * half_scale
                value = half + half * jnp.tanh(half)
                weights = jnp.where(mask, value, 0.0).astype(BF16)
                columns = slice(h * HEAD_DIM, (h + 1) * HEAD_DIM)
                att_ref[:, columns] += dot(weights, proj_ref[j, :, head(1, h)])
            return 0

        lax.fori_loop(0, i + 1, pair, 0)
        att_norm, att_inverse = normalize(att_ref[...])
        gate = proj_ref[i, :, 0:width].astype(F32)
        grad_mixed = dot_nt(cot_ref[i], w_out_ref[...])
        grad_norm = grad_mixed * gate
        gatt_ref[i] = norm_back(grad_norm, att_norm, att_inverse).astype(BF16)

        @pl.when(i == own)
        def _():
            mixed = (att_norm * gate).astype(BF16)
            out_ref[...] = (emb_refs[0][...].astype(F32) + dot(mixed, w_out_ref[...])).astype(BF16)
            join_ref[:, 0:width] = grad_mixed * att_norm

        return 0

    lax.fori_loop(own, count, forward, 0)
    join_ref[:, width:] = jnp.zeros((events, 3 * width), F32)

    def query_side(j, _):
        mask = (segc_ref[own][:, 0:1] == segr_ref[j][0:1, :]) & (
            iota((events, events), 0) + (own - j) * events >= iota((events, events), 1)
        )
        for h in range(HEADS):
            keys = proj_ref[j, :, head(3, h)]
            raw = dot_nt(proj_ref[own, :, head(2, h)], keys)
            half = raw * half_scale
            bend = jnp.tanh(half)
            value = half + half * bend
            sigma = 0.5 + 0.5 * bend
            slope = sigma + value - value * sigma
            columns = slice(h * HEAD_DIM, (h + 1) * HEAD_DIM)
            grad_weights = dot_nt(gatt_ref[own, :, columns], proj_ref[j, :, head(1, h)])
            grad_raw = jnp.where(mask, grad_weights * slope * scale, 0.0).astype(BF16)
            join_ref[:, head(2, h)] += dot(grad_raw, keys)
        return 0

    lax.fori_loop(0, own + 1, query_side, 0)

    def key_side(i, _):
        mask = (segc_ref[own][:, 0:1] == segr_ref[i][0:1, :]) & (
            iota((events, events), 0) <= iota((events, events), 1) + (i - own) * events
        )
        for h in range(HEADS):
            queries = proj_ref[i, :, head(2, h)]
            raw = dot_nt(proj_ref[own, :, head(3, h)], queries)
            half = raw * half_scale
            bend = jnp.tanh(half)
            value = half + half * bend
            sigma = 0.5 + 0.5 * bend
            slope = sigma + value - value * sigma
            columns = slice(h * HEAD_DIM, (h + 1) * HEAD_DIM)
            grad_att = gatt_ref[i, :, columns]
            grad_weights = dot_nt(proj_ref[own, :, head(1, h)], grad_att)
            grad_raw = jnp.where(mask, grad_weights * slope * scale, 0.0).astype(BF16)
            weights = jnp.where(mask, value, 0.0).astype(BF16)
            join_ref[:, head(3, h)] += dot(grad_raw, queries)
            join_ref[:, head(1, h)] += dot(weights, grad_att)
        return 0

    lax.fori_loop(own, count, key_side, 0)

    grad_proj = (join_ref[...] * slope_ref[...]).astype(BF16)
    grad_normed = dot_nt(grad_proj, w_in_ref[...])
    normed, inverse = normalize(emb_refs[0][...].astype(F32))
    grad = norm_back(grad_normed, normed, inverse) + cot_refs[0][...].astype(F32)
    slot = iota((grad_ref.shape[0], events), 0)
    hit = slot == slots_ref[0:1, :]
    for k in range(1, NIDS):
        hit = hit | (slot == slots_ref[k : k + 1, :])
    spread = jnp.where(hit, 1.0, 0.0).astype(BF16)
    grad_ref[...] = dot(spread, grad.astype(BF16)).astype(BF16)


def params():
    return pltpu.CompilerParams(vmem_limit_bytes=VMEM_LIMIT)


def gather_blocks(value, axis):
    count = lax.axis_size(axis)
    if count & (count - 1):
        return [value] + [
            lax.ppermute(value, axis, [((i + t) % count, i) for i in range(count)])
            for t in range(1, count)
        ]
    blocks = {0: value}
    bit = count // 2
    while bit:
        pairs = [(i, i ^ bit) for i in range(count)]
        for t in list(blocks):
            blocks[t | bit] = lax.ppermute(blocks[t], axis, pairs)
        bit //= 2
    return [blocks[t] for t in range(count)]


def block_index(axis):
    count = lax.axis_size(axis)
    own = lax.axis_index(axis).astype(jnp.int32)
    steps = jnp.arange(count, dtype=jnp.int32)
    if count & (count - 1):
        return (own + steps) % count
    return own ^ steps


def local(table, item_owner, item_row, segment_ids, w_in, w_out, cotangent):
    owners = lax.axis_size("table") * lax.axis_size("ctx")
    count = lax.axis_size("ctx")
    events, width = cotangent.shape
    id_count = events * NIDS
    capacity = 2 * ((id_count + owners - 1) // owners)
    slot_count = owners * capacity
    axes = ("table", "ctx")
    vmem = pl.BlockSpec(memory_space=pltpu.VMEM)

    def exchange(value):
        return lax.all_to_all(value, axes, split_axis=0, concat_axis=0, tiled=True)

    slots, wanted = pl.pallas_call(
        functools.partial(slots_kernel, capacity),
        out_shape=(
            jax.ShapeDtypeStruct((8, events), jnp.int32),
            jax.ShapeDtypeStruct((owners, capacity), jnp.int32),
        ),
        compiler_params=params(),
        name="slots",
    )(item_owner.T, item_row.T)
    asked = exchange(wanted)
    rows = pl.pallas_call(
        select_kernel,
        out_shape=jax.ShapeDtypeStruct((slot_count, width), BF16),
        compiler_params=params(),
        name="select",
    )(asked, table)
    fetched = exchange(rows.reshape(owners, capacity, width)).reshape(slot_count, width)
    embedded = pl.pallas_call(
        embed_kernel,
        out_shape=jax.ShapeDtypeStruct((events, width), BF16),
        compiler_params=params(),
        name="embed",
    )(slots, fetched)
    emb_blocks = gather_blocks(embedded, "ctx")
    cot_blocks = gather_blocks(cotangent, "ctx")
    seg_blocks = gather_blocks(segment_ids.reshape(1, events), "ctx")
    layer_out, slot_grad = pl.pallas_call(
        functools.partial(layer_kernel, count),
        out_shape=(
            jax.ShapeDtypeStruct((events, width), BF16),
            jax.ShapeDtypeStruct((slot_count, width), BF16),
        ),
        in_specs=[pl.BlockSpec(memory_space=pltpu.SMEM)] + [vmem] * (3 + 3 * count),
        out_specs=(vmem, vmem),
        scratch_shapes=[
            pltpu.VMEM((count, events, 4 * width), BF16),
            pltpu.VMEM((events, 4 * width), F32),
            pltpu.VMEM((count, events, width), BF16),
            pltpu.VMEM((count, events, 128), jnp.int32),
            pltpu.VMEM((count, 8, events), jnp.int32),
            pltpu.VMEM((events, width), F32),
            pltpu.VMEM((count, events, width), BF16),
            pltpu.VMEM((events, 4 * width), F32),
        ],
        compiler_params=params(),
        name="layer",
    )(block_index("ctx"), slots, *emb_blocks, *cot_blocks, *seg_blocks, w_in, w_out)
    returned = exchange(slot_grad.reshape(owners, capacity, width)).reshape(slot_count, width)
    row_grad = pl.pallas_call(
        collect_kernel,
        out_shape=jax.ShapeDtypeStruct(table.shape, F32),
        compiler_params=params(),
        name="collect",
    )(asked, returned)
    return layer_out, row_grad


def solution(mesh):
    rows = P(("table", "ctx"), None)
    return jax.shard_map(
        local,
        mesh=mesh,
        in_specs=(rows, rows, rows, P("table", "ctx"), P(), P(), rows),
        out_specs=(rows, rows),
        check_vma=False,
    )
```

```python
import functools

import jax
import jax.numpy as jnp
from jax import lax
from jax.experimental import pallas as pl
from jax.experimental.pallas import tpu as pltpu
from jax.sharding import PartitionSpec as P

HEADS = 4
HEAD_DIM = 128
NIDS = 2
EPS = 1e-06
VMEM_LIMIT = 50 * 1024 * 1024

F32 = jnp.float32
BF16 = jnp.bfloat16


def dot(a, b):
    return jnp.dot(a, b, preferred_element_type=F32)


def dot_nt(a, b):
    return lax.dot_general(a, b, (((1,), (1,)), ((), ())), preferred_element_type=F32)


def iota(shape, dim):
    return lax.broadcasted_iota(jnp.int32, shape, dim)


def normalize(values):
    centred = values - jnp.mean(values, -1, keepdims=True)
    inverse = lax.rsqrt(jnp.mean(centred * centred, -1, keepdims=True) + EPS)
    return centred * inverse, inverse


def norm_back(grad_norm, normed, inverse):
    mean_grad = jnp.mean(grad_norm, -1, keepdims=True)
    mean_cross = jnp.mean(grad_norm * normed, -1, keepdims=True)
    return (grad_norm - mean_grad - normed * mean_cross) * inverse


def split_exact(values):
    return (values >> 4).astype(F32).astype(BF16), (values & 15).astype(F32).astype(BF16)


def slots_kernel(capacity, owner_ref, row_ref, slots_ref, wanted_ref):
    events = owner_ref.shape[1]
    owners = wanted_ref.shape[0]
    owner = jnp.concatenate([owner_ref[k : k + 1, :] for k in range(NIDS)], 1)
    row = jnp.concatenate([row_ref[k : k + 1, :] for k in range(NIDS)], 1)
    ids = owner.shape[1]
    named = iota((owners, ids), 0) == owner
    named_f = jnp.where(named, 1.0, 0.0)
    before = jnp.where(iota((ids, ids), 0) < iota((ids, ids), 1), 1.0, 0.0).astype(BF16)
    earlier = dot(named_f.astype(BF16), before)
    rank = jnp.sum(earlier * named_f, 0, keepdims=True).astype(jnp.int32)
    slot = owner * capacity + rank
    slots_ref[...] = jnp.full(slots_ref.shape, -1, jnp.int32)
    for k in range(NIDS):
        slots_ref[k : k + 1, :] = slot[:, k * events : (k + 1) * events]
    ranked = jnp.where(iota((capacity, ids), 0) == rank, 1.0, 0.0).astype(BF16)
    high, low = (row >> 4).astype(F32), (row & 15).astype(F32)
    wanted = 16.0 * dot_nt((named_f * high).astype(BF16), ranked) + dot_nt(
        (named_f * low).astype(BF16), ranked
    )
    wanted_ref[...] = wanted.astype(jnp.int32)


def select_kernel(where_ref, asked_ref, own_ref, mate_ref, out_ref):
    owners, capacity = asked_ref.shape
    rows = own_ref.shape[0]
    slots = out_ref.shape[0]
    first, parity = where_ref[0], where_ref[1]
    high, low = split_exact(asked_ref[...])
    place = iota((slots, owners), 0) // capacity + first
    source = jnp.where(place == iota((slots, owners), 1), 1.0, 0.0).astype(BF16)
    spread = 16.0 * dot(source, high) + dot(source, low)
    mine = iota((slots, capacity), 0) % capacity == iota((slots, capacity), 1)
    asked = jnp.sum(jnp.where(mine, spread, 0.0), 1, keepdims=True).astype(jnp.int32)
    member = (iota((slots, 1), 0) // capacity) % 2
    lane = iota((slots, rows), 1)
    ours = jnp.where(lane == jnp.where(member == parity, asked, -1), 1.0, 0.0).astype(BF16)
    theirs = jnp.where(lane == jnp.where(member == parity, -1, asked), 1.0, 0.0).astype(BF16)
    out_ref[...] = (dot(ours, own_ref[...]) + dot(theirs, mate_ref[...])).astype(BF16)


def gather_events(slots_ref, base, fetched_ref, events):
    slots = fetched_ref.shape[0]
    column = jnp.transpose(slots_ref[...]) - base
    lane = iota((events, slots), 1)
    hit = lane == column[:, 0:1]
    for k in range(1, NIDS):
        hit = hit | (lane == column[:, k : k + 1])
    picked = jnp.where(hit, 1.0, 0.0).astype(BF16)
    return dot(picked, fetched_ref[...])


def scatter_events(slots_ref, base, grad, slots):
    events = grad.shape[0]
    slot = iota((slots, events), 0) + base
    hit = slot == slots_ref[0:1, :]
    for k in range(1, NIDS):
        hit = hit | (slot == slots_ref[k : k + 1, :])
    return dot(jnp.where(hit, 1.0, 0.0).astype(BF16), grad).astype(BF16)


def far_kernel(base_ref, slots_ref, fetched_ref, out_ref):
    out_ref[...] = gather_events(slots_ref, base_ref[0], fetched_ref, out_ref.shape[0]).astype(BF16)


def embed_kernel(base_ref, slots_ref, fetched_ref, far_ref, out_ref):
    near = gather_events(slots_ref, base_ref[0], fetched_ref, out_ref.shape[0])
    out_ref[...] = (near + far_ref[...].astype(F32)).astype(BF16)


def spread_kernel(base_ref, slots_ref, grad_ref, out_ref):
    out_ref[...] = scatter_events(slots_ref, base_ref[0], grad_ref[...], out_ref.shape[0])


def collect_kernel(asked_ref, near_ref, far_ref, out_ref):
    rows = out_ref.shape[0]
    slots = near_ref.shape[0]
    row = iota((rows, slots), 0)
    near = jnp.where(row == asked_ref[:, 0:slots], 1.0, 0.0).astype(BF16)
    far = jnp.where(row == asked_ref[:, slots:], 1.0, 0.0).astype(BF16)
    out_ref[...] = dot(near, near_ref[...]) + dot(far, far_ref[...])


def layer_kernel(count, *refs):
    index_ref = refs[0]
    slots_ref = refs[1]
    emb_refs = refs[2 : 2 + count]
    cot_refs = refs[2 + count : 2 + 2 * count]
    seg_refs = refs[2 + 2 * count : 2 + 3 * count]
    w_in_ref, w_out_ref = refs[2 + 3 * count : 4 + 3 * count]
    out_ref, grad_ref, near_ref = refs[4 + 3 * count : 7 + 3 * count]
    (
        proj_ref,
        slope_ref,
        cot_ref,
        segc_ref,
        segr_ref,
        att_ref,
        gatt_ref,
        join_ref,
    ) = refs[7 + 3 * count :]
    events, width = out_ref.shape
    half_scale = 0.5 * HEAD_DIM ** (-0.5)
    scale = HEAD_DIM ** (-0.5)
    own = index_ref[0]

    for t in range(count):
        place = index_ref[t]
        normed, _ = normalize(emb_refs[t][...].astype(F32))
        normed = normed.astype(BF16)
        for block in range(4):
            columns = slice(block * width, (block + 1) * width)
            before = dot(normed, w_in_ref[:, columns])
            half = 0.5 * before
            bend = jnp.tanh(half)
            value = half + half * bend
            proj_ref[place, :, columns] = value.astype(BF16)
            if t == 0:
                sigma = 0.5 + 0.5 * bend
                slope_ref[:, columns] = sigma + value - value * sigma
        cot_ref[place] = cot_refs[t][...]
        seg = jnp.broadcast_to(seg_refs[t][...], (8, events))
        segr_ref[place] = seg
        segc_ref[place] = jnp.broadcast_to(jnp.transpose(seg)[:, 0:1], segc_ref.shape[1:])

    def head(part, h):
        return slice(part * width + h * HEAD_DIM, part * width + (h + 1) * HEAD_DIM)

    def forward(i, _):
        att_ref[...] = jnp.zeros_like(att_ref)

        def pair(j, _):
            mask = (segc_ref[i][:, 0:1] == segr_ref[j][0:1, :]) & (
                iota((events, events), 0) + (i - j) * events >= iota((events, events), 1)
            )
            for h in range(HEADS):
                raw = dot_nt(proj_ref[i, :, head(2, h)], proj_ref[j, :, head(3, h)])
                half = raw * half_scale
                value = half + half * jnp.tanh(half)
                weights = jnp.where(mask, value, 0.0).astype(BF16)
                columns = slice(h * HEAD_DIM, (h + 1) * HEAD_DIM)
                att_ref[:, columns] += dot(weights, proj_ref[j, :, head(1, h)])
            return 0

        lax.fori_loop(0, i + 1, pair, 0)
        att_norm, att_inverse = normalize(att_ref[...])
        gate = proj_ref[i, :, 0:width].astype(F32)
        grad_mixed = dot_nt(cot_ref[i], w_out_ref[...])
        grad_norm = grad_mixed * gate
        gatt_ref[i] = norm_back(grad_norm, att_norm, att_inverse).astype(BF16)

        @pl.when(i == own)
        def _():
            mixed = (att_norm * gate).astype(BF16)
            out_ref[...] = (emb_refs[0][...].astype(F32) + dot(mixed, w_out_ref[...])).astype(BF16)
            join_ref[:, 0:width] = grad_mixed * att_norm

        return 0

    lax.fori_loop(own, count, forward, 0)
    join_ref[:, width:] = jnp.zeros((events, 3 * width), F32)

    def query_side(j, _):
        mask = (segc_ref[own][:, 0:1] == segr_ref[j][0:1, :]) & (
            iota((events, events), 0) + (own - j) * events >= iota((events, events), 1)
        )
        for h in range(HEADS):
            keys = proj_ref[j, :, head(3, h)]
            raw = dot_nt(proj_ref[own, :, head(2, h)], keys)
            half = raw * half_scale
            bend = jnp.tanh(half)
            value = half + half * bend
            sigma = 0.5 + 0.5 * bend
            slope = sigma + value - value * sigma
            columns = slice(h * HEAD_DIM, (h + 1) * HEAD_DIM)
            grad_weights = dot_nt(gatt_ref[own, :, columns], proj_ref[j, :, head(1, h)])
            grad_raw = jnp.where(mask, grad_weights * slope * scale, 0.0).astype(BF16)
            join_ref[:, head(2, h)] += dot(grad_raw, keys)
        return 0

    lax.fori_loop(0, own + 1, query_side, 0)

    def key_side(i, _):
        mask = (segc_ref[own][:, 0:1] == segr_ref[i][0:1, :]) & (
            iota((events, events), 0) <= iota((events, events), 1) + (i - own) * events
        )
        for h in range(HEADS):
            queries = proj_ref[i, :, head(2, h)]
            raw = dot_nt(proj_ref[own, :, head(3, h)], queries)
            half = raw * half_scale
            bend = jnp.tanh(half)
            value = half + half * bend
            sigma = 0.5 + 0.5 * bend
            slope = sigma + value - value * sigma
            columns = slice(h * HEAD_DIM, (h + 1) * HEAD_DIM)
            grad_att = gatt_ref[i, :, columns]
            grad_weights = dot_nt(proj_ref[own, :, head(1, h)], grad_att)
            grad_raw = jnp.where(mask, grad_weights * slope * scale, 0.0).astype(BF16)
            weights = jnp.where(mask, value, 0.0).astype(BF16)
            join_ref[:, head(3, h)] += dot(grad_raw, queries)
            join_ref[:, head(1, h)] += dot(weights, grad_att)
        return 0

    lax.fori_loop(own, count, key_side, 0)

    grad_proj = (join_ref[...] * slope_ref[...]).astype(BF16)
    grad_normed = dot_nt(grad_proj, w_in_ref[...])
    normed, inverse = normalize(emb_refs[0][...].astype(F32))
    grad = norm_back(grad_normed, normed, inverse) + cot_refs[0][...].astype(F32)
    grad_ref[...] = grad.astype(BF16)
    near_ref[...] = scatter_events(slots_ref, index_ref[count], grad.astype(BF16), near_ref.shape[0])


def params():
    return pltpu.CompilerParams(vmem_limit_bytes=VMEM_LIMIT)


def gather_blocks(value, axis):
    count = lax.axis_size(axis)
    if count & (count - 1):
        return [value] + [
            lax.ppermute(value, axis, [((i + t) % count, i) for i in range(count)])
            for t in range(1, count)
        ]
    blocks = {0: value}
    bit = count // 2
    while bit:
        pairs = [(i, i ^ bit) for i in range(count)]
        for t in list(blocks):
            blocks[t | bit] = lax.ppermute(blocks[t], axis, pairs)
        bit //= 2
    return [blocks[t] for t in range(count)]


def block_index(axis):
    count = lax.axis_size(axis)
    own = lax.axis_index(axis).astype(jnp.int32)
    steps = jnp.arange(count, dtype=jnp.int32)
    if count & (count - 1):
        return (own + steps) % count
    return own ^ steps


def local(table, item_owner, item_row, segment_ids, w_in, w_out, cotangent):
    tables, count = lax.axis_size("table"), lax.axis_size("ctx")
    owners = tables * count
    half = owners // 2
    events, width = cotangent.shape
    id_count = events * NIDS
    capacity = 2 * ((id_count + owners - 1) // owners)
    half_slots = half * capacity
    axes = ("table", "ctx")
    vmem = pl.BlockSpec(memory_space=pltpu.VMEM)
    smem = pl.BlockSpec(memory_space=pltpu.SMEM)

    parities = [[d for d in range(owners) if d % 2 == m] for m in range(2)]
    halves = [list(range(h * half, (h + 1) * half)) for h in range(2)]
    half_parities = [[d for d in group if d % 2 == m] for group in halves for m in range(2)]
    partners = [(t, t ^ (tables // 2)) for t in range(tables)]
    mates = [(c, c ^ 1) for c in range(count)]
    side = lax.axis_index("table").astype(jnp.int32) // (tables // 2)
    parity = lax.axis_index("ctx").astype(jnp.int32) % 2
    base = (side * half_slots).reshape(1)

    def exchange(value, groups):
        return lax.all_to_all(
            value, axes, split_axis=0, concat_axis=0, tiled=True, axis_index_groups=groups
        )

    def to_partner(value):
        return lax.ppermute(value, "table", partners)

    def to_mate(value):
        return lax.ppermute(value, "ctx", mates)

    def call(kernel, shape, name, smems, *operands):
        return pl.pallas_call(
            kernel,
            out_shape=jax.ShapeDtypeStruct(shape, F32 if name == "collect" else BF16),
            in_specs=[smem] * smems + [vmem] * (len(operands) - smems),
            out_specs=vmem,
            compiler_params=params(),
            name=name,
        )(*operands)

    table_mate = to_mate(table)
    slots, wanted = pl.pallas_call(
        functools.partial(slots_kernel, capacity),
        out_shape=(
            jax.ShapeDtypeStruct((8, events), jnp.int32),
            jax.ShapeDtypeStruct((owners, capacity), jnp.int32),
        ),
        compiler_params=params(),
        name="slots",
    )(item_owner.T, item_row.T)
    partner_slots = to_partner(slots)
    asked = exchange(wanted, parities)
    cot_blocks = gather_blocks(cotangent, "ctx")
    seg_blocks = gather_blocks(segment_ids.reshape(1, events), "ctx")

    def select(first, name):
        where = jnp.stack([first, parity])
        return call(select_kernel, (half_slots, width), name, 1, where, asked, table, table_mate)

    far_rows = select((1 - side) * half, "select_far")
    near_rows = select(side * half, "select_near")
    far_fetched = exchange(far_rows, half_parities)
    far_sum = call(far_kernel, (events, width), "far_sum", 1, base, partner_slots, far_fetched)
    near_rows, far_sum = lax.optimization_barrier((near_rows, far_sum))
    far_part = to_partner(far_sum)
    near_fetched = exchange(near_rows, half_parities)
    slots, cot_blocks, seg_blocks = lax.optimization_barrier((slots, cot_blocks, seg_blocks))
    embedded = call(
        embed_kernel, (events, width), "embed", 1, base, slots, near_fetched, far_part
    )
    emb_blocks = gather_blocks(embedded, "ctx")

    asked_mate = to_mate(asked)
    lists = jnp.stack(
        [jnp.where(parity == m, asked, asked_mate).reshape(half, 2, capacity) for m in range(2)], 1
    )
    lists = jnp.where(parity == 0, lists[:, :, 0], lists[:, :, 1]).reshape(2, half_slots)
    lists = jnp.where(side == 0, lists, lists[::-1]).reshape(1, 2 * half_slots)

    layer_out, grad, near_grad = pl.pallas_call(
        functools.partial(layer_kernel, count),
        out_shape=(
            jax.ShapeDtypeStruct((events, width), BF16),
            jax.ShapeDtypeStruct((events, width), BF16),
            jax.ShapeDtypeStruct((half_slots, width), BF16),
        ),
        in_specs=[smem] + [vmem] * (3 + 3 * count),
        out_specs=(vmem, vmem, vmem),
        scratch_shapes=[
            pltpu.VMEM((count, events, 4 * width), BF16),
            pltpu.VMEM((events, 4 * width), F32),
            pltpu.VMEM((count, events, width), BF16),
            pltpu.VMEM((count, events, 128), jnp.int32),
            pltpu.VMEM((count, 8, events), jnp.int32),
            pltpu.VMEM((events, width), F32),
            pltpu.VMEM((count, events, width), BF16),
            pltpu.VMEM((events, 4 * width), F32),
        ],
        compiler_params=params(),
        name="layer",
    )(
        jnp.concatenate([block_index("ctx"), base]),
        slots,
        *emb_blocks,
        *cot_blocks,
        *seg_blocks,
        w_in,
        w_out,
    )
    far_grad = to_partner(grad)
    near_returned = exchange(near_grad, halves)
    far_slots = call(
        spread_kernel, (half_slots, width), "spread_far", 1, base, partner_slots, far_grad
    )
    far_returned = exchange(far_slots, halves)
    row_grad = call(collect_kernel, table.shape, "collect", 0, lists, near_returned, far_returned)
    return layer_out, row_grad


def solution(mesh):
    rows = P(("table", "ctx"), None)
    return jax.shard_map(
        local,
        mesh=mesh,
        in_specs=(rows, rows, rows, P("table", "ctx"), P(), P(), rows),
        out_specs=(rows, rows),
        check_vma=False,
    )
```

```python
import functools

import jax
import jax.numpy as jnp
from jax import lax
from jax.experimental import pallas as pl
from jax.experimental.pallas import tpu as pltpu
from jax.sharding import PartitionSpec as P

HEADS = 4
HEAD_DIM = 128
NIDS = 2
EPS = 1e-06
VMEM_LIMIT = 50 * 1024 * 1024

F32 = jnp.float32
BF16 = jnp.bfloat16


def dot(a, b):
    return jnp.dot(a, b, preferred_element_type=F32)


def dot_nt(a, b):
    return lax.dot_general(a, b, (((1,), (1,)), ((), ())), preferred_element_type=F32)


def iota(shape, dim):
    return lax.broadcasted_iota(jnp.int32, shape, dim)


def normalize(values):
    centred = values - jnp.mean(values, -1, keepdims=True)
    inverse = lax.rsqrt(jnp.mean(centred * centred, -1, keepdims=True) + EPS)
    return centred * inverse, inverse


def norm_back(grad_norm, normed, inverse):
    mean_grad = jnp.mean(grad_norm, -1, keepdims=True)
    mean_cross = jnp.mean(grad_norm * normed, -1, keepdims=True)
    return (grad_norm - mean_grad - normed * mean_cross) * inverse


def split_exact(values):
    return (values >> 4).astype(F32).astype(BF16), (values & 15).astype(F32).astype(BF16)


def slots_kernel(capacity, group, me_ref, owner_ref, row_ref, slots_ref, *wanted_refs):
    events = owner_ref.shape[1]
    blocks = len(wanted_refs)
    owners = blocks * group
    owner = jnp.concatenate([owner_ref[k : k + 1, :] for k in range(NIDS)], 1)
    row = jnp.concatenate([row_ref[k : k + 1, :] for k in range(NIDS)], 1)
    relative = owner ^ me_ref[0]
    ids = owner.shape[1]
    named = jnp.where(iota((owners, ids), 0) == relative, 1.0, 0.0)
    before = jnp.where(iota((ids, ids), 0) < iota((ids, ids), 1), 1.0, 0.0).astype(BF16)
    earlier = dot(named.astype(BF16), before)
    rank = jnp.sum(earlier * named, 0, keepdims=True).astype(jnp.int32)
    slots_ref[...] = jnp.full(slots_ref.shape, -1, jnp.int32)
    for k in range(NIDS):
        part = slice(k * events, (k + 1) * events)
        slots_ref[k : k + 1, :] = (relative * capacity + rank)[:, part]
        slots_ref[NIDS + k : NIDS + k + 1, :] = (owner * capacity + rank)[:, part]
    place = (relative % group) * capacity + rank
    placed = jnp.where(iota((group * capacity, ids), 0) == place, 1.0, 0.0).astype(BF16)
    block = iota((blocks, ids), 0) == relative // group
    high = jnp.where(block, (row >> 4).astype(F32), 0.0).astype(BF16)
    low = jnp.where(block, (row & 15).astype(F32), 0.0).astype(BF16)
    wanted = (16.0 * dot_nt(high, placed) + dot_nt(low, placed)).astype(jnp.int32)
    for v in range(blocks):
        wanted_refs[v][...] = wanted[v : v + 1, :]


def select_kernel(capacity, peers, group, *refs):
    asked_refs, table_refs, out_refs = refs[:peers], refs[peers : peers + group], refs[peers + group :]
    rows = table_refs[0].shape[0]
    slots = group * capacity
    columns = []
    for u in range(peers):
        asked = jnp.broadcast_to(asked_refs[u][...], (8, slots))
        columns.append(jnp.transpose(asked)[:, 0:1])
    for x in range(group):
        part = slice(x * capacity, (x + 1) * capacity)
        asked = jnp.concatenate([column[part] for column in columns], 0)
        chosen = jnp.where(iota((peers * capacity, rows), 1) == asked, 1.0, 0.0).astype(BF16)
        picked = dot(chosen, table_refs[x][...]).astype(BF16)
        for u in range(peers):
            out_refs[u][part, :] = picked[u * capacity : (u + 1) * capacity]


def gather_events(slots_ref, first, fetched, events):
    slots = fetched.shape[0]
    column = jnp.transpose(slots_ref[...]) - first
    lane = iota((events, slots), 1)
    hit = lane == column[:, 0:1]
    for k in range(1, NIDS):
        hit = hit | (lane == column[:, k : k + 1])
    picked = jnp.where(hit, 1.0, 0.0).astype(BF16)
    return dot(picked, fetched)


def far_kernel(slots_ref, *refs):
    fetched = jnp.concatenate([ref[...] for ref in refs[:-1]], 0)
    far = gather_events(slots_ref, fetched.shape[0], fetched, refs[-1].shape[0])
    refs[-1][...] = far.astype(BF16)


def embed_kernel(slots_ref, far_ref, *refs):
    fetched = jnp.concatenate([ref[...] for ref in refs[:-1]], 0)
    near = gather_events(slots_ref, 0, fetched, refs[-1].shape[0])
    refs[-1][...] = (near + far_ref[...].astype(F32)).astype(BF16)


def collect_kernel(asked_ref, returned_ref, out_ref):
    rows = out_ref.shape[0]
    slots = returned_ref.shape[0]
    chosen = jnp.where(iota((rows, slots), 0) == asked_ref[...], 1.0, 0.0).astype(BF16)
    out_ref[...] = dot(chosen, returned_ref[...])


def layer_kernel(count, *refs):
    index_ref = refs[0]
    slots_ref = refs[1]
    emb_refs = refs[2 : 2 + count]
    cot_refs = refs[2 + count : 2 + 2 * count]
    seg_refs = refs[2 + 2 * count : 2 + 3 * count]
    w_in_ref, w_out_ref = refs[2 + 3 * count : 4 + 3 * count]
    out_ref, grad_ref = refs[4 + 3 * count : 6 + 3 * count]
    (
        proj_ref,
        slope_ref,
        cot_ref,
        segc_ref,
        segr_ref,
        att_ref,
        gatt_ref,
        join_ref,
    ) = refs[6 + 3 * count :]
    events, width = out_ref.shape
    half_scale = 0.5 * HEAD_DIM ** (-0.5)
    scale = HEAD_DIM ** (-0.5)
    own = index_ref[0]

    for t in range(count):
        place = index_ref[t]
        normed, _ = normalize(emb_refs[t][...].astype(F32))
        normed = normed.astype(BF16)
        for block in range(4):
            columns = slice(block * width, (block + 1) * width)
            before = dot(normed, w_in_ref[:, columns])
            half = 0.5 * before
            bend = jnp.tanh(half)
            value = half + half * bend
            proj_ref[place, :, columns] = value.astype(BF16)
            if t == 0:
                sigma = 0.5 + 0.5 * bend
                slope_ref[:, columns] = sigma + value - value * sigma
        cot_ref[place] = cot_refs[t][...]
        seg = jnp.broadcast_to(seg_refs[t][...], (8, events))
        segr_ref[place] = seg
        segc_ref[place] = jnp.broadcast_to(jnp.transpose(seg)[:, 0:1], segc_ref.shape[1:])

    def head(part, h):
        return slice(part * width + h * HEAD_DIM, part * width + (h + 1) * HEAD_DIM)

    def forward(i, _):
        att_ref[...] = jnp.zeros_like(att_ref)

        def pair(j, _):
            mask = (segc_ref[i][:, 0:1] == segr_ref[j][0:1, :]) & (
                iota((events, events), 0) + (i - j) * events >= iota((events, events), 1)
            )
            for h in range(HEADS):
                raw = dot_nt(proj_ref[i, :, head(2, h)], proj_ref[j, :, head(3, h)])
                half = raw * half_scale
                value = half + half * jnp.tanh(half)
                weights = jnp.where(mask, value, 0.0).astype(BF16)
                columns = slice(h * HEAD_DIM, (h + 1) * HEAD_DIM)
                att_ref[:, columns] += dot(weights, proj_ref[j, :, head(1, h)])
            return 0

        lax.fori_loop(0, i + 1, pair, 0)
        att_norm, att_inverse = normalize(att_ref[...])
        gate = proj_ref[i, :, 0:width].astype(F32)
        grad_mixed = dot_nt(cot_ref[i], w_out_ref[...])
        grad_norm = grad_mixed * gate
        gatt_ref[i] = norm_back(grad_norm, att_norm, att_inverse).astype(BF16)

        @pl.when(i == own)
        def _():
            mixed = (att_norm * gate).astype(BF16)
            out_ref[...] = (emb_refs[0][...].astype(F32) + dot(mixed, w_out_ref[...])).astype(BF16)
            join_ref[:, 0:width] = grad_mixed * att_norm

        return 0

    lax.fori_loop(own, count, forward, 0)
    join_ref[:, width:] = jnp.zeros((events, 3 * width), F32)

    def query_side(j, _):
        mask = (segc_ref[own][:, 0:1] == segr_ref[j][0:1, :]) & (
            iota((events, events), 0) + (own - j) * events >= iota((events, events), 1)
        )
        for h in range(HEADS):
            keys = proj_ref[j, :, head(3, h)]
            raw = dot_nt(proj_ref[own, :, head(2, h)], keys)
            half = raw * half_scale
            bend = jnp.tanh(half)
            value = half + half * bend
            sigma = 0.5 + 0.5 * bend
            slope = sigma + value - value * sigma
            columns = slice(h * HEAD_DIM, (h + 1) * HEAD_DIM)
            grad_weights = dot_nt(gatt_ref[own, :, columns], proj_ref[j, :, head(1, h)])
            grad_raw = jnp.where(mask, grad_weights * slope * scale, 0.0).astype(BF16)
            join_ref[:, head(2, h)] += dot(grad_raw, keys)
        return 0

    lax.fori_loop(0, own + 1, query_side, 0)

    def key_side(i, _):
        mask = (segc_ref[own][:, 0:1] == segr_ref[i][0:1, :]) & (
            iota((events, events), 0) <= iota((events, events), 1) + (i - own) * events
        )
        for h in range(HEADS):
            queries = proj_ref[i, :, head(2, h)]
            raw = dot_nt(proj_ref[own, :, head(3, h)], queries)
            half = raw * half_scale
            bend = jnp.tanh(half)
            value = half + half * bend
            sigma = 0.5 + 0.5 * bend
            slope = sigma + value - value * sigma
            columns = slice(h * HEAD_DIM, (h + 1) * HEAD_DIM)
            grad_att = gatt_ref[i, :, columns]
            grad_weights = dot_nt(proj_ref[own, :, head(1, h)], grad_att)
            grad_raw = jnp.where(mask, grad_weights * slope * scale, 0.0).astype(BF16)
            weights = jnp.where(mask, value, 0.0).astype(BF16)
            join_ref[:, head(3, h)] += dot(grad_raw, queries)
            join_ref[:, head(1, h)] += dot(weights, grad_att)
        return 0

    lax.fori_loop(own, count, key_side, 0)

    grad_proj = (join_ref[...] * slope_ref[...]).astype(BF16)
    grad_normed = dot_nt(grad_proj, w_in_ref[...])
    normed, inverse = normalize(emb_refs[0][...].astype(F32))
    grad = norm_back(grad_normed, normed, inverse) + cot_refs[0][...].astype(F32)
    slot = iota((grad_ref.shape[0], events), 0)
    hit = slot == slots_ref[NIDS : NIDS + 1, :]
    for k in range(1, NIDS):
        hit = hit | (slot == slots_ref[NIDS + k : NIDS + k + 1, :])
    spread = jnp.where(hit, 1.0, 0.0).astype(BF16)
    grad_ref[...] = dot(spread, grad.astype(BF16)).astype(BF16)


def params():
    return pltpu.CompilerParams(vmem_limit_bytes=VMEM_LIMIT)


def flip(value, axis, offset):
    count = lax.axis_size(axis)
    return lax.ppermute(value, axis, [(i, i ^ offset) for i in range(count)])


def gather_blocks(value, axis, opposite=None):
    bit = lax.axis_size(axis) // 2
    blocks = {0: value, bit: flip(value, axis, bit) if opposite is None else opposite}
    while bit > 1:
        bit //= 2
        for t in list(blocks):
            blocks[t | bit] = flip(blocks[t], axis, bit)
    return [blocks[t] for t in range(lax.axis_size(axis))]


def local(table, item_owner, item_row, segment_ids, w_in, w_out, cotangent):
    tables, count = lax.axis_size("table"), lax.axis_size("ctx")
    owners = tables * count
    events, width = cotangent.shape
    id_count = events * NIDS
    capacity = 2 * ((id_count + owners - 1) // owners)
    slot_count = owners * capacity
    peers = tables // 2
    block_slots = count * capacity
    vmem = pl.BlockSpec(memory_space=pltpu.VMEM)
    smem = pl.BlockSpec(memory_space=pltpu.SMEM)
    ctx_index = lax.axis_index("ctx").astype(jnp.int32)
    me = lax.axis_index("table").astype(jnp.int32) * count + ctx_index

    def call(kernel, shapes, name, *operands, smems=0):
        return pl.pallas_call(
            kernel,
            out_shape=shapes,
            in_specs=[smem] * smems + [vmem] * (len(operands) - smems),
            out_specs=jax.tree.map(lambda _: vmem, shapes),
            compiler_params=params(),
            name=name,
        )(*operands)

    def after(value, earlier):
        return lax.optimization_barrier((value, earlier))[0]

    table_far = flip(table, "ctx", count // 2)
    slots, *wanted = call(
        functools.partial(slots_kernel, capacity, count),
        (jax.ShapeDtypeStruct((8, events), jnp.int32),)
        + (jax.ShapeDtypeStruct((1, block_slots), jnp.int32),) * tables,
        "slots",
        me.reshape(1),
        item_owner.T,
        item_row.T,
        smems=1,
    )
    asked = [wanted[0]] + [flip(wanted[v], "table", v) for v in range(1, tables)]
    partner_slots = flip(slots, "table", peers)
    row_shapes = (jax.ShapeDtypeStruct((block_slots, width), BF16),) * peers
    event_shape = jax.ShapeDtypeStruct((events, width), BF16)
    select = functools.partial(select_kernel, capacity, peers, count)
    table_blocks = gather_blocks(table, "ctx", after(table_far, asked))
    far_rows = call(select, row_shapes, "select_far", *asked[peers:], *table_blocks)
    held = after(cotangent, far_rows)
    cot_far = flip(held, "ctx", count // 2)
    far_rows = [far_rows[0]] + [flip(far_rows[u], "table", u) for u in range(1, peers)]
    far_sum = call(far_kernel, event_shape, "far_sum", partner_slots, *far_rows)
    far_part = flip(far_sum, "table", peers)
    near_asked = after(asked[:peers], far_sum)
    near_rows = call(select, row_shapes, "select_near", *near_asked, *table_blocks)
    near_rows = [near_rows[0]] + [flip(near_rows[u], "table", u) for u in range(1, peers)]

    cot_blocks = gather_blocks(cotangent, "ctx", after(cot_far, near_rows[1]))
    seg_blocks = gather_blocks(after(segment_ids.reshape(1, events), held), "ctx")
    slots, cot_blocks, seg_blocks = lax.optimization_barrier((slots, cot_blocks, seg_blocks))
    embedded = call(embed_kernel, event_shape, "embed", slots, far_part, *near_rows)
    emb_blocks = gather_blocks(embedded, "ctx")

    stacked = after(jnp.concatenate(asked, 0), embedded)
    lists = [stacked[:, :capacity]] + [
        flip(stacked[:, x * capacity : (x + 1) * capacity], "ctx", x) for x in range(1, count)
    ]
    lists = jnp.stack(lists, 1).reshape(owners, capacity)
    lists = lists[jnp.arange(owners, dtype=jnp.int32) ^ me].reshape(1, slot_count)
    slots = after(slots, lists)

    layer_out, slot_grad = pl.pallas_call(
        functools.partial(layer_kernel, count),
        out_shape=(event_shape, jax.ShapeDtypeStruct((slot_count, width), BF16)),
        in_specs=[smem] + [vmem] * (3 + 3 * count),
        out_specs=(vmem, vmem),
        scratch_shapes=[
            pltpu.VMEM((count, events, 4 * width), BF16),
            pltpu.VMEM((events, 4 * width), F32),
            pltpu.VMEM((count, events, width), BF16),
            pltpu.VMEM((count, events, 128), jnp.int32),
            pltpu.VMEM((count, 8, events), jnp.int32),
            pltpu.VMEM((events, width), F32),
            pltpu.VMEM((count, events, width), BF16),
            pltpu.VMEM((events, 4 * width), F32),
        ],
        compiler_params=params(),
        name="layer",
    )(
        ctx_index ^ jnp.arange(count, dtype=jnp.int32),
        slots,
        *emb_blocks,
        *cot_blocks,
        *seg_blocks,
        w_in,
        w_out,
    )
    returned = lax.all_to_all(
        slot_grad.reshape(owners, capacity, width),
        ("table", "ctx"),
        split_axis=0,
        concat_axis=0,
        tiled=True,
    ).reshape(slot_count, width)
    row_grad = call(
        collect_kernel, jax.ShapeDtypeStruct(table.shape, F32), "collect", lists, returned
    )
    return layer_out, row_grad


def solution(mesh):
    rows = P(("table", "ctx"), None)
    return jax.shard_map(
        local,
        mesh=mesh,
        in_specs=(rows, rows, rows, P("table", "ctx"), P(), P(), rows),
        out_specs=(rows, rows),
        check_vma=False,
    )
```

```python
import functools

import jax
import jax.numpy as jnp
from jax import lax
from jax.experimental import pallas as pl
from jax.experimental.pallas import tpu as pltpu
from jax.sharding import PartitionSpec as P

HEADS = 4
HEAD_DIM = 128
NIDS = 2
EPS = 1e-06
VMEM_LIMIT = 40 * 1024 * 1024

F32 = jnp.float32
BF16 = jnp.bfloat16


def dot(a, b):
    return jnp.dot(a, b, preferred_element_type=F32)


def dot_nt(a, b):
    return lax.dot_general(a, b, (((1,), (1,)), ((), ())), preferred_element_type=F32)


def iota(shape, dim):
    return lax.broadcasted_iota(jnp.int32, shape, dim)


def normalize(values):
    centred = values - jnp.mean(values, -1, keepdims=True)
    inverse = lax.rsqrt(jnp.mean(centred * centred, -1, keepdims=True) + EPS)
    return centred * inverse, inverse


def norm_back(grad_norm, normed, inverse):
    mean_grad = jnp.mean(grad_norm, -1, keepdims=True)
    mean_cross = jnp.mean(grad_norm * normed, -1, keepdims=True)
    return (grad_norm - mean_grad - normed * mean_cross) * inverse


def split_exact(values):
    return (values >> 4).astype(F32).astype(BF16), (values & 15).astype(F32).astype(BF16)


EXTRA = 16


def slots_kernel(
    capacity, owner_ref, row_ref, seg_ref, cot_ref, slots_ref, wanted_ref, side_ref
):
    side_ref[0 : cot_ref.shape[0], :] = cot_ref[...]
    side_ref[cot_ref.shape[0] :, :] = jnp.zeros((EXTRA, side_ref.shape[1]), BF16)
    segments = seg_ref[...].astype(F32)
    side_ref[cot_ref.shape[0] :, 0 : seg_ref.shape[1]] = jnp.broadcast_to(
        segments, (EXTRA, seg_ref.shape[1])
    ).astype(BF16)
    events = owner_ref.shape[1]
    owners = wanted_ref.shape[0]
    owner = jnp.concatenate([owner_ref[k : k + 1, :] for k in range(NIDS)], 1)
    row = jnp.concatenate([row_ref[k : k + 1, :] for k in range(NIDS)], 1)
    ids = owner.shape[1]
    named = iota((owners, ids), 0) == owner
    named_f = jnp.where(named, 1.0, 0.0)
    before = jnp.where(iota((ids, ids), 0) < iota((ids, ids), 1), 1.0, 0.0).astype(BF16)
    earlier = dot(named_f.astype(BF16), before)
    rank = jnp.sum(earlier * named_f, 0, keepdims=True).astype(jnp.int32)
    slot = owner * capacity + rank
    slots_ref[...] = jnp.full(slots_ref.shape, -1, jnp.int32)
    for k in range(NIDS):
        slots_ref[k : k + 1, :] = slot[:, k * events : (k + 1) * events]
    ranked = jnp.where(iota((capacity, ids), 0) == rank, 1.0, 0.0).astype(BF16)
    high, low = (row >> 4).astype(F32), (row & 15).astype(F32)
    wanted = 16.0 * dot_nt((named_f * high).astype(BF16), ranked) + dot_nt(
        (named_f * low).astype(BF16), ranked
    )
    wanted_ref[...] = wanted.astype(jnp.int32)


def select_kernel(asked_ref, table_ref, out_ref):
    owners, capacity = asked_ref.shape
    rows = table_ref.shape[0]
    columns = jnp.transpose(asked_ref[...])
    lane = iota((capacity, rows), 1)
    chosen = jnp.concatenate(
        [jnp.where(lane == columns[:, s : s + 1], 1.0, 0.0) for s in range(owners)], 0
    )
    out_ref[...] = dot(chosen.astype(BF16), table_ref[...]).astype(BF16)


def embed_kernel(slots_ref, fetched_ref, out_ref):
    events = out_ref.shape[0]
    slots = fetched_ref.shape[0]
    column = jnp.transpose(slots_ref[...])
    lane = iota((events, slots), 1)
    hit = lane == column[:, 0:1]
    for k in range(1, NIDS):
        hit = hit | (lane == column[:, k : k + 1])
    picked = jnp.where(hit, 1.0, 0.0).astype(BF16)
    out_ref[...] = dot(picked, fetched_ref[...]).astype(BF16)


def collect_kernel(asked_ref, returned_ref, out_ref):
    owners, capacity = asked_ref.shape
    rows = out_ref.shape[0]
    slots = owners * capacity
    high, low = split_exact(asked_ref[...])
    place = jnp.where(
        iota((capacity, slots), 1) % capacity == iota((capacity, slots), 0), 1.0, 0.0
    ).astype(BF16)
    spread = 16.0 * dot(high, place) + dot(low, place)
    mine = iota((owners, slots), 1) // capacity == iota((owners, slots), 0)
    asked = jnp.sum(jnp.where(mine, spread, 0.0), 0, keepdims=True).astype(jnp.int32)
    chosen = jnp.where(iota((rows, slots), 0) == asked, 1.0, 0.0).astype(BF16)
    out_ref[...] = dot(chosen, returned_ref[...])


SCALE = HEAD_DIM ** (-0.5)


def head(part, h, width):
    return slice(part * width + h * HEAD_DIM, part * width + (h + 1) * HEAD_DIM)


def visible(query_chunk, key_chunk, segc_ref, segr_ref, flip):
    events = segr_ref.shape[2]
    first, second = iota((events, events), 0), iota((events, events), 1)
    if flip:
        same = segc_ref[key_chunk][:, 0:1] == segr_ref[query_chunk][0:1, :]
        return same & (first <= second + (query_chunk - key_chunk) * events)
    same = segc_ref[query_chunk][:, 0:1] == segr_ref[key_chunk][0:1, :]
    return same & (first + (query_chunk - key_chunk) * events >= second)


def project(emb, w_in_ref, write, slope_ref):
    width = emb.shape[1]
    normed = normalize(emb.astype(F32))[0].astype(BF16)
    for block in range(4):
        columns = slice(block * width, (block + 1) * width)
        half = 0.5 * dot(normed, w_in_ref[:, columns])
        bend = jnp.tanh(half)
        value = half + half * bend
        write(columns, value.astype(BF16))
        if slope_ref is not None:
            sigma = 0.5 + 0.5 * bend
            slope_ref[:, columns] = sigma + value - value * sigma


def hold_side(side_ref, place, cots_ref, segc_ref, segr_ref):
    events = cots_ref.shape[1]
    cots_ref[place] = side_ref[0:events, :]
    seg = side_ref[events : events + EXTRA, 0:events].astype(F32)[0:8]
    segr_ref[place] = seg
    segc_ref[place] = jnp.broadcast_to(jnp.transpose(seg)[:, 0:1], segc_ref.shape[1:])


class Chunks:
    def __init__(self, first, proj_ref, gatt_ref, segc_ref, segr_ref, join_ref):
        self.first, self.proj, self.gatt = first, proj_ref, gatt_ref
        self.segc, self.segr, self.join = segc_ref, segr_ref, join_ref
        self.width = gatt_ref.shape[2]

    def attend(self, i, start, stop, att_ref):
        def pair(j, _):
            mask = visible(i, j, self.segc, self.segr, False)
            qi, kj = i - self.first, j - self.first
            for h in range(HEADS):
                queries = self.proj[qi, :, head(2, h, self.width)]
                raw = dot_nt(queries, self.proj[kj, :, head(3, h, self.width)])
                half = raw * (0.5 * SCALE)
                value = half + half * jnp.tanh(half)
                weights = jnp.where(mask, value, 0.0).astype(BF16)
                added = dot(weights, self.proj[kj, :, head(1, h, self.width)])
                att_ref[:, head(0, h, self.width)] += added
            return 0

        lax.fori_loop(start, stop, pair, 0)

    def finish(self, i, own, att, cot, emb_ref, w_out_ref, out_ref):
        att_norm, att_inverse = normalize(att)
        gate = self.proj[i - self.first, :, 0 : self.width].astype(F32)
        grad_mixed = dot_nt(cot, w_out_ref[...])
        grad_att = norm_back(grad_mixed * gate, att_norm, att_inverse)
        self.gatt[i - self.first] = grad_att.astype(BF16)

        @pl.when(i == own)
        def _():
            mixed = (att_norm * gate).astype(BF16)
            out = emb_ref[...].astype(F32) + dot(mixed, w_out_ref[...])
            out_ref[...] = out.astype(BF16)
            self.join[:, 0 : self.width] = grad_mixed * att_norm

    def query_side(self, own, start, stop):
        def pair(j, _):
            mask = visible(own, j, self.segc, self.segr, False)
            me, kj = own - self.first, j - self.first
            for h in range(HEADS):
                keys = self.proj[kj, :, head(3, h, self.width)]
                half = dot_nt(self.proj[me, :, head(2, h, self.width)], keys) * (0.5 * SCALE)
                bend = jnp.tanh(half)
                value = half + half * bend
                sigma = 0.5 + 0.5 * bend
                slope = sigma + value - value * sigma
                grad_weights = dot_nt(
                    self.gatt[me, :, head(0, h, self.width)],
                    self.proj[kj, :, head(1, h, self.width)],
                )
                grad_raw = jnp.where(mask, grad_weights * slope * SCALE, 0.0).astype(BF16)
                self.join[:, head(2, h, self.width)] += dot(grad_raw, keys)
            return 0

        lax.fori_loop(start, stop, pair, 0)

    def key_side(self, own, start, stop):
        def pair(i, _):
            mask = visible(i, own, self.segc, self.segr, True)
            me, qi = own - self.first, i - self.first
            for h in range(HEADS):
                queries = self.proj[qi, :, head(2, h, self.width)]
                half = dot_nt(self.proj[me, :, head(3, h, self.width)], queries) * (0.5 * SCALE)
                bend = jnp.tanh(half)
                value = half + half * bend
                sigma = 0.5 + 0.5 * bend
                slope = sigma + value - value * sigma
                grad_att = self.gatt[qi, :, head(0, h, self.width)]
                grad_weights = dot_nt(self.proj[me, :, head(1, h, self.width)], grad_att)
                grad_raw = jnp.where(mask, grad_weights * slope * SCALE, 0.0).astype(BF16)
                weights = jnp.where(mask, value, 0.0).astype(BF16)
                self.join[:, head(3, h, self.width)] += dot(grad_raw, queries)
                self.join[:, head(1, h, self.width)] += dot(weights, grad_att)
            return 0

        lax.fori_loop(start, stop, pair, 0)


def early_kernel(
    index_ref,
    emb_ref,
    mate_ref,
    side_ref,
    side_mate_ref,
    w_in_ref,
    w_out_ref,
    proj_ref,
    att_ref,
    gatt_ref,
    join_ref,
    slope_ref,
    out_ref,
    segc_ref,
    segr_ref,
    cots_ref,
):
    own = index_ref[0]
    mate = index_ref[1]
    base = jnp.minimum(own, mate)
    last = jnp.maximum(own, mate)

    def write_to(place):
        def write(columns, value):
            proj_ref[place - base, :, columns] = value

        return write

    project(emb_ref[...], w_in_ref, write_to(own), slope_ref)
    project(mate_ref[...], w_in_ref, write_to(mate), None)
    hold_side(side_ref, own - base, cots_ref, segc_ref, segr_ref)
    hold_side(side_mate_ref, mate - base, cots_ref, segc_ref, segr_ref)
    att_ref[...] = jnp.zeros_like(att_ref)
    join_ref[...] = jnp.zeros_like(join_ref)
    chunks = Chunks(0, proj_ref, gatt_ref, segc_ref, segr_ref, join_ref)

    def forward(i, _):
        chunks.attend(i, 0, i + 1, att_ref.at[i])
        return 0

    lax.fori_loop(own - base, last - base + 1, forward, 0)

    @pl.when(base == 0)
    def _():
        def finish(i, _):
            chunks.finish(i, own, att_ref[i], cots_ref[i], emb_ref, w_out_ref, out_ref)
            return 0

        lax.fori_loop(own, last + 1, finish, 0)
        chunks.query_side(own, 0, own + 1)
        chunks.key_side(own, own, last + 1)


def late_kernel(count, *refs):
    index_ref, slots_ref = refs[:2]
    emb_refs = refs[2 : 2 + count]
    side_refs = refs[2 + count : 2 + 2 * count]
    (
        w_in_ref,
        w_out_ref,
        proj_pair_ref,
        att_pair_ref,
        gatt_pair_ref,
        join_early_ref,
        slope_ref,
        out_early_ref,
        out_ref,
        grad_ref,
        proj_ref,
        cot_ref,
        segc_ref,
        segr_ref,
        att_ref,
        gatt_ref,
        join_ref,
    ) = refs[2 + 2 * count :]
    own = index_ref[0]
    base = jnp.minimum(own, index_ref[1])
    last = jnp.maximum(own, index_ref[1])
    closed = base == 0

    for t in range(count):
        place = index_ref[t]
        hold_side(side_refs[t], place, cot_ref, segc_ref, segr_ref)
    for t in range(2):
        proj_ref[base + t] = proj_pair_ref[t]
        gatt_ref[base + t] = gatt_pair_ref[t]

    def write_to(place):
        def write(columns, value):
            proj_ref[place, :, columns] = value

        return write

    for t in range(2, count):
        project(emb_refs[t][...], w_in_ref, write_to(index_ref[t]), None)
    join_ref[...] = jnp.zeros_like(join_ref)
    chunks = Chunks(0, proj_ref, gatt_ref, segc_ref, segr_ref, join_ref)

    @pl.when(closed)
    def _():
        out_ref[...] = out_early_ref[...]

    def forward(i, _):
        begun = i <= last

        @pl.when(begun)
        def _():
            att_ref[...] = att_pair_ref[jnp.minimum(i - base, 1)]

        @pl.when(jnp.logical_not(begun))
        def _():
            att_ref[...] = jnp.zeros_like(att_ref)

        chunks.attend(i, 0, jnp.where(begun, base, i + 1), att_ref)
        chunks.finish(i, own, att_ref[...], cot_ref[i], emb_refs[0], w_out_ref, out_ref)
        return 0

    lax.fori_loop(jnp.where(closed, last + 1, own), count, forward, 0)
    chunks.query_side(own, jnp.where(closed, own + 1, 0), own + 1)
    chunks.key_side(own, jnp.where(closed, last + 1, own), count)

    grad_proj = ((join_ref[...] + join_early_ref[...]) * slope_ref[...]).astype(BF16)
    grad_normed = dot_nt(grad_proj, w_in_ref[...])
    normed, inverse = normalize(emb_refs[0][...].astype(F32))
    grad = norm_back(grad_normed, normed, inverse) + cot_ref[own].astype(F32)
    slot = iota((grad_ref.shape[0], grad.shape[0]), 0)
    hit = slot == slots_ref[0:1, :]
    for k in range(1, NIDS):
        hit = hit | (slot == slots_ref[k : k + 1, :])
    spread = jnp.where(hit, 1.0, 0.0).astype(BF16)
    grad_ref[...] = dot(spread, grad.astype(BF16)).astype(BF16)


def params():
    return pltpu.CompilerParams(vmem_limit_bytes=VMEM_LIMIT)


def flip(value, axis, offset):
    count = lax.axis_size(axis)
    return lax.ppermute(value, axis, [(i, i ^ offset) for i in range(count)])


def gather_blocks(value, axis, known):
    bit = lax.axis_size(axis)
    blocks = {0: value}
    while bit > 1:
        bit //= 2
        for t in list(blocks):
            blocks[t | bit] = known.get(t | bit)
            if blocks[t | bit] is None:
                blocks[t | bit] = flip(blocks[t], axis, bit)
    return [blocks[t] for t in range(lax.axis_size(axis))]


def after(value, earlier):
    return lax.optimization_barrier((value, earlier))[0]


def local(table, item_owner, item_row, segment_ids, w_in, w_out, cotangent):
    owners = lax.axis_size("table") * lax.axis_size("ctx")
    count = lax.axis_size("ctx")
    events, width = cotangent.shape
    id_count = events * NIDS
    capacity = 2 * ((id_count + owners - 1) // owners)
    slot_count = owners * capacity
    axes = ("table", "ctx")
    vmem = pl.BlockSpec(memory_space=pltpu.VMEM)
    smem = pl.BlockSpec(memory_space=pltpu.SMEM)

    def exchange(value):
        return lax.all_to_all(value, axes, split_axis=0, concat_axis=0, tiled=True)

    slots, wanted, side = pl.pallas_call(
        functools.partial(slots_kernel, capacity),
        out_shape=(
            jax.ShapeDtypeStruct((8, events), jnp.int32),
            jax.ShapeDtypeStruct((owners, capacity), jnp.int32),
            jax.ShapeDtypeStruct((events + EXTRA, width), BF16),
        ),
        compiler_params=params(),
        name="slots",
    )(item_owner.T, item_row.T, segment_ids.reshape(1, events), cotangent)
    asked = exchange(wanted)
    rows = pl.pallas_call(
        select_kernel,
        out_shape=jax.ShapeDtypeStruct((slot_count, width), BF16),
        compiler_params=params(),
        name="select",
    )(asked, table)
    fetched = exchange(rows.reshape(owners, capacity, width)).reshape(slot_count, width)
    held = after(side, rows)
    side_blocks = [side] + [flip(held, "ctx", t) for t in range(1, count)]
    slots, side_blocks = lax.optimization_barrier((slots, side_blocks))
    embedded = pl.pallas_call(
        embed_kernel,
        out_shape=jax.ShapeDtypeStruct((events, width), BF16),
        compiler_params=params(),
        name="embed",
    )(slots, fetched)
    emb_far = flip(embedded, "ctx", count // 2)
    emb_mate = flip(embedded, "ctx", 1)
    index = lax.axis_index("ctx").astype(jnp.int32) ^ jnp.arange(count, dtype=jnp.int32)
    event_shape = jax.ShapeDtypeStruct((events, width), BF16)
    early = pl.pallas_call(
        early_kernel,
        out_shape=(
            jax.ShapeDtypeStruct((2, events, 4 * width), BF16),
            jax.ShapeDtypeStruct((2, events, width), F32),
            jax.ShapeDtypeStruct((2, events, width), BF16),
            jax.ShapeDtypeStruct((events, 4 * width), F32),
            jax.ShapeDtypeStruct((events, 4 * width), F32),
            event_shape,
        ),
        in_specs=[smem] + [vmem] * 6,
        out_specs=(vmem,) * 6,
        scratch_shapes=[
            pltpu.VMEM((2, events, 128), F32),
            pltpu.VMEM((2, 8, events), F32),
            pltpu.VMEM((2, events, width), BF16),
        ],
        compiler_params=params(),
        name="early",
    )(index, embedded, emb_mate, *side_blocks[:2], w_in, w_out)
    emb_blocks = gather_blocks(embedded, "ctx", {1: emb_mate, count // 2: after(emb_far, early)})
    layer_out, slot_grad = pl.pallas_call(
        functools.partial(late_kernel, count),
        out_shape=(event_shape, jax.ShapeDtypeStruct((slot_count, width), BF16)),
        in_specs=[smem] + [vmem] * (9 + 2 * count),
        out_specs=(vmem, vmem),
        scratch_shapes=[
            pltpu.VMEM((count, events, 4 * width), BF16),
            pltpu.VMEM((count, events, width), BF16),
            pltpu.VMEM((count, events, 128), F32),
            pltpu.VMEM((count, 8, events), F32),
            pltpu.VMEM((events, width), F32),
            pltpu.VMEM((count, events, width), BF16),
            pltpu.VMEM((events, 4 * width), F32),
        ],
        compiler_params=params(),
        name="late",
    )(index, slots, *emb_blocks, *side_blocks, w_in, w_out, *early)
    returned = exchange(slot_grad.reshape(owners, capacity, width)).reshape(slot_count, width)
    row_grad = pl.pallas_call(
        collect_kernel,
        out_shape=jax.ShapeDtypeStruct(table.shape, F32),
        compiler_params=params(),
        name="collect",
    )(asked, returned)
    return layer_out, row_grad


def solution(mesh):
    rows = P(("table", "ctx"), None)
    return jax.shard_map(
        local,
        mesh=mesh,
        in_specs=(rows, rows, rows, P("table", "ctx"), P(), P(), rows),
        out_specs=(rows, rows),
        check_vma=False,
    )
```

```python
import functools

import jax
import jax.numpy as jnp
from jax import lax
from jax.experimental import pallas as pl
from jax.experimental.pallas import tpu as pltpu
from jax.sharding import PartitionSpec as P

HEADS = 4
HEAD_DIM = 128
NIDS = 2
EPS = 1e-06

F32 = jnp.float32
BF16 = jnp.bfloat16


def dot(a, b):
    return jnp.dot(a, b, preferred_element_type=F32)


def dot_nt(a, b):
    return lax.dot_general(a, b, (((1,), (1,)), ((), ())), preferred_element_type=F32)


def iota(shape, dim):
    return lax.broadcasted_iota(jnp.int32, shape, dim)


def normalize(values):
    centred = values - jnp.mean(values, -1, keepdims=True)
    inverse = lax.rsqrt(jnp.mean(centred * centred, -1, keepdims=True) + EPS)
    return centred * inverse, inverse


def norm_back(grad_norm, normed, inverse):
    mean_grad = jnp.mean(grad_norm, -1, keepdims=True)
    mean_cross = jnp.mean(grad_norm * normed, -1, keepdims=True)
    return (grad_norm - mean_grad - normed * mean_cross) * inverse


def split_exact(values):
    return (values >> 4).astype(F32).astype(BF16), (values & 15).astype(F32).astype(BF16)


EXTRA = 16
WHOLE = 61


def slots_kernel(
    capacity,
    owner_in,
    row_in,
    seg_in,
    cot_in,
    slots_ref,
    wanted_ref,
    side_ref,
    owner_ref,
    row_ref,
    seg_ref,
    sems,
):
    events, width = cot_in.shape
    pairs = (
        (owner_in, owner_ref),
        (row_in, row_ref),
        (seg_in, seg_ref),
        (cot_in, side_ref.at[0:events]),
    )
    copies = [pltpu.make_async_copy(a, b, sems.at[i]) for i, (a, b) in enumerate(pairs)]
    for copy in copies:
        copy.start()
    for copy in copies[:3]:
        copy.wait()
    side_ref[events:, :] = jnp.zeros((EXTRA, width), BF16)
    segments = jnp.broadcast_to(seg_ref[...].astype(F32), (EXTRA, events))
    side_ref[events:, 0:events] = segments.astype(BF16)
    owners = wanted_ref.shape[0]
    owner = jnp.concatenate([owner_ref[k : k + 1, :] for k in range(NIDS)], 1)
    row = jnp.concatenate([row_ref[k : k + 1, :] for k in range(NIDS)], 1)
    ids = owner.shape[1]
    named = iota((owners, ids), 0) == owner
    named_f = jnp.where(named, 1.0, 0.0)
    before = jnp.where(iota((ids, ids), 0) < iota((ids, ids), 1), 1.0, 0.0).astype(BF16)
    earlier = dot(named_f.astype(BF16), before)
    rank = jnp.sum(earlier * named_f, 0, keepdims=True).astype(jnp.int32)
    slot = owner * capacity + rank
    slots_ref[...] = jnp.full(slots_ref.shape, -1, jnp.int32)
    for k in range(NIDS):
        slots_ref[k : k + 1, :] = slot[:, k * events : (k + 1) * events]
    ranked = jnp.where(iota((capacity, ids), 0) == rank, 1.0, 0.0).astype(BF16)
    high, low = (row >> 4).astype(F32), (row & 15).astype(F32)
    wanted = 16.0 * dot_nt((named_f * high).astype(BF16), ranked) + dot_nt(
        (named_f * low).astype(BF16), ranked
    )
    wanted_ref[...] = wanted.astype(jnp.int32)
    for copy in copies[3:]:
        copy.wait()


def select_kernel(asked_in, table_in, out_ref, asked_ref, table_ref, sems):
    pairs = ((asked_in, asked_ref), (table_in, table_ref))
    copies = [pltpu.make_async_copy(a, b, sems.at[i]) for i, (a, b) in enumerate(pairs)]
    for copy in copies:
        copy.start()
    copies[0].wait()
    owners, capacity = asked_ref.shape
    rows = table_ref.shape[0]
    columns = jnp.transpose(asked_ref[...])
    lane = iota((capacity, rows), 1)
    chosen = jnp.concatenate(
        [jnp.where(lane == columns[:, s : s + 1], 1.0, 0.0) for s in range(owners)], 0
    )
    chosen = chosen.astype(BF16)
    copies[1].wait()
    out_ref[...] = dot(chosen, table_ref[...]).astype(BF16)


def embed_kernel(slots_ref, fetched_ref, out_ref):
    events = out_ref.shape[0]
    slots = fetched_ref.shape[0]
    column = jnp.transpose(slots_ref[...])
    lane = iota((events, slots), 1)
    hit = lane == column[:, 0:1]
    for k in range(1, NIDS):
        hit = hit | (lane == column[:, k : k + 1])
    picked = jnp.where(hit, 1.0, 0.0).astype(BF16)
    out_ref[...] = dot(picked, fetched_ref[...]).astype(BF16)


def collect_kernel(asked_ref, returned_ref, out_ref):
    owners, capacity = asked_ref.shape
    rows = out_ref.shape[0]
    slots = owners * capacity
    high, low = split_exact(asked_ref[...])
    place = jnp.where(
        iota((capacity, slots), 1) % capacity == iota((capacity, slots), 0), 1.0, 0.0
    ).astype(BF16)
    spread = 16.0 * dot(high, place) + dot(low, place)
    mine = iota((owners, slots), 1) // capacity == iota((owners, slots), 0)
    asked = jnp.sum(jnp.where(mine, spread, 0.0), 0, keepdims=True).astype(jnp.int32)
    chosen = jnp.where(iota((rows, slots), 0) == asked, 1.0, 0.0).astype(BF16)
    out_ref[...] = dot(chosen, returned_ref[...])


SCALE = HEAD_DIM ** (-0.5)


def head(part, h, width):
    return slice(part * width + h * HEAD_DIM, part * width + (h + 1) * HEAD_DIM)


def visible(query_chunk, key_chunk, segc_ref, segr_ref, flip):
    events = segr_ref.shape[2]
    first, second = iota((events, events), 0), iota((events, events), 1)
    if flip:
        same = segc_ref[key_chunk][:, 0:1] == segr_ref[query_chunk][0:1, :]
        return same & (first <= second + (query_chunk - key_chunk) * events)
    same = segc_ref[query_chunk][:, 0:1] == segr_ref[key_chunk][0:1, :]
    return same & (first + (query_chunk - key_chunk) * events >= second)


def project(emb, w_in_ref, write, slope_ref):
    width = emb.shape[1]
    normed = normalize(emb.astype(F32))[0].astype(BF16)
    for block in range(4):
        columns = slice(block * width, (block + 1) * width)
        half = 0.5 * dot(normed, w_in_ref[:, columns])
        bend = jnp.tanh(half)
        value = half + half * bend
        write(columns, value.astype(BF16))
        if slope_ref is not None:
            sigma = 0.5 + 0.5 * bend
            slope_ref[:, columns] = sigma + value - value * sigma


def hold_side(side_ref, place, cots_ref, segc_ref, segr_ref):
    events = cots_ref.shape[1]
    cots_ref[place] = side_ref[0:events, :]
    seg = side_ref[events : events + EXTRA, 0:events].astype(F32)[0:8]
    segr_ref[place] = seg
    segc_ref[place] = jnp.broadcast_to(jnp.transpose(seg)[:, 0:1], segc_ref.shape[1:])


class Chunks:
    def __init__(self, first, proj_ref, gatt_ref, segc_ref, segr_ref, join_ref):
        self.first, self.proj, self.gatt = first, proj_ref, gatt_ref
        self.segc, self.segr, self.join = segc_ref, segr_ref, join_ref
        self.width = gatt_ref.shape[2]

    def attend(self, i, start, stop, att_ref):
        def pair(j, _):
            mask = visible(i, j, self.segc, self.segr, False)
            qi, kj = i - self.first, j - self.first
            for h in range(HEADS):
                queries = self.proj[qi, :, head(2, h, self.width)]
                raw = dot_nt(queries, self.proj[kj, :, head(3, h, self.width)])
                half = raw * (0.5 * SCALE)
                value = half + half * jnp.tanh(half)
                weights = jnp.where(mask, value, 0.0).astype(BF16)
                added = dot(weights, self.proj[kj, :, head(1, h, self.width)])
                att_ref[:, head(0, h, self.width)] += added
            return 0

        lax.fori_loop(start, stop, pair, 0)

    def finish(self, i, own, att, cot, emb_ref, w_out_ref, out_ref):
        att_norm, att_inverse = normalize(att)
        gate = self.proj[i - self.first, :, 0 : self.width].astype(F32)
        grad_mixed = dot_nt(cot, w_out_ref[...])
        grad_att = norm_back(grad_mixed * gate, att_norm, att_inverse)
        self.gatt[i - self.first] = grad_att.astype(BF16)

        @pl.when(i == own)
        def _():
            mixed = (att_norm * gate).astype(BF16)
            out = emb_ref[...].astype(F32) + dot(mixed, w_out_ref[...])
            out_ref[...] = out.astype(BF16)
            self.join[:, 0 : self.width] = grad_mixed * att_norm

    def query_side(self, own, start, stop):
        def pair(j, _):
            mask = visible(own, j, self.segc, self.segr, False)
            me, kj = own - self.first, j - self.first
            for h in range(HEADS):
                keys = self.proj[kj, :, head(3, h, self.width)]
                half = dot_nt(self.proj[me, :, head(2, h, self.width)], keys) * (0.5 * SCALE)
                bend = jnp.tanh(half)
                value = half + half * bend
                sigma = 0.5 + 0.5 * bend
                slope = sigma + value - value * sigma
                grad_weights = dot_nt(
                    self.gatt[me, :, head(0, h, self.width)],
                    self.proj[kj, :, head(1, h, self.width)],
                )
                grad_raw = jnp.where(mask, grad_weights * slope * SCALE, 0.0).astype(BF16)
                self.join[:, head(2, h, self.width)] += dot(grad_raw, keys)
            return 0

        lax.fori_loop(start, stop, pair, 0)

    def key_side(self, own, start, stop):
        def pair(i, _):
            mask = visible(i, own, self.segc, self.segr, True)
            me, qi = own - self.first, i - self.first
            for h in range(HEADS):
                queries = self.proj[qi, :, head(2, h, self.width)]
                half = dot_nt(self.proj[me, :, head(3, h, self.width)], queries) * (0.5 * SCALE)
                bend = jnp.tanh(half)
                value = half + half * bend
                sigma = 0.5 + 0.5 * bend
                slope = sigma + value - value * sigma
                grad_att = self.gatt[qi, :, head(0, h, self.width)]
                grad_weights = dot_nt(self.proj[me, :, head(1, h, self.width)], grad_att)
                grad_raw = jnp.where(mask, grad_weights * slope * SCALE, 0.0).astype(BF16)
                weights = jnp.where(mask, value, 0.0).astype(BF16)
                self.join[:, head(3, h, self.width)] += dot(grad_raw, queries)
                self.join[:, head(1, h, self.width)] += dot(weights, grad_att)
            return 0

        lax.fori_loop(start, stop, pair, 0)


def early_kernel(
    index_ref,
    emb_ref,
    mate_ref,
    side_ref,
    side_mate_ref,
    w_in_ref,
    w_out_ref,
    proj_ref,
    att_ref,
    gatt_ref,
    join_ref,
    slope_ref,
    out_ref,
    segc_ref,
    segr_ref,
    cots_ref,
):
    own = index_ref[0]
    mate = index_ref[1]
    base = jnp.minimum(own, mate)
    last = jnp.maximum(own, mate)

    def write_to(place):
        def write(columns, value):
            proj_ref[place - base, :, columns] = value

        return write

    project(emb_ref[...], w_in_ref, write_to(own), slope_ref)
    project(mate_ref[...], w_in_ref, write_to(mate), None)
    hold_side(side_ref, own - base, cots_ref, segc_ref, segr_ref)
    hold_side(side_mate_ref, mate - base, cots_ref, segc_ref, segr_ref)
    att_ref[...] = jnp.zeros_like(att_ref)
    join_ref[...] = jnp.zeros_like(join_ref)
    chunks = Chunks(0, proj_ref, gatt_ref, segc_ref, segr_ref, join_ref)

    def forward(i, _):
        chunks.attend(i, 0, i + 1, att_ref.at[i])
        return 0

    lax.fori_loop(own - base, last - base + 1, forward, 0)

    @pl.when(base == 0)
    def _():
        def finish(i, _):
            chunks.finish(i, own, att_ref[i], cots_ref[i], emb_ref, w_out_ref, out_ref)
            return 0

        lax.fori_loop(own, last + 1, finish, 0)
        chunks.query_side(own, 0, own + 1)
        chunks.key_side(own, own, last + 1)


def late_kernel(count, *refs):
    index_ref, slots_ref = refs[:2]
    emb_refs = refs[2 : 2 + count]
    side_refs = refs[2 + count : 2 + 2 * count]
    (
        w_in_ref,
        w_out_ref,
        proj_pair_ref,
        att_pair_ref,
        gatt_pair_ref,
        join_early_ref,
        slope_ref,
        out_early_ref,
        out_ref,
        grad_ref,
        proj_ref,
        cot_ref,
        segc_ref,
        segr_ref,
        att_ref,
        gatt_ref,
        join_ref,
    ) = refs[2 + 2 * count :]
    own = index_ref[0]
    base = jnp.minimum(own, index_ref[1])
    last = jnp.maximum(own, index_ref[1])
    closed = base == 0

    for t in range(count):
        place = index_ref[t]
        hold_side(side_refs[t], place, cot_ref, segc_ref, segr_ref)
    for t in range(2):
        proj_ref[base + t] = proj_pair_ref[t]
        gatt_ref[base + t] = gatt_pair_ref[t]

    def write_to(place):
        def write(columns, value):
            proj_ref[place, :, columns] = value

        return write

    for t in range(2, count):
        project(emb_refs[t][...], w_in_ref, write_to(index_ref[t]), None)
    join_ref[...] = jnp.zeros_like(join_ref)
    chunks = Chunks(0, proj_ref, gatt_ref, segc_ref, segr_ref, join_ref)

    @pl.when(closed)
    def _():
        out_ref[...] = out_early_ref[...]

    def forward(i, _):
        begun = i <= last

        @pl.when(begun)
        def _():
            att_ref[...] = att_pair_ref[jnp.minimum(i - base, 1)]

        @pl.when(jnp.logical_not(begun))
        def _():
            att_ref[...] = jnp.zeros_like(att_ref)

        chunks.attend(i, 0, jnp.where(begun, base, i + 1), att_ref)
        chunks.finish(i, own, att_ref[...], cot_ref[i], emb_refs[0], w_out_ref, out_ref)
        return 0

    lax.fori_loop(jnp.where(closed, last + 1, own), count, forward, 0)
    chunks.query_side(own, jnp.where(closed, own + 1, 0), own + 1)
    chunks.key_side(own, jnp.where(closed, last + 1, own), count)

    grad_proj = ((join_ref[...] + join_early_ref[...]) * slope_ref[...]).astype(BF16)
    grad_normed = dot_nt(grad_proj, w_in_ref[...])
    normed, inverse = normalize(emb_refs[0][...].astype(F32))
    grad = norm_back(grad_normed, normed, inverse) + cot_ref[own].astype(F32)
    slot = iota((grad_ref.shape[0], grad.shape[0]), 0)
    hit = slot == slots_ref[0:1, :]
    for k in range(1, NIDS):
        hit = hit | (slot == slots_ref[k : k + 1, :])
    spread = jnp.where(hit, 1.0, 0.0).astype(BF16)
    grad_ref[...] = dot(spread, grad.astype(BF16)).astype(BF16)


def params(mebibytes=12):
    return pltpu.CompilerParams(vmem_limit_bytes=mebibytes * 1024 * 1024)


def flip(value, axis, offset):
    count = lax.axis_size(axis)
    return lax.ppermute(value, axis, [(i, i ^ offset) for i in range(count)])


def gather_blocks(value, axis, known):
    bit = lax.axis_size(axis)
    blocks = {0: value}
    while bit > 1:
        bit //= 2
        for t in list(blocks):
            blocks[t | bit] = known.get(t | bit)
            if blocks[t | bit] is None:
                blocks[t | bit] = flip(blocks[t], axis, bit)
    return [blocks[t] for t in range(lax.axis_size(axis))]


def after(value, earlier):
    return lax.optimization_barrier((value, earlier))[0]


def local(table, item_owner, item_row, segment_ids, w_in, w_out, cotangent):
    owners = lax.axis_size("table") * lax.axis_size("ctx")
    count = lax.axis_size("ctx")
    events, width = cotangent.shape
    id_count = events * NIDS
    capacity = 2 * ((id_count + owners - 1) // owners)
    slot_count = owners * capacity
    axes = ("table", "ctx")
    vmem = pl.BlockSpec(memory_space=pltpu.VMEM)
    smem = pl.BlockSpec(memory_space=pltpu.SMEM)

    def exchange(value):
        return lax.all_to_all(value, axes, split_axis=0, concat_axis=0, tiled=True)

    anywhere = pl.BlockSpec(memory_space=pl.ANY)
    slots, wanted, side = pl.pallas_call(
        functools.partial(slots_kernel, capacity),
        out_shape=(
            jax.ShapeDtypeStruct((8, events), jnp.int32),
            jax.ShapeDtypeStruct((owners, capacity), jnp.int32),
            jax.ShapeDtypeStruct((events + EXTRA, width), BF16),
        ),
        in_specs=[anywhere] * 4,
        out_specs=(vmem,) * 3,
        scratch_shapes=[
            pltpu.VMEM((NIDS, events), jnp.int32),
            pltpu.VMEM((NIDS, events), jnp.int32),
            pltpu.VMEM((1, events), jnp.int32),
            pltpu.SemaphoreType.DMA((4,)),
        ],
        compiler_params=params(WHOLE),
        name="slots",
    )(item_owner.T, item_row.T, segment_ids.reshape(1, events), cotangent)
    asked = exchange(wanted)
    rows = pl.pallas_call(
        select_kernel,
        out_shape=jax.ShapeDtypeStruct((slot_count, width), BF16),
        in_specs=[anywhere] * 2,
        out_specs=vmem,
        scratch_shapes=[
            pltpu.VMEM((owners, capacity), jnp.int32),
            pltpu.VMEM(table.shape, BF16),
            pltpu.SemaphoreType.DMA((2,)),
        ],
        compiler_params=params(WHOLE),
        name="select",
    )(asked, table)
    fetched = exchange(rows.reshape(owners, capacity, width)).reshape(slot_count, width)
    side_far = flip(side, "ctx", count // 2)
    side_mate = flip(side, "ctx", 1)
    side_blocks = gather_blocks(side, "ctx", {1: side_mate, count // 2: after(side_far, rows)})
    slots, side_blocks = lax.optimization_barrier((slots, side_blocks))
    embedded = pl.pallas_call(
        embed_kernel,
        out_shape=jax.ShapeDtypeStruct((events, width), BF16),
        compiler_params=params(),
        name="embed",
    )(slots, fetched)
    emb_far = flip(embedded, "ctx", count // 2)
    emb_mate = flip(embedded, "ctx", 1)
    index = lax.axis_index("ctx").astype(jnp.int32) ^ jnp.arange(count, dtype=jnp.int32)
    event_shape = jax.ShapeDtypeStruct((events, width), BF16)
    early = pl.pallas_call(
        early_kernel,
        out_shape=(
            jax.ShapeDtypeStruct((2, events, 4 * width), BF16),
            jax.ShapeDtypeStruct((2, events, width), F32),
            jax.ShapeDtypeStruct((2, events, width), BF16),
            jax.ShapeDtypeStruct((events, 4 * width), F32),
            jax.ShapeDtypeStruct((events, 4 * width), F32),
            event_shape,
        ),
        in_specs=[smem] + [vmem] * 6,
        out_specs=(vmem,) * 6,
        scratch_shapes=[
            pltpu.VMEM((2, events, 128), F32),
            pltpu.VMEM((2, 8, events), F32),
            pltpu.VMEM((2, events, width), BF16),
        ],
        compiler_params=params(20),
        name="early",
    )(index, embedded, emb_mate, *side_blocks[:2], w_in, w_out)
    emb_blocks = gather_blocks(embedded, "ctx", {1: emb_mate, count // 2: after(emb_far, early)})
    layer_out, slot_grad = pl.pallas_call(
        functools.partial(late_kernel, count),
        out_shape=(event_shape, jax.ShapeDtypeStruct((slot_count, width), BF16)),
        in_specs=[smem] + [vmem] * (9 + 2 * count),
        out_specs=(vmem, vmem),
        scratch_shapes=[
            pltpu.VMEM((count, events, 4 * width), BF16),
            pltpu.VMEM((count, events, width), BF16),
            pltpu.VMEM((count, events, 128), F32),
            pltpu.VMEM((count, 8, events), F32),
            pltpu.VMEM((events, width), F32),
            pltpu.VMEM((count, events, width), BF16),
            pltpu.VMEM((events, 4 * width), F32),
        ],
        compiler_params=params(28),
        name="late",
    )(index, slots, *emb_blocks, *side_blocks, w_in, w_out, *early)
    returned = exchange(slot_grad.reshape(owners, capacity, width)).reshape(slot_count, width)
    row_grad = pl.pallas_call(
        collect_kernel,
        out_shape=jax.ShapeDtypeStruct(table.shape, F32),
        compiler_params=params(),
        name="collect",
    )(asked, returned)
    return layer_out, row_grad


def solution(mesh):
    rows = P(("table", "ctx"), None)
    return jax.shard_map(
        local,
        mesh=mesh,
        in_specs=(rows, rows, rows, P("table", "ctx"), P(), P(), rows),
        out_specs=(rows, rows),
        check_vma=False,
    )
```

```python
import functools

import jax
import jax.numpy as jnp
from jax import lax
from jax.experimental import pallas as pl
from jax.experimental.pallas import tpu as pltpu
from jax.sharding import PartitionSpec as P

HEADS = 4
HEAD_DIM = 128
NIDS = 2
EPS = 1e-06

F32 = jnp.float32
BF16 = jnp.bfloat16


def dot(a, b):
    return jnp.dot(a, b, preferred_element_type=F32)


def dot_nt(a, b):
    return lax.dot_general(a, b, (((1,), (1,)), ((), ())), preferred_element_type=F32)


def iota(shape, dim):
    return lax.broadcasted_iota(jnp.int32, shape, dim)


def normalize(values):
    centred = values - jnp.mean(values, -1, keepdims=True)
    inverse = lax.rsqrt(jnp.mean(centred * centred, -1, keepdims=True) + EPS)
    return centred * inverse, inverse


def norm_back(grad_norm, normed, inverse):
    mean_grad = jnp.mean(grad_norm, -1, keepdims=True)
    mean_cross = jnp.mean(grad_norm * normed, -1, keepdims=True)
    return (grad_norm - mean_grad - normed * mean_cross) * inverse


def split_exact(values):
    return (values >> 4).astype(F32).astype(BF16), (values & 15).astype(F32).astype(BF16)


EXTRA = 16
WHOLE = 61


def slots_kernel(
    capacity,
    owner_in,
    row_in,
    seg_in,
    cot_in,
    slots_ref,
    wanted_ref,
    side_ref,
    owner_ref,
    row_ref,
    seg_ref,
    sems,
):
    events, width = cot_in.shape
    pairs = (
        (owner_in, owner_ref),
        (row_in, row_ref),
        (seg_in, seg_ref),
        (cot_in, side_ref.at[0:events]),
    )
    copies = [pltpu.make_async_copy(a, b, sems.at[i]) for i, (a, b) in enumerate(pairs)]
    for copy in copies:
        copy.start()
    for copy in copies[:3]:
        copy.wait()
    side_ref[events:, :] = jnp.zeros((EXTRA, width), BF16)
    segments = jnp.broadcast_to(seg_ref[...].astype(F32), (EXTRA, events))
    side_ref[events:, 0:events] = segments.astype(BF16)
    owners = wanted_ref.shape[0]
    owner = jnp.concatenate([owner_ref[k : k + 1, :] for k in range(NIDS)], 1)
    row = jnp.concatenate([row_ref[k : k + 1, :] for k in range(NIDS)], 1)
    ids = owner.shape[1]
    named = iota((owners, ids), 0) == owner
    named_f = jnp.where(named, 1.0, 0.0)
    before = jnp.where(iota((ids, ids), 0) < iota((ids, ids), 1), 1.0, 0.0).astype(BF16)
    earlier = dot(named_f.astype(BF16), before)
    rank = jnp.sum(earlier * named_f, 0, keepdims=True).astype(jnp.int32)
    slot = owner * capacity + rank
    slots_ref[...] = jnp.full(slots_ref.shape, -1, jnp.int32)
    for k in range(NIDS):
        slots_ref[k : k + 1, :] = slot[:, k * events : (k + 1) * events]
    ranked = jnp.where(iota((capacity, ids), 0) == rank, 1.0, 0.0).astype(BF16)
    high, low = (row >> 4).astype(F32), (row & 15).astype(F32)
    wanted = 16.0 * dot_nt((named_f * high).astype(BF16), ranked) + dot_nt(
        (named_f * low).astype(BF16), ranked
    )
    wanted_ref[...] = wanted.astype(jnp.int32)
    for copy in copies[3:]:
        copy.wait()


def select_kernel(asked_in, table_in, out_ref, asked_ref, table_ref, sems):
    pairs = ((asked_in, asked_ref), (table_in, table_ref))
    copies = [pltpu.make_async_copy(a, b, sems.at[i]) for i, (a, b) in enumerate(pairs)]
    for copy in copies:
        copy.start()
    copies[0].wait()
    owners, capacity = asked_ref.shape
    rows = table_ref.shape[0]
    columns = jnp.transpose(asked_ref[...])
    lane = iota((capacity, rows), 1)
    chosen = jnp.concatenate(
        [jnp.where(lane == columns[:, s : s + 1], 1.0, 0.0) for s in range(owners)], 0
    )
    chosen = chosen.astype(BF16)
    copies[1].wait()
    out_ref[...] = dot(chosen, table_ref[...]).astype(BF16)


def start_copies(pairs, sems):
    copies = [pltpu.make_async_copy(a, b, sems.at[i]) for i, (a, b) in enumerate(pairs)]
    for copy in copies:
        copy.start()
    return copies


def embed_kernel(count, slots_in, fetched_ref, w_in_in, w_out_in, *refs):
    side_ins = refs[:count]
    out_ref, slots_ref, w_in_ref, w_out_ref, sides_ref, sems = refs[count:]
    pairs = [(slots_in, slots_ref), (w_in_in, w_in_ref), (w_out_in, w_out_ref)]
    pairs += [(side_ins[t], sides_ref.at[t]) for t in range(count)]
    copies = start_copies(pairs, sems)
    events = out_ref.shape[0]
    slots = fetched_ref.shape[0]
    copies[0].wait()
    column = jnp.transpose(slots_ref[...])
    lane = iota((events, slots), 1)
    hit = lane == column[:, 0:1]
    for k in range(1, NIDS):
        hit = hit | (lane == column[:, k : k + 1])
    picked = jnp.where(hit, 1.0, 0.0).astype(BF16)
    out_ref[...] = dot(picked, fetched_ref[...]).astype(BF16)
    for copy in copies[1:]:
        copy.wait()


def collect_kernel(asked_ref, returned_ref, out_ref):
    owners, capacity = asked_ref.shape
    rows = out_ref.shape[0]
    slots = owners * capacity
    high, low = split_exact(asked_ref[...])
    place = jnp.where(
        iota((capacity, slots), 1) % capacity == iota((capacity, slots), 0), 1.0, 0.0
    ).astype(BF16)
    spread = 16.0 * dot(high, place) + dot(low, place)
    mine = iota((owners, slots), 1) // capacity == iota((owners, slots), 0)
    asked = jnp.sum(jnp.where(mine, spread, 0.0), 0, keepdims=True).astype(jnp.int32)
    chosen = jnp.where(iota((rows, slots), 0) == asked, 1.0, 0.0).astype(BF16)
    out_ref[...] = dot(chosen, returned_ref[...])


SCALE = HEAD_DIM ** (-0.5)


def head(part, h, width):
    return slice(part * width + h * HEAD_DIM, part * width + (h + 1) * HEAD_DIM)


def visible(query_chunk, key_chunk, segc_ref, segr_ref, flip):
    events = segr_ref.shape[2]
    first, second = iota((events, events), 0), iota((events, events), 1)
    if flip:
        same = segc_ref[key_chunk][:, 0:1] == segr_ref[query_chunk][0:1, :]
        return same & (first <= second + (query_chunk - key_chunk) * events)
    same = segc_ref[query_chunk][:, 0:1] == segr_ref[key_chunk][0:1, :]
    return same & (first + (query_chunk - key_chunk) * events >= second)


def project(emb, w_in_ref, write, slope_ref):
    width = emb.shape[1]
    normed = normalize(emb.astype(F32))[0].astype(BF16)
    for block in range(4):
        columns = slice(block * width, (block + 1) * width)
        half = 0.5 * dot(normed, w_in_ref[:, columns])
        bend = jnp.tanh(half)
        value = half + half * bend
        write(columns, value.astype(BF16))
        if slope_ref is not None:
            sigma = 0.5 + 0.5 * bend
            slope_ref[:, columns] = sigma + value - value * sigma


def hold_side(side_ref, place, cots_ref, segc_ref, segr_ref):
    events = cots_ref.shape[1]
    cots_ref[place] = side_ref[0:events, :]
    seg = side_ref[events : events + EXTRA, 0:events].astype(F32)[0:8]
    segr_ref[place] = seg
    segc_ref[place] = jnp.broadcast_to(jnp.transpose(seg)[:, 0:1], segc_ref.shape[1:])


class Chunks:
    def __init__(self, first, proj_ref, gatt_ref, segc_ref, segr_ref, join_ref):
        self.first, self.proj, self.gatt = first, proj_ref, gatt_ref
        self.segc, self.segr, self.join = segc_ref, segr_ref, join_ref
        self.width = gatt_ref.shape[2]

    def attend(self, i, start, stop, att_ref):
        def pair(j, _):
            mask = visible(i, j, self.segc, self.segr, False)
            qi, kj = i - self.first, j - self.first
            for h in range(HEADS):
                queries = self.proj[qi, :, head(2, h, self.width)]
                raw = dot_nt(queries, self.proj[kj, :, head(3, h, self.width)])
                half = raw * (0.5 * SCALE)
                value = half + half * jnp.tanh(half)
                weights = jnp.where(mask, value, 0.0).astype(BF16)
                added = dot(weights, self.proj[kj, :, head(1, h, self.width)])
                att_ref[:, head(0, h, self.width)] += added
            return 0

        lax.fori_loop(start, stop, pair, 0)

    def finish(self, i, own, att, cot, emb_ref, w_out_ref, out_ref):
        att_norm, att_inverse = normalize(att)
        gate = self.proj[i - self.first, :, 0 : self.width].astype(F32)
        grad_mixed = dot_nt(cot, w_out_ref[...])
        grad_att = norm_back(grad_mixed * gate, att_norm, att_inverse)
        self.gatt[i - self.first] = grad_att.astype(BF16)

        @pl.when(i == own)
        def _():
            mixed = (att_norm * gate).astype(BF16)
            out = emb_ref[...].astype(F32) + dot(mixed, w_out_ref[...])
            out_ref[...] = out.astype(BF16)
            self.join[:, 0 : self.width] = grad_mixed * att_norm

    def query_side(self, own, start, stop):
        def pair(j, _):
            mask = visible(own, j, self.segc, self.segr, False)
            me, kj = own - self.first, j - self.first
            for h in range(HEADS):
                keys = self.proj[kj, :, head(3, h, self.width)]
                half = dot_nt(self.proj[me, :, head(2, h, self.width)], keys) * (0.5 * SCALE)
                bend = jnp.tanh(half)
                value = half + half * bend
                sigma = 0.5 + 0.5 * bend
                slope = sigma + value - value * sigma
                grad_weights = dot_nt(
                    self.gatt[me, :, head(0, h, self.width)],
                    self.proj[kj, :, head(1, h, self.width)],
                )
                grad_raw = jnp.where(mask, grad_weights * slope * SCALE, 0.0).astype(BF16)
                self.join[:, head(2, h, self.width)] += dot(grad_raw, keys)
            return 0

        lax.fori_loop(start, stop, pair, 0)

    def key_side(self, own, start, stop):
        def pair(i, _):
            mask = visible(i, own, self.segc, self.segr, True)
            me, qi = own - self.first, i - self.first
            for h in range(HEADS):
                queries = self.proj[qi, :, head(2, h, self.width)]
                half = dot_nt(self.proj[me, :, head(3, h, self.width)], queries) * (0.5 * SCALE)
                bend = jnp.tanh(half)
                value = half + half * bend
                sigma = 0.5 + 0.5 * bend
                slope = sigma + value - value * sigma
                grad_att = self.gatt[qi, :, head(0, h, self.width)]
                grad_weights = dot_nt(self.proj[me, :, head(1, h, self.width)], grad_att)
                grad_raw = jnp.where(mask, grad_weights * slope * SCALE, 0.0).astype(BF16)
                weights = jnp.where(mask, value, 0.0).astype(BF16)
                self.join[:, head(3, h, self.width)] += dot(grad_raw, queries)
                self.join[:, head(1, h, self.width)] += dot(weights, grad_att)
            return 0

        lax.fori_loop(start, stop, pair, 0)


def early_kernel(
    index_ref,
    emb_ref,
    mate_ref,
    slots_ref,
    w_in_ref,
    w_out_ref,
    sides_ref,
    proj_ref,
    att_ref,
    gatt_ref,
    join_ref,
    slope_ref,
    out_ref,
    slots_on,
    w_in_on,
    w_out_on,
    sides_on,
    segc_ref,
    segr_ref,
    cots_ref,
    sems,
):
    copies = start_copies(
        ((slots_ref, slots_on), (w_in_ref, w_in_on), (w_out_ref, w_out_on), (sides_ref, sides_on)),
        sems,
    )
    own = index_ref[0]
    mate = index_ref[1]
    base = jnp.minimum(own, mate)
    last = jnp.maximum(own, mate)

    def write_to(place):
        def write(columns, value):
            proj_ref[place - base, :, columns] = value

        return write

    project(emb_ref[...], w_in_ref, write_to(own), slope_ref)
    project(mate_ref[...], w_in_ref, write_to(mate), None)
    hold_side(sides_ref.at[0], own - base, cots_ref, segc_ref, segr_ref)
    hold_side(sides_ref.at[1], mate - base, cots_ref, segc_ref, segr_ref)
    att_ref[...] = jnp.zeros_like(att_ref)
    join_ref[...] = jnp.zeros_like(join_ref)
    chunks = Chunks(0, proj_ref, gatt_ref, segc_ref, segr_ref, join_ref)

    def forward(i, _):
        chunks.attend(i, 0, i + 1, att_ref.at[i])
        return 0

    lax.fori_loop(own - base, last - base + 1, forward, 0)

    @pl.when(base == 0)
    def _():
        def finish(i, _):
            chunks.finish(i, own, att_ref[i], cots_ref[i], emb_ref, w_out_ref, out_ref)
            return 0

        lax.fori_loop(own, last + 1, finish, 0)
        chunks.query_side(own, 0, own + 1)
        chunks.key_side(own, own, last + 1)

    for copy in copies:
        copy.wait()


def late_kernel(count, *refs):
    index_ref = refs[0]
    emb_refs = refs[1 : 1 + count]
    (
        proj_pair_ref,
        att_pair_ref,
        gatt_pair_ref,
        join_early_ref,
        slope_ref,
        out_early_ref,
        slots_ref,
        w_in_ref,
        w_out_ref,
        sides_ref,
        out_ref,
        grad_ref,
        proj_ref,
        cot_ref,
        segc_ref,
        segr_ref,
        att_ref,
        gatt_ref,
        join_ref,
    ) = refs[1 + count :]
    own = index_ref[0]
    base = jnp.minimum(own, index_ref[1])
    last = jnp.maximum(own, index_ref[1])
    closed = base == 0

    for t in range(count):
        place = index_ref[t]
        hold_side(sides_ref.at[t], place, cot_ref, segc_ref, segr_ref)
    for t in range(2):
        proj_ref[base + t] = proj_pair_ref[t]
        gatt_ref[base + t] = gatt_pair_ref[t]

    def write_to(place):
        def write(columns, value):
            proj_ref[place, :, columns] = value

        return write

    for t in range(2, count):
        project(emb_refs[t][...], w_in_ref, write_to(index_ref[t]), None)
    join_ref[...] = jnp.zeros_like(join_ref)
    chunks = Chunks(0, proj_ref, gatt_ref, segc_ref, segr_ref, join_ref)

    @pl.when(closed)
    def _():
        out_ref[...] = out_early_ref[...]

    def forward(i, _):
        begun = i <= last

        @pl.when(begun)
        def _():
            att_ref[...] = att_pair_ref[jnp.minimum(i - base, 1)]

        @pl.when(jnp.logical_not(begun))
        def _():
            att_ref[...] = jnp.zeros_like(att_ref)

        chunks.attend(i, 0, jnp.where(begun, base, i + 1), att_ref)
        chunks.finish(i, own, att_ref[...], cot_ref[i], emb_refs[0], w_out_ref, out_ref)
        return 0

    lax.fori_loop(jnp.where(closed, last + 1, own), count, forward, 0)
    chunks.query_side(own, jnp.where(closed, own + 1, 0), own + 1)
    chunks.key_side(own, jnp.where(closed, last + 1, own), count)

    grad_proj = ((join_ref[...] + join_early_ref[...]) * slope_ref[...]).astype(BF16)
    grad_normed = dot_nt(grad_proj, w_in_ref[...])
    normed, inverse = normalize(emb_refs[0][...].astype(F32))
    grad = norm_back(grad_normed, normed, inverse) + cot_ref[own].astype(F32)
    slot = iota((grad_ref.shape[0], grad.shape[0]), 0)
    hit = slot == slots_ref[0:1, :]
    for k in range(1, NIDS):
        hit = hit | (slot == slots_ref[k : k + 1, :])
    spread = jnp.where(hit, 1.0, 0.0).astype(BF16)
    grad_ref[...] = dot(spread, grad.astype(BF16)).astype(BF16)


def params(mebibytes=12):
    return pltpu.CompilerParams(vmem_limit_bytes=mebibytes * 1024 * 1024)


def flip(value, axis, offset):
    count = lax.axis_size(axis)
    return lax.ppermute(value, axis, [(i, i ^ offset) for i in range(count)])


def gather_blocks(value, axis, known):
    bit = lax.axis_size(axis)
    blocks = {0: value}
    while bit > 1:
        bit //= 2
        for t in list(blocks):
            blocks[t | bit] = known.get(t | bit)
            if blocks[t | bit] is None:
                blocks[t | bit] = flip(blocks[t], axis, bit)
    return [blocks[t] for t in range(lax.axis_size(axis))]


def after(value, earlier):
    return lax.optimization_barrier((value, earlier))[0]


def local(table, item_owner, item_row, segment_ids, w_in, w_out, cotangent):
    owners = lax.axis_size("table") * lax.axis_size("ctx")
    count = lax.axis_size("ctx")
    events, width = cotangent.shape
    id_count = events * NIDS
    capacity = 2 * ((id_count + owners - 1) // owners)
    slot_count = owners * capacity
    axes = ("table", "ctx")
    vmem = pl.BlockSpec(memory_space=pltpu.VMEM)
    smem = pl.BlockSpec(memory_space=pltpu.SMEM)

    def exchange(value):
        return lax.all_to_all(value, axes, split_axis=0, concat_axis=0, tiled=True)

    anywhere = pl.BlockSpec(memory_space=pl.ANY)
    slots, wanted, side = pl.pallas_call(
        functools.partial(slots_kernel, capacity),
        out_shape=(
            jax.ShapeDtypeStruct((8, events), jnp.int32),
            jax.ShapeDtypeStruct((owners, capacity), jnp.int32),
            jax.ShapeDtypeStruct((events + EXTRA, width), BF16),
        ),
        in_specs=[anywhere] * 4,
        out_specs=(vmem,) * 3,
        scratch_shapes=[
            pltpu.VMEM((NIDS, events), jnp.int32),
            pltpu.VMEM((NIDS, events), jnp.int32),
            pltpu.VMEM((1, events), jnp.int32),
            pltpu.SemaphoreType.DMA((4,)),
        ],
        compiler_params=params(WHOLE),
        name="slots",
    )(item_owner.T, item_row.T, segment_ids.reshape(1, events), cotangent)
    asked = exchange(wanted)
    rows = pl.pallas_call(
        select_kernel,
        out_shape=jax.ShapeDtypeStruct((slot_count, width), BF16),
        in_specs=[anywhere] * 2,
        out_specs=vmem,
        scratch_shapes=[
            pltpu.VMEM((owners, capacity), jnp.int32),
            pltpu.VMEM(table.shape, BF16),
            pltpu.SemaphoreType.DMA((2,)),
        ],
        compiler_params=params(WHOLE),
        name="select",
    )(asked, table)
    fetched = exchange(rows.reshape(owners, capacity, width)).reshape(slot_count, width)
    side_far = flip(side, "ctx", count // 2)
    side_mate = flip(side, "ctx", 1)
    side_blocks = gather_blocks(side, "ctx", {1: side_mate, count // 2: after(side_far, rows)})
    held_shapes = (
        jax.ShapeDtypeStruct(slots.shape, jnp.int32),
        jax.ShapeDtypeStruct(w_in.shape, BF16),
        jax.ShapeDtypeStruct(w_out.shape, BF16),
        jax.ShapeDtypeStruct((count, events + EXTRA, width), BF16),
    )
    embedded, *held = pl.pallas_call(
        functools.partial(embed_kernel, count),
        out_shape=(jax.ShapeDtypeStruct((events, width), BF16),) + held_shapes,
        in_specs=[anywhere, vmem] + [anywhere] * (2 + count),
        out_specs=(vmem,) * 5,
        scratch_shapes=[pltpu.SemaphoreType.DMA((3 + count,))],
        compiler_params=params(),
        name="embed",
    )(slots, fetched, w_in, w_out, *side_blocks)
    emb_far = flip(embedded, "ctx", count // 2)
    emb_mate = flip(embedded, "ctx", 1)
    index = lax.axis_index("ctx").astype(jnp.int32) ^ jnp.arange(count, dtype=jnp.int32)
    event_shape = jax.ShapeDtypeStruct((events, width), BF16)
    early = pl.pallas_call(
        early_kernel,
        out_shape=(
            jax.ShapeDtypeStruct((2, events, 4 * width), BF16),
            jax.ShapeDtypeStruct((2, events, width), F32),
            jax.ShapeDtypeStruct((2, events, width), BF16),
            jax.ShapeDtypeStruct((events, 4 * width), F32),
            jax.ShapeDtypeStruct((events, 4 * width), F32),
            event_shape,
        )
        + held_shapes,
        in_specs=[smem] + [vmem] * 6,
        out_specs=(vmem,) * 10,
        scratch_shapes=[
            pltpu.VMEM((2, events, 128), F32),
            pltpu.VMEM((2, 8, events), F32),
            pltpu.VMEM((2, events, width), BF16),
            pltpu.SemaphoreType.DMA((4,)),
        ],
        compiler_params=params(20),
        name="early",
    )(index, embedded, emb_mate, *held)
    emb_blocks = gather_blocks(embedded, "ctx", {1: emb_mate, count // 2: after(emb_far, early)})
    layer_out, slot_grad = pl.pallas_call(
        functools.partial(late_kernel, count),
        out_shape=(event_shape, jax.ShapeDtypeStruct((slot_count, width), BF16)),
        in_specs=[smem] + [vmem] * (10 + count),
        out_specs=(vmem, vmem),
        scratch_shapes=[
            pltpu.VMEM((count, events, 4 * width), BF16),
            pltpu.VMEM((count, events, width), BF16),
            pltpu.VMEM((count, events, 128), F32),
            pltpu.VMEM((count, 8, events), F32),
            pltpu.VMEM((events, width), F32),
            pltpu.VMEM((count, events, width), BF16),
            pltpu.VMEM((events, 4 * width), F32),
        ],
        compiler_params=params(28),
        name="late",
    )(index, *emb_blocks, *early)
    returned = exchange(slot_grad.reshape(owners, capacity, width)).reshape(slot_count, width)
    row_grad = pl.pallas_call(
        collect_kernel,
        out_shape=jax.ShapeDtypeStruct(table.shape, F32),
        compiler_params=params(),
        name="collect",
    )(asked, returned)
    return layer_out, row_grad


def solution(mesh):
    rows = P(("table", "ctx"), None)
    return jax.shard_map(
        local,
        mesh=mesh,
        in_specs=(rows, rows, rows, P("table", "ctx"), P(), P(), rows),
        out_specs=(rows, rows),
        check_vma=False,
    )
```

```python
import functools

import jax
import jax.numpy as jnp
from jax import lax
from jax.experimental import pallas as pl
from jax.experimental.pallas import tpu as pltpu
from jax.sharding import PartitionSpec as P

HEADS = 4
HEAD_DIM = 128
NIDS = 2
EPS = 1e-06

F32 = jnp.float32
BF16 = jnp.bfloat16


def dot(a, b):
    return jnp.dot(a, b, preferred_element_type=F32)


def dot_nt(a, b):
    return lax.dot_general(a, b, (((1,), (1,)), ((), ())), preferred_element_type=F32)


def iota(shape, dim):
    return lax.broadcasted_iota(jnp.int32, shape, dim)


def normalize(values):
    centred = values - jnp.mean(values, -1, keepdims=True)
    inverse = lax.rsqrt(jnp.mean(centred * centred, -1, keepdims=True) + EPS)
    return centred * inverse, inverse


def norm_back(grad_norm, normed, inverse):
    mean_grad = jnp.mean(grad_norm, -1, keepdims=True)
    mean_cross = jnp.mean(grad_norm * normed, -1, keepdims=True)
    return (grad_norm - mean_grad - normed * mean_cross) * inverse


def split_exact(values):
    return (values >> 4).astype(F32).astype(BF16), (values & 15).astype(F32).astype(BF16)


def start_copies(pairs, sems):
    copies = [pltpu.make_async_copy(a, b, sems.at[i]) for i, (a, b) in enumerate(pairs)]
    for copy in copies:
        copy.start()
    return copies


EXTRA = 16


def slots_kernel(
    capacity,
    owner_in,
    row_in,
    seg_in,
    cot_in,
    slots_ref,
    wanted_ref,
    side_out,
    owner_ref,
    row_ref,
    seg_ref,
    mark_ref,
    sems,
):
    events, width = cot_in.shape
    pairs = (
        (owner_in, owner_ref),
        (row_in, row_ref),
        (seg_in, seg_ref),
        (cot_in, side_out.at[0:events]),
    )
    copies = start_copies(pairs, sems)
    for copy in copies[:3]:
        copy.wait()
    mark_ref[...] = jnp.zeros((EXTRA, width), BF16)
    segments = jnp.broadcast_to(seg_ref[...].astype(F32), (EXTRA, events))
    mark_ref[:, 0:events] = segments.astype(BF16)
    mark = pltpu.make_async_copy(mark_ref, side_out.at[events : events + EXTRA], sems.at[4])
    mark.start()
    copies.append(mark)
    owners = wanted_ref.shape[0]
    owner = jnp.concatenate([owner_ref[k : k + 1, :] for k in range(NIDS)], 1)
    row = jnp.concatenate([row_ref[k : k + 1, :] for k in range(NIDS)], 1)
    ids = owner.shape[1]
    named = iota((owners, ids), 0) == owner
    named_f = jnp.where(named, 1.0, 0.0)
    before = jnp.where(iota((ids, ids), 0) < iota((ids, ids), 1), 1.0, 0.0).astype(BF16)
    earlier = dot(named_f.astype(BF16), before)
    rank = jnp.sum(earlier * named_f, 0, keepdims=True).astype(jnp.int32)
    slot = owner * capacity + rank
    slots_ref[...] = jnp.full(slots_ref.shape, -1, jnp.int32)
    for k in range(NIDS):
        slots_ref[k : k + 1, :] = slot[:, k * events : (k + 1) * events]
    ranked = jnp.where(iota((capacity, ids), 0) == rank, 1.0, 0.0).astype(BF16)
    high, low = (row >> 4).astype(F32), (row & 15).astype(F32)
    wanted = 16.0 * dot_nt((named_f * high).astype(BF16), ranked) + dot_nt(
        (named_f * low).astype(BF16), ranked
    )
    wanted_ref[...] = wanted.astype(jnp.int32)
    for copy in copies[3:]:
        copy.wait()


def select_kernel(asked_ref, table_in, out_ref, table_ref, rows_ref, sems):
    (table_copy,) = start_copies(((table_in, table_ref),), sems)
    owners, capacity = asked_ref.shape
    rows = table_ref.shape[0]
    parts = sems.shape[0] - 1
    step = owners // parts
    columns = jnp.transpose(asked_ref[...])
    lane = iota((capacity, rows), 1)
    copies = []
    for part in range(parts):
        sources = range(part * step, (part + 1) * step)
        chosen = [jnp.where(lane == columns[:, s : s + 1], 1.0, 0.0) for s in sources]
        chosen = jnp.concatenate(chosen, 0).astype(BF16)
        if part == 0:
            table_copy.wait()
        place = pl.ds(part * step * capacity, step * capacity)
        rows_ref[place, :] = dot(chosen, table_ref[...]).astype(BF16)
        copy = pltpu.make_async_copy(rows_ref.at[place], out_ref.at[place], sems.at[1 + part])
        copy.start()
        copies.append(copy)
    for copy in copies:
        copy.wait()


def embed_kernel(slots_ref, fetched_ref, out_ref):
    events = out_ref.shape[0]
    slots = fetched_ref.shape[0]
    column = jnp.transpose(slots_ref[...])
    lane = iota((events, slots), 1)
    hit = lane == column[:, 0:1]
    for k in range(1, NIDS):
        hit = hit | (lane == column[:, k : k + 1])
    picked = jnp.where(hit, 1.0, 0.0).astype(BF16)
    out_ref[...] = dot(picked, fetched_ref[...]).astype(BF16)


def collect_kernel(asked_ref, returned_ref, out_ref):
    owners, capacity = asked_ref.shape
    rows = out_ref.shape[0]
    slots = owners * capacity
    high, low = split_exact(asked_ref[...])
    place = jnp.where(
        iota((capacity, slots), 1) % capacity == iota((capacity, slots), 0), 1.0, 0.0
    ).astype(BF16)
    spread = 16.0 * dot(high, place) + dot(low, place)
    mine = iota((owners, slots), 1) // capacity == iota((owners, slots), 0)
    asked = jnp.sum(jnp.where(mine, spread, 0.0), 0, keepdims=True).astype(jnp.int32)
    chosen = jnp.where(iota((rows, slots), 0) == asked, 1.0, 0.0).astype(BF16)
    out_ref[...] = dot(chosen, returned_ref[...])


SCALE = HEAD_DIM ** (-0.5)


def head(part, h, width):
    return slice(part * width + h * HEAD_DIM, part * width + (h + 1) * HEAD_DIM)


def visible(query_chunk, key_chunk, segc_ref, segr_ref, flip):
    events = segr_ref.shape[2]
    first, second = iota((events, events), 0), iota((events, events), 1)
    if flip:
        same = segc_ref[key_chunk][:, 0:1] == segr_ref[query_chunk][0:1, :]
        return same & (first <= second + (query_chunk - key_chunk) * events)
    same = segc_ref[query_chunk][:, 0:1] == segr_ref[key_chunk][0:1, :]
    return same & (first + (query_chunk - key_chunk) * events >= second)


def project(emb, w_in_ref, write, slope_ref):
    width = emb.shape[1]
    normed = normalize(emb.astype(F32))[0].astype(BF16)
    for block in range(4):
        columns = slice(block * width, (block + 1) * width)
        half = 0.5 * dot(normed, w_in_ref[:, columns])
        bend = jnp.tanh(half)
        value = half + half * bend
        write(columns, value.astype(BF16))
        if slope_ref is not None:
            sigma = 0.5 + 0.5 * bend
            slope_ref[:, columns] = sigma + value - value * sigma


def hold_side(side_ref, place, cots_ref, segc_ref, segr_ref):
    events = cots_ref.shape[1]
    cots_ref[place] = side_ref[0:events, :]
    seg = side_ref[events : events + EXTRA, 0:events].astype(F32)[0:8]
    segr_ref[place] = seg
    segc_ref[place] = jnp.broadcast_to(jnp.transpose(seg)[:, 0:1], segc_ref.shape[1:])


class Chunks:
    def __init__(self, first, proj_ref, gatt_ref, segc_ref, segr_ref, join_ref):
        self.first, self.proj, self.gatt = first, proj_ref, gatt_ref
        self.segc, self.segr, self.join = segc_ref, segr_ref, join_ref
        self.width = gatt_ref.shape[2]

    def attend(self, i, start, stop, att_ref):
        def pair(j, _):
            mask = visible(i, j, self.segc, self.segr, False)
            qi, kj = i - self.first, j - self.first
            for h in range(HEADS):
                queries = self.proj[qi, :, head(2, h, self.width)]
                raw = dot_nt(queries, self.proj[kj, :, head(3, h, self.width)])
                half = raw * (0.5 * SCALE)
                value = half + half * jnp.tanh(half)
                weights = jnp.where(mask, value, 0.0).astype(BF16)
                added = dot(weights, self.proj[kj, :, head(1, h, self.width)])
                att_ref[:, head(0, h, self.width)] += added
            return 0

        lax.fori_loop(start, stop, pair, 0)

    def finish(self, i, own, att, cot, emb_ref, w_out_ref, out_ref):
        att_norm, att_inverse = normalize(att)
        gate = self.proj[i - self.first, :, 0 : self.width].astype(F32)
        grad_mixed = dot_nt(cot, w_out_ref[...])
        grad_att = norm_back(grad_mixed * gate, att_norm, att_inverse)
        self.gatt[i - self.first] = grad_att.astype(BF16)

        @pl.when(i == own)
        def _():
            mixed = (att_norm * gate).astype(BF16)
            out = emb_ref[...].astype(F32) + dot(mixed, w_out_ref[...])
            out_ref[...] = out.astype(BF16)
            self.join[:, 0 : self.width] = grad_mixed * att_norm

    def query_side(self, own, start, stop):
        def pair(j, _):
            mask = visible(own, j, self.segc, self.segr, False)
            me, kj = own - self.first, j - self.first
            for h in range(HEADS):
                keys = self.proj[kj, :, head(3, h, self.width)]
                half = dot_nt(self.proj[me, :, head(2, h, self.width)], keys) * (0.5 * SCALE)
                bend = jnp.tanh(half)
                value = half + half * bend
                sigma = 0.5 + 0.5 * bend
                slope = sigma + value - value * sigma
                grad_weights = dot_nt(
                    self.gatt[me, :, head(0, h, self.width)],
                    self.proj[kj, :, head(1, h, self.width)],
                )
                grad_raw = jnp.where(mask, grad_weights * slope * SCALE, 0.0).astype(BF16)
                self.join[:, head(2, h, self.width)] += dot(grad_raw, keys)
            return 0

        lax.fori_loop(start, stop, pair, 0)

    def key_side(self, own, start, stop):
        def pair(i, _):
            mask = visible(i, own, self.segc, self.segr, True)
            me, qi = own - self.first, i - self.first
            for h in range(HEADS):
                queries = self.proj[qi, :, head(2, h, self.width)]
                half = dot_nt(self.proj[me, :, head(3, h, self.width)], queries) * (0.5 * SCALE)
                bend = jnp.tanh(half)
                value = half + half * bend
                sigma = 0.5 + 0.5 * bend
                slope = sigma + value - value * sigma
                grad_att = self.gatt[qi, :, head(0, h, self.width)]
                grad_weights = dot_nt(self.proj[me, :, head(1, h, self.width)], grad_att)
                grad_raw = jnp.where(mask, grad_weights * slope * SCALE, 0.0).astype(BF16)
                weights = jnp.where(mask, value, 0.0).astype(BF16)
                self.join[:, head(3, h, self.width)] += dot(grad_raw, queries)
                self.join[:, head(1, h, self.width)] += dot(weights, grad_att)
            return 0

        lax.fori_loop(start, stop, pair, 0)


def early_kernel(count, index_ref, emb_ref, mate_ref, slots_in, w_in_in, w_out_in, *refs):
    (
        proj_ref,
        att_ref,
        gatt_ref,
        join_ref,
        slope_ref,
        out_ref,
        slots_ref,
        w_in_ref,
        w_out_ref,
        sides_ref,
        segc_ref,
        segr_ref,
        cots_ref,
        sems,
    ) = refs[count:]
    pairs = [(w_in_in, w_in_ref), (w_out_in, w_out_ref), (slots_in, slots_ref)]
    pairs += [(refs[t], sides_ref.at[t]) for t in range(count)]
    copies = start_copies(pairs, sems)
    copies[0].wait()
    own = index_ref[0]
    mate = index_ref[1]
    base = jnp.minimum(own, mate)
    last = jnp.maximum(own, mate)

    def write_to(place):
        def write(columns, value):
            proj_ref[place - base, :, columns] = value

        return write

    project(emb_ref[...], w_in_ref, write_to(own), slope_ref)
    project(mate_ref[...], w_in_ref, write_to(mate), None)
    for copy in copies[1:]:
        copy.wait()
    hold_side(sides_ref.at[0], own - base, cots_ref, segc_ref, segr_ref)
    hold_side(sides_ref.at[1], mate - base, cots_ref, segc_ref, segr_ref)
    att_ref[...] = jnp.zeros_like(att_ref)
    join_ref[...] = jnp.zeros_like(join_ref)
    chunks = Chunks(0, proj_ref, gatt_ref, segc_ref, segr_ref, join_ref)

    def forward(i, _):
        chunks.attend(i, 0, i + 1, att_ref.at[i])
        return 0

    lax.fori_loop(own - base, last - base + 1, forward, 0)

    @pl.when(base == 0)
    def _():
        def finish(i, _):
            chunks.finish(i, own, att_ref[i], cots_ref[i], emb_ref, w_out_ref, out_ref)
            return 0

        lax.fori_loop(own, last + 1, finish, 0)
        chunks.query_side(own, 0, own + 1)
        chunks.key_side(own, own, last + 1)


def late_kernel(count, *refs):
    index_ref = refs[0]
    emb_refs = refs[1 : 1 + count]
    (
        proj_pair_ref,
        att_pair_ref,
        gatt_pair_ref,
        join_early_ref,
        slope_ref,
        out_early_ref,
        slots_ref,
        w_in_ref,
        w_out_ref,
        sides_ref,
        out_ref,
        grad_ref,
        proj_ref,
        cot_ref,
        segc_ref,
        segr_ref,
        att_ref,
        gatt_ref,
        join_ref,
    ) = refs[1 + count :]
    own = index_ref[0]
    base = jnp.minimum(own, index_ref[1])
    last = jnp.maximum(own, index_ref[1])
    closed = base == 0

    for t in range(count):
        place = index_ref[t]
        hold_side(sides_ref.at[t], place, cot_ref, segc_ref, segr_ref)
    for t in range(2):
        proj_ref[base + t] = proj_pair_ref[t]
        gatt_ref[base + t] = gatt_pair_ref[t]

    def write_to(place):
        def write(columns, value):
            proj_ref[place, :, columns] = value

        return write

    for t in range(2, count):
        project(emb_refs[t][...], w_in_ref, write_to(index_ref[t]), None)
    join_ref[...] = jnp.zeros_like(join_ref)
    chunks = Chunks(0, proj_ref, gatt_ref, segc_ref, segr_ref, join_ref)

    @pl.when(closed)
    def _():
        out_ref[...] = out_early_ref[...]

    def forward(i, _):
        begun = i <= last

        @pl.when(begun)
        def _():
            att_ref[...] = att_pair_ref[jnp.minimum(i - base, 1)]

        @pl.when(jnp.logical_not(begun))
        def _():
            att_ref[...] = jnp.zeros_like(att_ref)

        chunks.attend(i, 0, jnp.where(begun, base, i + 1), att_ref)
        chunks.finish(i, own, att_ref[...], cot_ref[i], emb_refs[0], w_out_ref, out_ref)
        return 0

    lax.fori_loop(jnp.where(closed, last + 1, own), count, forward, 0)
    chunks.query_side(own, jnp.where(closed, own + 1, 0), own + 1)
    chunks.key_side(own, jnp.where(closed, last + 1, own), count)

    grad_proj = ((join_ref[...] + join_early_ref[...]) * slope_ref[...]).astype(BF16)
    grad_normed = dot_nt(grad_proj, w_in_ref[...])
    normed, inverse = normalize(emb_refs[0][...].astype(F32))
    grad = norm_back(grad_normed, normed, inverse) + cot_ref[own].astype(F32)
    slot = iota((grad_ref.shape[0], grad.shape[0]), 0)
    hit = slot == slots_ref[0:1, :]
    for k in range(1, NIDS):
        hit = hit | (slot == slots_ref[k : k + 1, :])
    spread = jnp.where(hit, 1.0, 0.0).astype(BF16)
    grad_ref[...] = dot(spread, grad.astype(BF16)).astype(BF16)


def in_hbm(*arrays):
    return [pltpu.with_memory_space_constraint(a, pltpu.HBM) for a in arrays]


def params(mebibytes=12):
    return pltpu.CompilerParams(vmem_limit_bytes=mebibytes * 1024 * 1024)


def flip(value, axis, offset):
    count = lax.axis_size(axis)
    return lax.ppermute(value, axis, [(i, i ^ offset) for i in range(count)])


def gather_blocks(value, axis, known):
    bit = lax.axis_size(axis)
    blocks = {0: value}
    while bit > 1:
        bit //= 2
        for t in list(blocks):
            blocks[t | bit] = known.get(t | bit)
            if blocks[t | bit] is None:
                blocks[t | bit] = flip(blocks[t], axis, bit)
    return [blocks[t] for t in range(lax.axis_size(axis))]


def after(value, earlier):
    return lax.optimization_barrier((value, earlier))[0]


def local(table, item_owner, item_row, segment_ids, w_in, w_out, cotangent):
    owners = lax.axis_size("table") * lax.axis_size("ctx")
    count = lax.axis_size("ctx")
    events, width = cotangent.shape
    id_count = events * NIDS
    capacity = 2 * ((id_count + owners - 1) // owners)
    slot_count = owners * capacity
    axes = ("table", "ctx")
    vmem = pl.BlockSpec(memory_space=pltpu.VMEM)
    smem = pl.BlockSpec(memory_space=pltpu.SMEM)

    def exchange(value):
        return lax.all_to_all(value, axes, split_axis=0, concat_axis=0, tiled=True)

    hbm = pl.BlockSpec(memory_space=pltpu.HBM)
    slots, wanted, side = pl.pallas_call(
        functools.partial(slots_kernel, capacity),
        out_shape=(
            jax.ShapeDtypeStruct((8, events), jnp.int32),
            jax.ShapeDtypeStruct((owners, capacity), jnp.int32),
            pltpu.HBM((events + EXTRA, width), BF16),
        ),
        in_specs=[hbm] * 4,
        out_specs=(vmem, vmem, hbm),
        scratch_shapes=[
            pltpu.VMEM((NIDS, events), jnp.int32),
            pltpu.VMEM((NIDS, events), jnp.int32),
            pltpu.VMEM((1, events), jnp.int32),
            pltpu.VMEM((EXTRA, width), BF16),
            pltpu.SemaphoreType.DMA((5,)),
        ],
        compiler_params=params(),
        name="slots",
    )(*in_hbm(item_owner.T, item_row.T, segment_ids.reshape(1, events), cotangent))
    asked = exchange(wanted)
    rows = pl.pallas_call(
        select_kernel,
        out_shape=pltpu.HBM((slot_count, width), BF16),
        in_specs=[vmem, hbm],
        out_specs=hbm,
        scratch_shapes=[
            pltpu.VMEM(table.shape, BF16),
            pltpu.VMEM((slot_count, width), BF16),
            pltpu.SemaphoreType.DMA((5,)),
        ],
        compiler_params=params(),
        name="select",
    )(asked, *in_hbm(table))
    fetched = exchange(rows.reshape(owners, capacity, width)).reshape(slot_count, width)
    side_far = flip(side, "ctx", count // 2)
    side_mate = flip(side, "ctx", 1)
    side_blocks = gather_blocks(side, "ctx", {1: side_mate, count // 2: after(side_far, rows)})
    held_shapes = (
        jax.ShapeDtypeStruct(slots.shape, jnp.int32),
        jax.ShapeDtypeStruct(w_in.shape, BF16),
        jax.ShapeDtypeStruct(w_out.shape, BF16),
        jax.ShapeDtypeStruct((count, events + EXTRA, width), BF16),
    )
    side_blocks = in_hbm(*side_blocks)
    fetched, side_blocks = lax.optimization_barrier((fetched, side_blocks))
    embedded = pl.pallas_call(
        embed_kernel,
        out_shape=jax.ShapeDtypeStruct((events, width), BF16),
        compiler_params=params(),
        name="embed",
    )(slots, fetched)
    emb_far = flip(embedded, "ctx", count // 2)
    emb_mate = flip(embedded, "ctx", 1)
    index = lax.axis_index("ctx").astype(jnp.int32) ^ jnp.arange(count, dtype=jnp.int32)
    event_shape = jax.ShapeDtypeStruct((events, width), BF16)
    early = pl.pallas_call(
        functools.partial(early_kernel, count),
        out_shape=(
            jax.ShapeDtypeStruct((2, events, 4 * width), BF16),
            jax.ShapeDtypeStruct((2, events, width), F32),
            jax.ShapeDtypeStruct((2, events, width), BF16),
            jax.ShapeDtypeStruct((events, 4 * width), F32),
            jax.ShapeDtypeStruct((events, 4 * width), F32),
            event_shape,
        )
        + held_shapes,
        in_specs=[smem, vmem, vmem] + [hbm] * (3 + count),
        out_specs=(vmem,) * 10,
        scratch_shapes=[
            pltpu.VMEM((2, events, 128), F32),
            pltpu.VMEM((2, 8, events), F32),
            pltpu.VMEM((2, events, width), BF16),
            pltpu.SemaphoreType.DMA((3 + count,)),
        ],
        compiler_params=params(20),
        name="early",
    )(index, embedded, emb_mate, *in_hbm(slots, w_in, w_out), *side_blocks)
    emb_blocks = gather_blocks(embedded, "ctx", {1: emb_mate, count // 2: after(emb_far, early)})
    layer_out, slot_grad = pl.pallas_call(
        functools.partial(late_kernel, count),
        out_shape=(event_shape, jax.ShapeDtypeStruct((slot_count, width), BF16)),
        in_specs=[smem] + [vmem] * (10 + count),
        out_specs=(vmem, vmem),
        scratch_shapes=[
            pltpu.VMEM((count, events, 4 * width), BF16),
            pltpu.VMEM((count, events, width), BF16),
            pltpu.VMEM((count, events, 128), F32),
            pltpu.VMEM((count, 8, events), F32),
            pltpu.VMEM((events, width), F32),
            pltpu.VMEM((count, events, width), BF16),
            pltpu.VMEM((events, 4 * width), F32),
        ],
        compiler_params=params(28),
        name="late",
    )(index, *emb_blocks, *early)
    returned = exchange(slot_grad.reshape(owners, capacity, width)).reshape(slot_count, width)
    row_grad = pl.pallas_call(
        collect_kernel,
        out_shape=jax.ShapeDtypeStruct(table.shape, F32),
        compiler_params=params(),
        name="collect",
    )(asked, returned)
    return layer_out, row_grad


def solution(mesh):
    rows = P(("table", "ctx"), None)
    return jax.shard_map(
        local,
        mesh=mesh,
        in_specs=(rows, rows, rows, P("table", "ctx"), P(), P(), rows),
        out_specs=(rows, rows),
        check_vma=False,
    )
```

```python
import functools

import jax
import jax.numpy as jnp
from jax import lax
from jax.experimental import pallas as pl
from jax.experimental.pallas import tpu as pltpu
from jax.sharding import PartitionSpec as P

HEADS = 4
HEAD_DIM = 128
NIDS = 2
EPS = 1e-06

F32 = jnp.float32
BF16 = jnp.bfloat16


def dot(a, b):
    return jnp.dot(a, b, preferred_element_type=F32)


def dot_nt(a, b):
    return lax.dot_general(a, b, (((1,), (1,)), ((), ())), preferred_element_type=F32)


def iota(shape, dim):
    return lax.broadcasted_iota(jnp.int32, shape, dim)


def normalize(values):
    centred = values - jnp.mean(values, -1, keepdims=True)
    inverse = lax.rsqrt(jnp.mean(centred * centred, -1, keepdims=True) + EPS)
    return centred * inverse, inverse


def norm_back(grad_norm, normed, inverse):
    mean_grad = jnp.mean(grad_norm, -1, keepdims=True)
    mean_cross = jnp.mean(grad_norm * normed, -1, keepdims=True)
    return (grad_norm - mean_grad - normed * mean_cross) * inverse


def split_exact(values):
    return (values >> 4).astype(F32).astype(BF16), (values & 15).astype(F32).astype(BF16)


def start_copies(pairs, sems):
    copies = [pltpu.make_async_copy(a, b, sems.at[i]) for i, (a, b) in enumerate(pairs)]
    for copy in copies:
        copy.start()
    return copies


EXTRA = 16


def slots_kernel(
    capacity,
    owner_in,
    row_in,
    seg_in,
    cot_in,
    slots_ref,
    wanted_ref,
    side_ref,
    owner_ref,
    row_ref,
    seg_ref,
    sems,
):
    events, width = cot_in.shape
    pairs = (
        (owner_in, owner_ref),
        (row_in, row_ref),
        (seg_in, seg_ref),
        (cot_in, side_ref.at[0:events]),
    )
    copies = start_copies(pairs, sems)
    for copy in copies[:3]:
        copy.wait()
    side_ref[events:, :] = jnp.zeros((EXTRA, width), BF16)
    segments = jnp.broadcast_to(seg_ref[...].astype(F32), (EXTRA, events))
    side_ref[events:, 0:events] = segments.astype(BF16)
    owners = wanted_ref.shape[0]
    owner = jnp.concatenate([owner_ref[k : k + 1, :] for k in range(NIDS)], 1)
    row = jnp.concatenate([row_ref[k : k + 1, :] for k in range(NIDS)], 1)
    ids = owner.shape[1]
    named = iota((owners, ids), 0) == owner
    named_f = jnp.where(named, 1.0, 0.0)
    before = jnp.where(iota((ids, ids), 0) < iota((ids, ids), 1), 1.0, 0.0).astype(BF16)
    earlier = dot(named_f.astype(BF16), before)
    rank = jnp.sum(earlier * named_f, 0, keepdims=True).astype(jnp.int32)
    slot = owner * capacity + rank
    slots_ref[...] = jnp.full(slots_ref.shape, -1, jnp.int32)
    for k in range(NIDS):
        slots_ref[k : k + 1, :] = slot[:, k * events : (k + 1) * events]
    ranked = jnp.where(iota((capacity, ids), 0) == rank, 1.0, 0.0).astype(BF16)
    high, low = (row >> 4).astype(F32), (row & 15).astype(F32)
    wanted = 16.0 * dot_nt((named_f * high).astype(BF16), ranked) + dot_nt(
        (named_f * low).astype(BF16), ranked
    )
    wanted_ref[...] = wanted.astype(jnp.int32)
    for copy in copies[3:]:
        copy.wait()


def select_kernel(asked_ref, table_in, out_ref, table_ref, rows_ref, sems):
    (table_copy,) = start_copies(((table_in, table_ref),), sems)
    owners, capacity = asked_ref.shape
    rows = table_ref.shape[0]
    parts = sems.shape[0] - 1
    step = owners // parts
    columns = jnp.transpose(asked_ref[...])
    lane = iota((capacity, rows), 1)
    copies = []
    for part in range(parts):
        sources = range(part * step, (part + 1) * step)
        chosen = [jnp.where(lane == columns[:, s : s + 1], 1.0, 0.0) for s in sources]
        chosen = jnp.concatenate(chosen, 0).astype(BF16)
        if part == 0:
            table_copy.wait()
        place = pl.ds(part * step * capacity, step * capacity)
        rows_ref[place, :] = dot(chosen, table_ref[...]).astype(BF16)
        copy = pltpu.make_async_copy(rows_ref.at[place], out_ref.at[place], sems.at[1 + part])
        copy.start()
        copies.append(copy)
    for copy in copies:
        copy.wait()


def embed_kernel(slots_ref, fetched_ref, out_ref):
    events = out_ref.shape[0]
    slots = fetched_ref.shape[0]
    column = jnp.transpose(slots_ref[...])
    lane = iota((events, slots), 1)
    hit = lane == column[:, 0:1]
    for k in range(1, NIDS):
        hit = hit | (lane == column[:, k : k + 1])
    picked = jnp.where(hit, 1.0, 0.0).astype(BF16)
    out_ref[...] = dot(picked, fetched_ref[...]).astype(BF16)


def collect_kernel(asked_ref, returned_ref, out_ref):
    owners, capacity = asked_ref.shape
    rows = out_ref.shape[0]
    slots = owners * capacity
    high, low = split_exact(asked_ref[...])
    place = jnp.where(
        iota((capacity, slots), 1) % capacity == iota((capacity, slots), 0), 1.0, 0.0
    ).astype(BF16)
    spread = 16.0 * dot(high, place) + dot(low, place)
    mine = iota((owners, slots), 1) // capacity == iota((owners, slots), 0)
    asked = jnp.sum(jnp.where(mine, spread, 0.0), 0, keepdims=True).astype(jnp.int32)
    chosen = jnp.where(iota((rows, slots), 0) == asked, 1.0, 0.0).astype(BF16)
    out_ref[...] = dot(chosen, returned_ref[...])


SCALE = HEAD_DIM ** (-0.5)


def head(part, h, width):
    return slice(part * width + h * HEAD_DIM, part * width + (h + 1) * HEAD_DIM)


def visible(query_chunk, key_chunk, segc_ref, segr_ref, flip):
    events = segr_ref.shape[2]
    first, second = iota((events, events), 0), iota((events, events), 1)
    if flip:
        same = segc_ref[key_chunk][:, 0:1] == segr_ref[query_chunk][0:1, :]
        return same & (first <= second + (query_chunk - key_chunk) * events)
    same = segc_ref[query_chunk][:, 0:1] == segr_ref[key_chunk][0:1, :]
    return same & (first + (query_chunk - key_chunk) * events >= second)


def project(emb, w_in_ref, write, slope_ref, copies=()):
    width = emb.shape[1]
    normed = normalize(emb.astype(F32))[0].astype(BF16)
    for block in range(4):
        columns = slice(block * width, (block + 1) * width)
        if copies:
            copies[block].wait()
        half = 0.5 * dot(normed, w_in_ref[:, columns])
        bend = jnp.tanh(half)
        value = half + half * bend
        write(columns, value.astype(BF16))
        if slope_ref is not None:
            sigma = 0.5 + 0.5 * bend
            slope_ref[:, columns] = sigma + value - value * sigma


def hold_side(side_ref, place, cots_ref, segc_ref, segr_ref):
    events = cots_ref.shape[1]
    cots_ref[place] = side_ref[0:events, :]
    seg = side_ref[events : events + EXTRA, 0:events].astype(F32)[0:8]
    segr_ref[place] = seg
    segc_ref[place] = jnp.broadcast_to(jnp.transpose(seg)[:, 0:1], segc_ref.shape[1:])


HIDDEN = -1e4


def bent(raw, mask):
    half = jnp.where(mask, raw * (0.5 * SCALE), HIDDEN)
    bend = jnp.tanh(half)
    product = half * bend
    return half + product, (1.0 + bend) * (1.0 + (half - product))


class Chunks:
    def __init__(self, first, proj_ref, gatt_ref, segc_ref, segr_ref, join_ref):
        self.first, self.proj, self.gatt = first, proj_ref, gatt_ref
        self.segc, self.segr, self.join = segc_ref, segr_ref, join_ref
        self.width = gatt_ref.shape[2]

    def attend(self, i, start, stop, att_ref):
        def pair(j, _):
            mask = visible(i, j, self.segc, self.segr, False)
            qi, kj = i - self.first, j - self.first

            def scores(h):
                queries = self.proj[qi, :, head(2, h, self.width)]
                return dot_nt(queries, self.proj[kj, :, head(3, h, self.width)])

            raw = scores(0)
            for h in range(HEADS):
                later = scores(h + 1) if h + 1 < HEADS else None
                half = jnp.where(mask, raw * (0.5 * SCALE), HIDDEN)
                weights = (half + half * jnp.tanh(half)).astype(BF16)
                added = dot(weights, self.proj[kj, :, head(1, h, self.width)])
                att_ref[:, head(0, h, self.width)] += added
                raw = later
            return 0

        lax.fori_loop(start, stop, pair, 0)

    def finish(self, i, own, att, cot, emb_ref, w_out_ref, out_ref):
        att_norm, att_inverse = normalize(att)
        gate = self.proj[i - self.first, :, 0 : self.width].astype(F32)
        grad_mixed = dot_nt(cot, w_out_ref[...])
        grad_att = norm_back(grad_mixed * gate, att_norm, att_inverse)
        self.gatt[i - self.first] = grad_att.astype(BF16)

        @pl.when(i == own)
        def _():
            mixed = (att_norm * gate).astype(BF16)
            out = emb_ref[...].astype(F32) + dot(mixed, w_out_ref[...])
            out_ref[...] = out.astype(BF16)
            self.join[:, 0 : self.width] = grad_mixed * att_norm

    def query_side(self, own, start, stop):
        def pair(j, _):
            mask = visible(own, j, self.segc, self.segr, False)
            me, kj = own - self.first, j - self.first

            def scores(h):
                raw = dot_nt(
                    self.proj[me, :, head(2, h, self.width)],
                    self.proj[kj, :, head(3, h, self.width)],
                )
                grad_weights = dot_nt(
                    self.gatt[me, :, head(0, h, self.width)],
                    self.proj[kj, :, head(1, h, self.width)],
                )
                return raw, grad_weights

            raw, grad_weights = scores(0)
            for h in range(HEADS):
                later = scores(h + 1) if h + 1 < HEADS else (None, None)
                _, slope = bent(raw, mask)
                grad_raw = (grad_weights * slope).astype(BF16)
                added = dot(grad_raw, self.proj[kj, :, head(3, h, self.width)])
                self.join[:, head(2, h, self.width)] += added
                raw, grad_weights = later
            return 0

        lax.fori_loop(start, stop, pair, 0)

    def key_side(self, own, start, stop):
        def pair(i, _):
            mask = visible(i, own, self.segc, self.segr, True)
            me, qi = own - self.first, i - self.first

            def scores(h):
                raw = dot_nt(
                    self.proj[me, :, head(3, h, self.width)],
                    self.proj[qi, :, head(2, h, self.width)],
                )
                grad_weights = dot_nt(
                    self.proj[me, :, head(1, h, self.width)],
                    self.gatt[qi, :, head(0, h, self.width)],
                )
                return raw, grad_weights

            raw, grad_weights = scores(0)
            for h in range(HEADS):
                later = scores(h + 1) if h + 1 < HEADS else (None, None)
                value, slope = bent(raw, mask)
                grad_raw = (grad_weights * slope).astype(BF16)
                queries = self.proj[qi, :, head(2, h, self.width)]
                grad_att = self.gatt[qi, :, head(0, h, self.width)]
                self.join[:, head(3, h, self.width)] += dot(grad_raw, queries)
                self.join[:, head(1, h, self.width)] += dot(value.astype(BF16), grad_att)
                raw, grad_weights = later
            return 0

        lax.fori_loop(start, stop, pair, 0)


def early_kernel(count, index_ref, emb_ref, mate_ref, slots_in, w_in_in, w_out_in, *refs):
    (
        proj_ref,
        att_ref,
        gatt_ref,
        join_ref,
        slope_ref,
        out_ref,
        slots_ref,
        w_in_ref,
        w_out_ref,
        sides_ref,
        segc_ref,
        segr_ref,
        cots_ref,
        sems,
    ) = refs[count:]
    width = emb_ref.shape[1]
    blocks = [pl.ds(block * width, width) for block in range(4)]
    pairs = [(w_in_in.at[:, block], w_in_ref.at[:, block]) for block in blocks]
    pairs += [(w_out_in, w_out_ref), (slots_in, slots_ref)]
    pairs += [(refs[t], sides_ref.at[t]) for t in range(count)]
    copies = start_copies(pairs, sems)
    own = index_ref[0]
    mate = index_ref[1]
    base = jnp.minimum(own, mate)
    last = jnp.maximum(own, mate)

    def write_to(place):
        def write(columns, value):
            proj_ref[place - base, :, columns] = value

        return write

    project(emb_ref[...], w_in_ref, write_to(own), slope_ref, copies[:4])
    project(mate_ref[...], w_in_ref, write_to(mate), None)
    for copy in copies[4:]:
        copy.wait()
    hold_side(sides_ref.at[0], own - base, cots_ref, segc_ref, segr_ref)
    hold_side(sides_ref.at[1], mate - base, cots_ref, segc_ref, segr_ref)
    att_ref[...] = jnp.zeros_like(att_ref)
    join_ref[...] = jnp.zeros_like(join_ref)
    chunks = Chunks(0, proj_ref, gatt_ref, segc_ref, segr_ref, join_ref)

    def forward(i, _):
        chunks.attend(i, 0, i + 1, att_ref.at[i])
        return 0

    lax.fori_loop(own - base, last - base + 1, forward, 0)

    @pl.when(base == 0)
    def _():
        def finish(i, _):
            chunks.finish(i, own, att_ref[i], cots_ref[i], emb_ref, w_out_ref, out_ref)
            return 0

        lax.fori_loop(own, last + 1, finish, 0)
        chunks.query_side(own, 0, own + 1)
        chunks.key_side(own, own, last + 1)


def late_kernel(count, *refs):
    index_ref = refs[0]
    emb_refs = refs[1 : 1 + count]
    (
        proj_pair_ref,
        att_pair_ref,
        gatt_pair_ref,
        join_early_ref,
        slope_ref,
        out_early_ref,
        slots_ref,
        w_in_ref,
        w_out_ref,
        sides_ref,
        out_ref,
        grad_ref,
        proj_ref,
        cot_ref,
        segc_ref,
        segr_ref,
        att_ref,
        gatt_ref,
        join_ref,
    ) = refs[1 + count :]
    own = index_ref[0]
    base = jnp.minimum(own, index_ref[1])
    last = jnp.maximum(own, index_ref[1])
    closed = base == 0

    for t in range(count):
        place = index_ref[t]
        hold_side(sides_ref.at[t], place, cot_ref, segc_ref, segr_ref)
    for t in range(2):
        proj_ref[base + t] = proj_pair_ref[t]
        gatt_ref[base + t] = gatt_pair_ref[t]

    def write_to(place):
        def write(columns, value):
            proj_ref[place, :, columns] = value

        return write

    for t in range(2, count):
        project(emb_refs[t][...], w_in_ref, write_to(index_ref[t]), None)
    join_ref[...] = jnp.zeros_like(join_ref)
    chunks = Chunks(0, proj_ref, gatt_ref, segc_ref, segr_ref, join_ref)

    @pl.when(closed)
    def _():
        out_ref[...] = out_early_ref[...]

    def forward(i, _):
        begun = i <= last

        @pl.when(begun)
        def _():
            att_ref[...] = att_pair_ref[jnp.minimum(i - base, 1)]

        @pl.when(jnp.logical_not(begun))
        def _():
            att_ref[...] = jnp.zeros_like(att_ref)

        chunks.attend(i, 0, jnp.where(begun, base, i + 1), att_ref)
        chunks.finish(i, own, att_ref[...], cot_ref[i], emb_refs[0], w_out_ref, out_ref)
        return 0

    lax.fori_loop(jnp.where(closed, last + 1, own), count, forward, 0)
    chunks.query_side(own, jnp.where(closed, own + 1, 0), own + 1)
    chunks.key_side(own, jnp.where(closed, last + 1, own), count)

    width = gatt_ref.shape[2]
    scaled = jnp.where(iota((1, 4 * width), 1) < 2 * width, 1.0, 0.5 * SCALE)
    joined = (join_ref[...] + join_early_ref[...]) * scaled
    grad_proj = (joined * slope_ref[...]).astype(BF16)
    grad_normed = dot_nt(grad_proj, w_in_ref[...])
    normed, inverse = normalize(emb_refs[0][...].astype(F32))
    grad = norm_back(grad_normed, normed, inverse) + cot_ref[own].astype(F32)
    slot = iota((grad_ref.shape[0], grad.shape[0]), 0)
    hit = slot == slots_ref[0:1, :]
    for k in range(1, NIDS):
        hit = hit | (slot == slots_ref[k : k + 1, :])
    spread = jnp.where(hit, 1.0, 0.0).astype(BF16)
    grad_ref[...] = dot(spread, grad.astype(BF16)).astype(BF16)


def in_hbm(*arrays):
    return [pltpu.with_memory_space_constraint(a, pltpu.HBM) for a in arrays]


def params(mebibytes=12):
    return pltpu.CompilerParams(vmem_limit_bytes=mebibytes * 1024 * 1024)


def flip(value, axis, offset):
    count = lax.axis_size(axis)
    return lax.ppermute(value, axis, [(i, i ^ offset) for i in range(count)])


def gather_blocks(value, axis, known):
    bit = lax.axis_size(axis)
    blocks = {0: value}
    while bit > 1:
        bit //= 2
        for t in list(blocks):
            blocks[t | bit] = known.get(t | bit)
            if blocks[t | bit] is None:
                blocks[t | bit] = flip(blocks[t], axis, bit)
    return [blocks[t] for t in range(lax.axis_size(axis))]


def after(value, earlier):
    return lax.optimization_barrier((value, earlier))[0]


def local(table, item_owner, item_row, segment_ids, w_in, w_out, cotangent):
    owners = lax.axis_size("table") * lax.axis_size("ctx")
    count = lax.axis_size("ctx")
    events, width = cotangent.shape
    id_count = events * NIDS
    capacity = 2 * ((id_count + owners - 1) // owners)
    slot_count = owners * capacity
    axes = ("table", "ctx")
    vmem = pl.BlockSpec(memory_space=pltpu.VMEM)
    smem = pl.BlockSpec(memory_space=pltpu.SMEM)

    def exchange(value):
        return lax.all_to_all(value, axes, split_axis=0, concat_axis=0, tiled=True)

    hbm = pl.BlockSpec(memory_space=pltpu.HBM)
    slots, wanted, side = pl.pallas_call(
        functools.partial(slots_kernel, capacity),
        out_shape=(
            jax.ShapeDtypeStruct((8, events), jnp.int32),
            jax.ShapeDtypeStruct((owners, capacity), jnp.int32),
            jax.ShapeDtypeStruct((events + EXTRA, width), BF16),
        ),
        in_specs=[hbm] * 4,
        out_specs=(vmem, vmem, vmem),
        scratch_shapes=[
            pltpu.VMEM((NIDS, events), jnp.int32),
            pltpu.VMEM((NIDS, events), jnp.int32),
            pltpu.VMEM((1, events), jnp.int32),
            pltpu.SemaphoreType.DMA((4,)),
        ],
        compiler_params=params(),
        name="slots",
    )(*in_hbm(item_owner.T, item_row.T, segment_ids.reshape(1, events), cotangent))
    asked = exchange(wanted)
    rows = pl.pallas_call(
        select_kernel,
        out_shape=pltpu.HBM((slot_count, width), BF16),
        in_specs=[vmem, hbm],
        out_specs=hbm,
        scratch_shapes=[
            pltpu.VMEM(table.shape, BF16),
            pltpu.VMEM((slot_count, width), BF16),
            pltpu.SemaphoreType.DMA((5,)),
        ],
        compiler_params=params(),
        name="select",
    )(asked, *in_hbm(table))
    fetched = exchange(rows.reshape(owners, capacity, width)).reshape(slot_count, width)
    side_far = flip(side, "ctx", count // 2)
    side_mate = flip(side, "ctx", 1)
    side_blocks = gather_blocks(side, "ctx", {1: side_mate, count // 2: after(side_far, rows)})
    held_shapes = (
        jax.ShapeDtypeStruct(slots.shape, jnp.int32),
        jax.ShapeDtypeStruct(w_in.shape, BF16),
        jax.ShapeDtypeStruct(w_out.shape, BF16),
        jax.ShapeDtypeStruct((count, events + EXTRA, width), BF16),
    )
    side_blocks = in_hbm(*side_blocks)
    fetched, side_blocks = lax.optimization_barrier((fetched, side_blocks))
    embedded = pl.pallas_call(
        embed_kernel,
        out_shape=jax.ShapeDtypeStruct((events, width), BF16),
        compiler_params=params(),
        name="embed",
    )(slots, fetched)
    emb_far = flip(embedded, "ctx", count // 2)
    emb_mate = flip(embedded, "ctx", 1)
    index = lax.axis_index("ctx").astype(jnp.int32) ^ jnp.arange(count, dtype=jnp.int32)
    event_shape = jax.ShapeDtypeStruct((events, width), BF16)
    early = pl.pallas_call(
        functools.partial(early_kernel, count),
        out_shape=(
            jax.ShapeDtypeStruct((2, events, 4 * width), BF16),
            jax.ShapeDtypeStruct((2, events, width), F32),
            jax.ShapeDtypeStruct((2, events, width), BF16),
            jax.ShapeDtypeStruct((events, 4 * width), F32),
            jax.ShapeDtypeStruct((events, 4 * width), F32),
            event_shape,
        )
        + held_shapes,
        in_specs=[smem, vmem, vmem] + [hbm] * (3 + count),
        out_specs=(vmem,) * 10,
        scratch_shapes=[
            pltpu.VMEM((2, events, 128), F32),
            pltpu.VMEM((2, 8, events), F32),
            pltpu.VMEM((2, events, width), BF16),
            pltpu.SemaphoreType.DMA((6 + count,)),
        ],
        compiler_params=params(20),
        name="early",
    )(index, embedded, emb_mate, *in_hbm(slots, w_in, w_out), *side_blocks)
    emb_blocks = gather_blocks(embedded, "ctx", {1: emb_mate, count // 2: after(emb_far, early)})
    layer_out, slot_grad = pl.pallas_call(
        functools.partial(late_kernel, count),
        out_shape=(event_shape, jax.ShapeDtypeStruct((slot_count, width), BF16)),
        in_specs=[smem] + [vmem] * (10 + count),
        out_specs=(vmem, vmem),
        scratch_shapes=[
            pltpu.VMEM((count, events, 4 * width), BF16),
            pltpu.VMEM((count, events, width), BF16),
            pltpu.VMEM((count, events, 128), F32),
            pltpu.VMEM((count, 8, events), F32),
            pltpu.VMEM((events, width), F32),
            pltpu.VMEM((count, events, width), BF16),
            pltpu.VMEM((events, 4 * width), F32),
        ],
        compiler_params=params(28),
        name="late",
    )(index, *emb_blocks, *early)
    returned = exchange(slot_grad.reshape(owners, capacity, width)).reshape(slot_count, width)
    row_grad = pl.pallas_call(
        collect_kernel,
        out_shape=jax.ShapeDtypeStruct(table.shape, F32),
        compiler_params=params(),
        name="collect",
    )(asked, returned)
    return layer_out, row_grad


def solution(mesh):
    rows = P(("table", "ctx"), None)
    return jax.shard_map(
        local,
        mesh=mesh,
        in_specs=(rows, rows, rows, P("table", "ctx"), P(), P(), rows),
        out_specs=(rows, rows),
        check_vma=False,
    )
```

```python
import functools

import jax
import jax.numpy as jnp
from jax import lax
from jax.experimental import pallas as pl
from jax.experimental.pallas import tpu as pltpu
from jax.sharding import PartitionSpec as P

HEADS = 4
HEAD_DIM = 128
NIDS = 2
EPS = 1e-06

F32 = jnp.float32
BF16 = jnp.bfloat16


def dot(a, b):
    return jnp.dot(a, b, preferred_element_type=F32)


def dot_nt(a, b):
    return lax.dot_general(a, b, (((1,), (1,)), ((), ())), preferred_element_type=F32)


def iota(shape, dim):
    return lax.broadcasted_iota(jnp.int32, shape, dim)


def normalize(values):
    centred = values - jnp.mean(values, -1, keepdims=True)
    inverse = lax.rsqrt(jnp.mean(centred * centred, -1, keepdims=True) + EPS)
    return centred * inverse, inverse


def norm_back(grad_norm, normed, inverse):
    mean_grad = jnp.mean(grad_norm, -1, keepdims=True)
    mean_cross = jnp.mean(grad_norm * normed, -1, keepdims=True)
    return (grad_norm - mean_grad - normed * mean_cross) * inverse


def split_exact(values):
    return (values >> 4).astype(F32).astype(BF16), (values & 15).astype(F32).astype(BF16)


def start_copies(pairs, sems):
    copies = [pltpu.make_async_copy(a, b, sems.at[i]) for i, (a, b) in enumerate(pairs)]
    for copy in copies:
        copy.start()
    return copies


EXTRA = 16


def slots_kernel(
    capacity,
    owner_in,
    row_in,
    seg_in,
    cot_in,
    slots_ref,
    wanted_ref,
    side_ref,
    owner_ref,
    row_ref,
    seg_ref,
    sems,
):
    events, width = cot_in.shape
    pairs = (
        (owner_in, owner_ref),
        (row_in, row_ref),
        (seg_in, seg_ref),
        (cot_in, side_ref.at[0:events]),
    )
    copies = start_copies(pairs, sems)
    for copy in copies[:3]:
        copy.wait()
    side_ref[events:, :] = jnp.zeros((EXTRA, width), BF16)
    segments = jnp.broadcast_to(seg_ref[...].astype(F32), (EXTRA, events))
    side_ref[events:, 0:events] = segments.astype(BF16)
    owners = wanted_ref.shape[0]
    owner = jnp.concatenate([owner_ref[k : k + 1, :] for k in range(NIDS)], 1)
    row = jnp.concatenate([row_ref[k : k + 1, :] for k in range(NIDS)], 1)
    ids = owner.shape[1]
    named = iota((owners, ids), 0) == owner
    named_f = jnp.where(named, 1.0, 0.0)
    before = jnp.where(iota((ids, ids), 0) < iota((ids, ids), 1), 1.0, 0.0).astype(BF16)
    earlier = dot(named_f.astype(BF16), before)
    rank = jnp.sum(earlier * named_f, 0, keepdims=True).astype(jnp.int32)
    slot = owner * capacity + rank
    slots_ref[...] = jnp.full(slots_ref.shape, -1, jnp.int32)
    for k in range(NIDS):
        slots_ref[k : k + 1, :] = slot[:, k * events : (k + 1) * events]
    ranked = jnp.where(iota((capacity, ids), 0) == rank, 1.0, 0.0).astype(BF16)
    high, low = (row >> 4).astype(F32), (row & 15).astype(F32)
    wanted = 16.0 * dot_nt((named_f * high).astype(BF16), ranked) + dot_nt(
        (named_f * low).astype(BF16), ranked
    )
    wanted_ref[...] = wanted.astype(jnp.int32)
    for copy in copies[3:]:
        copy.wait()


def select_kernel(asked_ref, table_in, out_ref, table_ref, rows_ref, sems):
    (table_copy,) = start_copies(((table_in, table_ref),), sems)
    owners, capacity = asked_ref.shape
    rows = table_ref.shape[0]
    parts = sems.shape[0] - 1
    step = owners // parts
    columns = jnp.transpose(asked_ref[...])
    lane = iota((capacity, rows), 1)
    copies = []
    for part in range(parts):
        sources = range(part * step, (part + 1) * step)
        chosen = [jnp.where(lane == columns[:, s : s + 1], 1.0, 0.0) for s in sources]
        chosen = jnp.concatenate(chosen, 0).astype(BF16)
        if part == 0:
            table_copy.wait()
        place = pl.ds(part * step * capacity, step * capacity)
        rows_ref[place, :] = dot(chosen, table_ref[...]).astype(BF16)
        copy = pltpu.make_async_copy(rows_ref.at[place], out_ref.at[place], sems.at[1 + part])
        copy.start()
        copies.append(copy)
    for copy in copies:
        copy.wait()


def embed_kernel(slots_ref, fetched_ref, out_ref):
    events = out_ref.shape[0]
    slots = fetched_ref.shape[0]
    column = jnp.transpose(slots_ref[...])
    lane = iota((events, slots), 1)
    hit = lane == column[:, 0:1]
    for k in range(1, NIDS):
        hit = hit | (lane == column[:, k : k + 1])
    picked = jnp.where(hit, 1.0, 0.0).astype(BF16)
    out_ref[...] = dot(picked, fetched_ref[...]).astype(BF16)


def collect_kernel(chosen_ref, returned_ref, out_ref, rows_ref, sems):
    parts = sems.shape[0]
    step = rows_ref.shape[0] // parts
    copies = []
    for part in range(parts):
        place = pl.ds(part * step, step)
        rows_ref[place, :] = dot(chosen_ref[place, :], returned_ref[...])
        copy = pltpu.make_async_copy(rows_ref.at[place], out_ref.at[place], sems.at[part])
        copy.start()
        copies.append(copy)
    for copy in copies:
        copy.wait()


SCALE = HEAD_DIM ** (-0.5)


def head(part, h, width):
    return slice(part * width + h * HEAD_DIM, part * width + (h + 1) * HEAD_DIM)


def visible(query_chunk, key_chunk, segc_ref, segr_ref, flip):
    events = segr_ref.shape[2]
    first, second = iota((events, events), 0), iota((events, events), 1)
    if flip:
        same = segc_ref[key_chunk][:, 0:1] == segr_ref[query_chunk][0:1, :]
        return same & (first <= second + (query_chunk - key_chunk) * events)
    same = segc_ref[query_chunk][:, 0:1] == segr_ref[key_chunk][0:1, :]
    return same & (first + (query_chunk - key_chunk) * events >= second)


def project(emb, w_in_ref, write, slope_ref, copies=()):
    width = emb.shape[1]
    normed = (0.5 * normalize(emb.astype(F32))[0]).astype(BF16)
    for block in range(4):
        columns = slice(block * width, (block + 1) * width)
        if copies:
            copies[block].wait()
        half = dot(normed, w_in_ref[:, columns])
        bend = jnp.tanh(half)
        value = half + half * bend
        write(columns, value.astype(BF16))
        if slope_ref is not None:
            sigma = 0.5 + 0.5 * bend
            slope_ref[:, columns] = sigma + value - value * sigma


def prep_kernel(count, index_ref, slots_ref, asked_ref, w_out_ref, *refs):
    mixed_ref, segc_ref, segr_ref, spread_ref, chosen_ref = refs[count:]
    events = spread_ref.shape[1]
    for t in range(count):
        place = index_ref[t]
        mixed_ref[place] = dot_nt(refs[t][0:events, :], w_out_ref[...])
        seg = refs[t][events : events + EXTRA, 0:events].astype(F32)[0:8]
        segr_ref[place] = seg
        segc_ref[place] = jnp.broadcast_to(jnp.transpose(seg)[:, 0:1], segc_ref.shape[1:])
    slot = iota(spread_ref.shape, 0)
    hit = slot == slots_ref[0:1, :]
    for k in range(1, NIDS):
        hit = hit | (slot == slots_ref[k : k + 1, :])
    spread_ref[...] = jnp.where(hit, 1.0, 0.0).astype(BF16)
    owners, capacity = asked_ref.shape
    slots = owners * capacity
    high, low = split_exact(asked_ref[...])
    place = jnp.where(
        iota((capacity, slots), 1) % capacity == iota((capacity, slots), 0), 1.0, 0.0
    ).astype(BF16)
    values = 16.0 * dot(high, place) + dot(low, place)
    mine = iota((owners, slots), 1) // capacity == iota((owners, slots), 0)
    asked = jnp.sum(jnp.where(mine, values, 0.0), 0, keepdims=True).astype(jnp.int32)
    chosen_ref[...] = jnp.where(iota(chosen_ref.shape, 0) == asked, 1.0, 0.0).astype(BF16)


HIDDEN = -1e4


def bent(raw, mask):
    half = jnp.where(mask, raw * (0.5 * SCALE), HIDDEN)
    raised = (1.0 + jnp.tanh(half)).astype(BF16)
    half = half.astype(BF16)
    one, two = BF16(1.0), BF16(2.0)
    return half * raised, raised * (one + half * (two - raised))


class Chunks:
    def __init__(self, first, proj_ref, gatt_ref, segc_ref, segr_ref, join_ref):
        self.first, self.proj, self.gatt = first, proj_ref, gatt_ref
        self.segc, self.segr, self.join = segc_ref, segr_ref, join_ref
        self.width = gatt_ref.shape[2]

    def attend(self, i, start, stop, att_ref):
        def pair(j, _):
            mask = visible(i, j, self.segc, self.segr, False)
            qi, kj = i - self.first, j - self.first

            def scores(h):
                queries = self.proj[qi, :, head(2, h, self.width)]
                return dot_nt(queries, self.proj[kj, :, head(3, h, self.width)])

            raw = scores(0)
            for h in range(HEADS):
                later = scores(h + 1) if h + 1 < HEADS else None
                half = jnp.where(mask, raw * (0.5 * SCALE), HIDDEN)
                weights = (half + half * jnp.tanh(half)).astype(BF16)
                added = dot(weights, self.proj[kj, :, head(1, h, self.width)])
                att_ref[:, head(0, h, self.width)] += added
                raw = later
            return 0

        lax.fori_loop(start, stop, pair, 0)

    def finish(self, i, own, att, grad_mixed, emb_ref, w_out_ref, out_ref):
        att_norm, att_inverse = normalize(att)
        gate = self.proj[i - self.first, :, 0 : self.width].astype(F32)
        grad_att = norm_back(grad_mixed * gate, att_norm, att_inverse)
        self.gatt[i - self.first] = grad_att.astype(BF16)

        @pl.when(i == own)
        def _():
            mixed = (att_norm * gate).astype(BF16)
            out = emb_ref[...].astype(F32) + dot(mixed, w_out_ref[...])
            out_ref[...] = out.astype(BF16)
            self.join[:, 0 : self.width] = grad_mixed * att_norm

    def query_side(self, own, start, stop):
        def pair(j, _):
            mask = visible(own, j, self.segc, self.segr, False)
            me, kj = own - self.first, j - self.first

            def scores(h):
                raw = dot_nt(
                    self.proj[me, :, head(2, h, self.width)],
                    self.proj[kj, :, head(3, h, self.width)],
                )
                grad_weights = dot_nt(
                    self.gatt[me, :, head(0, h, self.width)],
                    self.proj[kj, :, head(1, h, self.width)],
                )
                return raw, grad_weights

            raw, grad_weights = scores(0)
            for h in range(HEADS):
                later = scores(h + 1) if h + 1 < HEADS else (None, None)
                _, slope = bent(raw, mask)
                grad_raw = grad_weights.astype(BF16) * slope
                added = dot(grad_raw, self.proj[kj, :, head(3, h, self.width)])
                self.join[:, head(2, h, self.width)] += added
                raw, grad_weights = later
            return 0

        lax.fori_loop(start, stop, pair, 0)

    def key_side(self, own, start, stop):
        def pair(i, _):
            mask = visible(i, own, self.segc, self.segr, True)
            me, qi = own - self.first, i - self.first

            def scores(h):
                raw = dot_nt(
                    self.proj[me, :, head(3, h, self.width)],
                    self.proj[qi, :, head(2, h, self.width)],
                )
                grad_weights = dot_nt(
                    self.proj[me, :, head(1, h, self.width)],
                    self.gatt[qi, :, head(0, h, self.width)],
                )
                return raw, grad_weights

            raw, grad_weights = scores(0)
            for h in range(HEADS):
                later = scores(h + 1) if h + 1 < HEADS else (None, None)
                value, slope = bent(raw, mask)
                grad_raw = grad_weights.astype(BF16) * slope
                queries = self.proj[qi, :, head(2, h, self.width)]
                grad_att = self.gatt[qi, :, head(0, h, self.width)]
                self.join[:, head(3, h, self.width)] += dot(grad_raw, queries)
                self.join[:, head(1, h, self.width)] += dot(value, grad_att)
                raw, grad_weights = later
            return 0

        lax.fori_loop(start, stop, pair, 0)


def early_kernel(index_ref, emb_ref, mate_ref, *refs):
    w_in_in, w_out_in, mixed_in, segc_in, segr_in, spread_in, side_in = refs[:7]
    proj_ref, att_ref, gatt_ref, join_ref, slope_ref, out_ref = refs[7:13]
    w_in_ref, w_out_ref, mixed_ref, segc_ref, segr_ref, spread_ref, side_ref, sems = refs[13:]
    width = emb_ref.shape[1]
    blocks = [pl.ds(block * width, width) for block in range(4)]
    pairs = [(w_in_in.at[:, block], w_in_ref.at[:, block]) for block in blocks]
    pairs += [(segc_in, segc_ref), (segr_in, segr_ref), (mixed_in, mixed_ref)]
    pairs += [(w_out_in, w_out_ref), (spread_in, spread_ref), (side_in, side_ref)]
    copies = start_copies(pairs, sems)
    own = index_ref[0]
    mate = index_ref[1]
    base = jnp.minimum(own, mate)
    last = jnp.maximum(own, mate)

    def write_to(place):
        def write(columns, value):
            proj_ref[place - base, :, columns] = value

        return write

    project(emb_ref[...], w_in_ref, write_to(own), slope_ref, copies[:4])
    project(mate_ref[...], w_in_ref, write_to(mate), None)
    for copy in copies[4:]:
        copy.wait()
    att_ref[...] = jnp.zeros_like(att_ref)
    join_ref[...] = jnp.zeros_like(join_ref)
    pair_rows = pl.ds(base, 2)
    chunks = Chunks(
        0, proj_ref, gatt_ref, segc_ref.at[pair_rows], segr_ref.at[pair_rows], join_ref
    )

    def forward(i, _):
        chunks.attend(i, 0, i + 1, att_ref.at[i])
        return 0

    lax.fori_loop(own - base, last - base + 1, forward, 0)

    @pl.when(base == 0)
    def _():
        def finish(i, _):
            chunks.finish(i, own, att_ref[i], mixed_ref[i], emb_ref, w_out_ref, out_ref)
            return 0

        lax.fori_loop(own, last + 1, finish, 0)
        chunks.query_side(own, 0, own + 1)
        chunks.key_side(own, own, last + 1)


def late_kernel(count, *refs):
    index_ref = refs[0]
    emb_refs = refs[1 : 1 + count]
    (
        proj_pair_ref,
        att_pair_ref,
        gatt_pair_ref,
        join_early_ref,
        slope_ref,
        out_early_ref,
        w_in_ref,
        w_out_ref,
        mixed_ref,
        segc_ref,
        segr_ref,
        spread_ref,
        side_ref,
        out_ref,
        grad_ref,
        proj_ref,
        att_ref,
        gatt_ref,
        join_ref,
    ) = refs[1 + count :]
    own = index_ref[0]
    base = jnp.minimum(own, index_ref[1])
    last = jnp.maximum(own, index_ref[1])
    closed = base == 0

    for t in range(2):
        proj_ref[base + t] = proj_pair_ref[t]
        gatt_ref[base + t] = gatt_pair_ref[t]

    def write_to(place):
        def write(columns, value):
            proj_ref[place, :, columns] = value

        return write

    for t in range(2, count):
        project(emb_refs[t][...], w_in_ref, write_to(index_ref[t]), None)
    join_ref[...] = jnp.zeros_like(join_ref)
    chunks = Chunks(0, proj_ref, gatt_ref, segc_ref, segr_ref, join_ref)

    @pl.when(closed)
    def _():
        out_ref[...] = out_early_ref[...]

    def forward(i, _):
        begun = i <= last

        @pl.when(begun)
        def _():
            att_ref[...] = att_pair_ref[jnp.minimum(i - base, 1)]

        @pl.when(jnp.logical_not(begun))
        def _():
            att_ref[...] = jnp.zeros_like(att_ref)

        chunks.attend(i, 0, jnp.where(begun, base, i + 1), att_ref)
        chunks.finish(i, own, att_ref[...], mixed_ref[i], emb_refs[0], w_out_ref, out_ref)
        return 0

    lax.fori_loop(jnp.where(closed, last + 1, own), count, forward, 0)
    chunks.query_side(own, jnp.where(closed, own + 1, 0), own + 1)
    chunks.key_side(own, jnp.where(closed, last + 1, own), count)

    width = gatt_ref.shape[2]
    scaled = jnp.where(iota((1, 4 * width), 1) < 2 * width, 1.0, 0.5 * SCALE)
    joined = (join_ref[...] + join_early_ref[...]) * scaled
    grad_proj = (joined * slope_ref[...]).astype(BF16)
    grad_normed = dot_nt(grad_proj, w_in_ref[...])
    normed, inverse = normalize(emb_refs[0][...].astype(F32))
    grad = norm_back(grad_normed, normed, inverse) + side_ref[0 : emb_refs[0].shape[0], :].astype(F32)
    grad_ref[...] = dot(spread_ref[...], grad.astype(BF16)).astype(BF16)


def in_hbm(*arrays):
    return [pltpu.with_memory_space_constraint(a, pltpu.HBM) for a in arrays]


def params(mebibytes=12):
    return pltpu.CompilerParams(vmem_limit_bytes=mebibytes * 1024 * 1024)


def flip(value, axis, offset):
    count = lax.axis_size(axis)
    return lax.ppermute(value, axis, [(i, i ^ offset) for i in range(count)])


def gather_blocks(value, axis, known):
    bit = lax.axis_size(axis)
    blocks = {0: value}
    while bit > 1:
        bit //= 2
        for t in list(blocks):
            blocks[t | bit] = known.get(t | bit)
            if blocks[t | bit] is None:
                blocks[t | bit] = flip(blocks[t], axis, bit)
    return [blocks[t] for t in range(lax.axis_size(axis))]


def after(value, earlier):
    return lax.optimization_barrier((value, earlier))[0]


def local(table, item_owner, item_row, segment_ids, w_in, w_out, cotangent):
    owners = lax.axis_size("table") * lax.axis_size("ctx")
    count = lax.axis_size("ctx")
    events, width = cotangent.shape
    id_count = events * NIDS
    capacity = 2 * ((id_count + owners - 1) // owners)
    slot_count = owners * capacity
    axes = ("table", "ctx")
    vmem = pl.BlockSpec(memory_space=pltpu.VMEM)
    smem = pl.BlockSpec(memory_space=pltpu.SMEM)

    def exchange(value):
        return lax.all_to_all(value, axes, split_axis=0, concat_axis=0, tiled=True)

    hbm = pl.BlockSpec(memory_space=pltpu.HBM)
    slots, wanted, side = pl.pallas_call(
        functools.partial(slots_kernel, capacity),
        out_shape=(
            jax.ShapeDtypeStruct((8, events), jnp.int32),
            jax.ShapeDtypeStruct((owners, capacity), jnp.int32),
            jax.ShapeDtypeStruct((events + EXTRA, width), BF16),
        ),
        in_specs=[hbm] * 4,
        out_specs=(vmem, vmem, vmem),
        scratch_shapes=[
            pltpu.VMEM((NIDS, events), jnp.int32),
            pltpu.VMEM((NIDS, events), jnp.int32),
            pltpu.VMEM((1, events), jnp.int32),
            pltpu.SemaphoreType.DMA((4,)),
        ],
        compiler_params=params(),
        name="slots",
    )(*in_hbm(item_owner.T, item_row.T, segment_ids.reshape(1, events), cotangent))
    asked = exchange(wanted)
    rows = pl.pallas_call(
        select_kernel,
        out_shape=pltpu.HBM((slot_count, width), BF16),
        in_specs=[vmem, hbm],
        out_specs=hbm,
        scratch_shapes=[
            pltpu.VMEM(table.shape, BF16),
            pltpu.VMEM((slot_count, width), BF16),
            pltpu.SemaphoreType.DMA((5,)),
        ],
        compiler_params=params(),
        name="select",
    )(asked, *in_hbm(table))
    fetched = exchange(rows.reshape(owners, capacity, width)).reshape(slot_count, width)
    side_far = flip(side, "ctx", count // 2)
    side_mate = flip(side, "ctx", 1)
    side_blocks = gather_blocks(side, "ctx", {1: side_mate, count // 2: after(side_far, rows)})
    index = lax.axis_index("ctx").astype(jnp.int32) ^ jnp.arange(count, dtype=jnp.int32)
    prep_shapes = (
        jax.ShapeDtypeStruct((count, events, width), F32),
        jax.ShapeDtypeStruct((count, events, 128), F32),
        jax.ShapeDtypeStruct((count, 8, events), F32),
        jax.ShapeDtypeStruct((slot_count, events), BF16),
    )
    *prepared, chosen = pl.pallas_call(
        functools.partial(prep_kernel, count),
        out_shape=tuple(pltpu.HBM(a.shape, a.dtype) for a in prep_shapes)
        + (jax.ShapeDtypeStruct((table.shape[0], slot_count), BF16),),
        in_specs=[smem] + [vmem] * (3 + count),
        out_specs=(vmem,) * 5,
        compiler_params=params(20),
        name="prep",
    )(index, slots, asked, w_out, *side_blocks)
    prepared = in_hbm(*prepared)
    fetched, prepared = lax.optimization_barrier((fetched, prepared))
    embedded = pl.pallas_call(
        embed_kernel,
        out_shape=jax.ShapeDtypeStruct((events, width), BF16),
        compiler_params=params(),
        name="embed",
    )(slots, fetched)
    emb_far = flip(embedded, "ctx", count // 2)
    emb_mate = flip(embedded, "ctx", 1)
    event_shape = jax.ShapeDtypeStruct((events, width), BF16)
    early = pl.pallas_call(
        early_kernel,
        out_shape=(
            jax.ShapeDtypeStruct((2, events, 4 * width), BF16),
            jax.ShapeDtypeStruct((2, events, width), F32),
            jax.ShapeDtypeStruct((2, events, width), BF16),
            jax.ShapeDtypeStruct((events, 4 * width), F32),
            jax.ShapeDtypeStruct((events, 4 * width), F32),
            event_shape,
        )
        + tuple(jax.ShapeDtypeStruct(a.shape, BF16) for a in (w_in, w_out))
        + prep_shapes
        + (jax.ShapeDtypeStruct(side.shape, BF16),),
        in_specs=[smem, vmem, vmem] + [hbm] * 7,
        out_specs=(vmem,) * 13,
        scratch_shapes=[pltpu.SemaphoreType.DMA((10,))],
        compiler_params=params(20),
        name="early",
    )(index, embedded, emb_mate, *in_hbm(w_in, w_out), *prepared, *in_hbm(side))
    emb_blocks = gather_blocks(embedded, "ctx", {1: emb_mate, count // 2: after(emb_far, early)})
    layer_out, slot_grad = pl.pallas_call(
        functools.partial(late_kernel, count),
        out_shape=(event_shape, jax.ShapeDtypeStruct((slot_count, width), BF16)),
        in_specs=[smem] + [vmem] * (13 + count),
        out_specs=(vmem, vmem),
        scratch_shapes=[
            pltpu.VMEM((count, events, 4 * width), BF16),
            pltpu.VMEM((events, width), F32),
            pltpu.VMEM((count, events, width), BF16),
            pltpu.VMEM((events, 4 * width), F32),
        ],
        compiler_params=params(28),
        name="late",
    )(index, *emb_blocks, *early)
    returned = exchange(slot_grad.reshape(owners, capacity, width)).reshape(slot_count, width)
    row_grad = pl.pallas_call(
        collect_kernel,
        out_shape=pltpu.HBM(table.shape, F32),
        in_specs=[vmem, vmem],
        out_specs=hbm,
        scratch_shapes=[pltpu.VMEM(table.shape, F32), pltpu.SemaphoreType.DMA((4,))],
        compiler_params=params(),
        name="collect",
    )(chosen, returned)
    return layer_out, row_grad


def solution(mesh):
    rows = P(("table", "ctx"), None)
    return jax.shard_map(
        local,
        mesh=mesh,
        in_specs=(rows, rows, rows, P("table", "ctx"), P(), P(), rows),
        out_specs=(rows, rows),
        check_vma=False,
    )
```

```python
import functools

import jax
import jax.numpy as jnp
from jax import lax
from jax.experimental import pallas as pl
from jax.experimental.pallas import tpu as pltpu
from jax.sharding import PartitionSpec as P

HEADS = 4
HEAD_DIM = 128
NIDS = 2
EPS = 1e-06

F32 = jnp.float32
BF16 = jnp.bfloat16


def dot(a, b):
    return jnp.dot(a, b, preferred_element_type=F32)


def dot_nt(a, b):
    return lax.dot_general(a, b, (((1,), (1,)), ((), ())), preferred_element_type=F32)


def iota(shape, dim):
    return lax.broadcasted_iota(jnp.int32, shape, dim)


def normalize(values):
    centred = values - jnp.mean(values, -1, keepdims=True)
    inverse = lax.rsqrt(jnp.mean(centred * centred, -1, keepdims=True) + EPS)
    return centred * inverse, inverse


def norm_back(grad_norm, normed, inverse):
    mean_grad = jnp.mean(grad_norm, -1, keepdims=True)
    mean_cross = jnp.mean(grad_norm * normed, -1, keepdims=True)
    return (grad_norm - mean_grad - normed * mean_cross) * inverse


def split_exact(values):
    return (values >> 4).astype(F32).astype(BF16), (values & 15).astype(F32).astype(BF16)


def start_copies(pairs, sems):
    copies = [pltpu.make_async_copy(a, b, sems.at[i]) for i, (a, b) in enumerate(pairs)]
    for copy in copies:
        copy.start()
    return copies


EXTRA = 16


def slots_kernel(
    capacity,
    owner_in,
    row_in,
    seg_in,
    cot_in,
    slots_ref,
    wanted_ref,
    side_ref,
    owner_ref,
    row_ref,
    seg_ref,
    sems,
):
    events, width = cot_in.shape
    pairs = (
        (owner_in, owner_ref),
        (row_in, row_ref),
        (seg_in, seg_ref),
        (cot_in, side_ref.at[0:events]),
    )
    copies = start_copies(pairs, sems)
    for copy in copies[:3]:
        copy.wait()
    side_ref[events:, :] = jnp.zeros((EXTRA, width), BF16)
    segments = jnp.broadcast_to(seg_ref[...].astype(F32), (EXTRA, events))
    side_ref[events:, 0:events] = segments.astype(BF16)
    owners = wanted_ref.shape[0]
    owner = jnp.concatenate([owner_ref[k : k + 1, :] for k in range(NIDS)], 1)
    row = jnp.concatenate([row_ref[k : k + 1, :] for k in range(NIDS)], 1)
    ids = owner.shape[1]
    named = iota((owners, ids), 0) == owner
    named_f = jnp.where(named, 1.0, 0.0)
    before = jnp.where(iota((ids, ids), 0) < iota((ids, ids), 1), 1.0, 0.0).astype(BF16)
    earlier = dot(named_f.astype(BF16), before)
    rank = jnp.sum(earlier * named_f, 0, keepdims=True).astype(jnp.int32)
    slot = owner * capacity + rank
    slots_ref[...] = jnp.full(slots_ref.shape, -1, jnp.int32)
    for k in range(NIDS):
        slots_ref[k : k + 1, :] = slot[:, k * events : (k + 1) * events]
    ranked = jnp.where(iota((capacity, ids), 0) == rank, 1.0, 0.0).astype(BF16)
    high, low = (row >> 4).astype(F32), (row & 15).astype(F32)
    wanted = 16.0 * dot_nt((named_f * high).astype(BF16), ranked) + dot_nt(
        (named_f * low).astype(BF16), ranked
    )
    wanted_ref[...] = wanted.astype(jnp.int32)
    for copy in copies[3:]:
        copy.wait()


def select_kernel(asked_ref, table_in, out_ref, table_ref, rows_ref, sems):
    (table_copy,) = start_copies(((table_in, table_ref),), sems)
    owners, capacity = asked_ref.shape
    rows = table_ref.shape[0]
    parts = sems.shape[0] - 1
    step = owners // parts
    columns = jnp.transpose(asked_ref[...])
    lane = iota((capacity, rows), 1)
    copies = []
    for part in range(parts):
        sources = range(part * step, (part + 1) * step)
        chosen = [jnp.where(lane == columns[:, s : s + 1], 1.0, 0.0) for s in sources]
        chosen = jnp.concatenate(chosen, 0).astype(BF16)
        if part == 0:
            table_copy.wait()
        place = pl.ds(part * step * capacity, step * capacity)
        rows_ref[place, :] = dot(chosen, table_ref[...]).astype(BF16)
        copy = pltpu.make_async_copy(rows_ref.at[place], out_ref.at[place], sems.at[1 + part])
        copy.start()
        copies.append(copy)
    for copy in copies:
        copy.wait()


def embed_kernel(slots_ref, fetched_ref, out_ref):
    events = out_ref.shape[0]
    slots = fetched_ref.shape[0]
    column = jnp.transpose(slots_ref[...])
    lane = iota((events, slots), 1)
    hit = lane == column[:, 0:1]
    for k in range(1, NIDS):
        hit = hit | (lane == column[:, k : k + 1])
    picked = jnp.where(hit, 1.0, 0.0).astype(BF16)
    out_ref[...] = dot(picked, fetched_ref[...]).astype(BF16)


def collect_kernel(chosen_ref, returned_ref, out_ref, rows_ref, sems):
    parts = sems.shape[0]
    step = rows_ref.shape[0] // parts
    copies = []
    for part in range(parts):
        place = pl.ds(part * step, step)
        rows_ref[place, :] = dot(chosen_ref[place, :], returned_ref[...])
        copy = pltpu.make_async_copy(rows_ref.at[place], out_ref.at[place], sems.at[part])
        copy.start()
        copies.append(copy)
    for copy in copies:
        copy.wait()


SCALE = HEAD_DIM ** (-0.5)


def head(part, h, width):
    return slice(part * width + h * HEAD_DIM, part * width + (h + 1) * HEAD_DIM)


def visible(query_chunk, key_chunk, segc_ref, segr_ref, flip):
    events = segr_ref.shape[2]
    first, second = iota((events, events), 0), iota((events, events), 1)
    if flip:
        same = segc_ref[key_chunk][:, 0:1] == segr_ref[query_chunk][0:1, :]
        return same & (first <= second + (query_chunk - key_chunk) * events)
    same = segc_ref[query_chunk][:, 0:1] == segr_ref[key_chunk][0:1, :]
    return same & (first + (query_chunk - key_chunk) * events >= second)


def project(emb, w_in_ref, write, slope_ref, copies=()):
    width = emb.shape[1]
    normed = (0.5 * normalize(emb.astype(F32))[0]).astype(BF16)
    for block in range(4):
        columns = slice(block * width, (block + 1) * width)
        if copies:
            copies[block].wait()
        half = dot(normed, w_in_ref[:, columns])
        bend = jnp.tanh(half)
        value = half + half * bend
        write(columns, value.astype(BF16))
        if slope_ref is not None:
            sigma = 0.5 + 0.5 * bend
            slope_ref[:, columns] = sigma + value - value * sigma


def prep_kernel(count, index_ref, slots_ref, asked_ref, w_out_ref, *refs):
    mixed_ref, segc_ref, segr_ref, spread_ref, chosen_ref = refs[count:]
    events = spread_ref.shape[1]
    for t in range(count):
        place = index_ref[t]
        mixed_ref[place] = dot_nt(refs[t][0:events, :], w_out_ref[...])
        seg = refs[t][events : events + EXTRA, 0:events].astype(F32)[0:8]
        segr_ref[place] = seg
        segc_ref[place] = jnp.broadcast_to(jnp.transpose(seg)[:, 0:1], segc_ref.shape[1:])
    slot = iota(spread_ref.shape, 0)
    hit = slot == slots_ref[0:1, :]
    for k in range(1, NIDS):
        hit = hit | (slot == slots_ref[k : k + 1, :])
    spread_ref[...] = jnp.where(hit, 1.0, 0.0).astype(BF16)
    owners, capacity = asked_ref.shape
    slots = owners * capacity
    high, low = split_exact(asked_ref[...])
    place = jnp.where(
        iota((capacity, slots), 1) % capacity == iota((capacity, slots), 0), 1.0, 0.0
    ).astype(BF16)
    values = 16.0 * dot(high, place) + dot(low, place)
    mine = iota((owners, slots), 1) // capacity == iota((owners, slots), 0)
    asked = jnp.sum(jnp.where(mine, values, 0.0), 0, keepdims=True).astype(jnp.int32)
    chosen_ref[...] = jnp.where(iota(chosen_ref.shape, 0) == asked, 1.0, 0.0).astype(BF16)


HIDDEN = -1e4


def bent(raw, mask):
    half = jnp.where(mask, raw * (0.5 * SCALE), HIDDEN)
    raised = (1.0 + jnp.tanh(half)).astype(BF16)
    half = half.astype(BF16)
    one, two = BF16(1.0), BF16(2.0)
    return half * raised, raised * (one + half * (two - raised))


def by_twos(start, stop, work):
    twos = (stop - start) // 2

    def step(k, _):
        work([start + 2 * k, start + 2 * k + 1])
        return 0

    lax.fori_loop(0, twos, step, 0)

    @pl.when(stop - start > 2 * twos)
    def _():
        work([stop - 1])


def pipelined(numbers, mask_of, scores, finish):
    masks = {}
    items = [(n, h) for n in range(len(numbers)) for h in range(HEADS)]
    ready = scores(numbers[0], 0)
    for at, (n, h) in enumerate(items):
        now = ready
        if at + 1 < len(items):
            later, later_head = items[at + 1]
            ready = scores(numbers[later], later_head)
        if n not in masks:
            masks[n] = mask_of(numbers[n])
        finish(numbers[n], h, now, masks[n])


class Chunks:
    def __init__(self, proj_ref, gatt_ref, segc_ref, segr_ref, join_ref):
        self.proj, self.gatt = proj_ref, gatt_ref
        self.segc, self.segr, self.join = segc_ref, segr_ref, join_ref
        self.width = gatt_ref.shape[2]

    def cut(self, chunk, part, h):
        return self.proj[chunk, :, head(part, h, self.width)]

    def attend(self, i, start, stop, att_ref):
        def scores(j, h):
            return dot_nt(self.cut(i, 2, h), self.cut(j, 3, h))

        def finish(j, h, raw, mask):
            half = jnp.where(mask, raw * (0.5 * SCALE), HIDDEN)
            weights = (half + half * jnp.tanh(half)).astype(BF16)
            att_ref[:, head(0, h, self.width)] += dot(weights, self.cut(j, 1, h))

        def mask_of(j):
            return visible(i, j, self.segc, self.segr, False)

        by_twos(start, stop, lambda js: pipelined(js, mask_of, scores, finish))

    def finish(self, i, own, att, grad_mixed, emb_ref, w_out_ref, out_ref):
        att_norm, att_inverse = normalize(att)
        gate = self.proj[i, :, 0 : self.width].astype(F32)
        grad_att = norm_back(grad_mixed * gate, att_norm, att_inverse)
        self.gatt[i] = grad_att.astype(BF16)

        @pl.when(i == own)
        def _():
            mixed = (att_norm * gate).astype(BF16)
            out = emb_ref[...].astype(F32) + dot(mixed, w_out_ref[...])
            out_ref[...] = out.astype(BF16)
            self.join[:, 0 : self.width] = grad_mixed * att_norm

    def query_side(self, own, start, stop):
        def scores(j, h):
            grad_att = self.gatt[own, :, head(0, h, self.width)]
            return (
                dot_nt(self.cut(own, 2, h), self.cut(j, 3, h)),
                dot_nt(grad_att, self.cut(j, 1, h)),
            )

        def finish(j, h, pair, mask):
            raw, grad_weights = pair
            _, slope = bent(raw, mask)
            grad_raw = grad_weights.astype(BF16) * slope
            self.join[:, head(2, h, self.width)] += dot(grad_raw, self.cut(j, 3, h))

        def mask_of(j):
            return visible(own, j, self.segc, self.segr, False)

        by_twos(start, stop, lambda js: pipelined(js, mask_of, scores, finish))

    def key_side(self, own, start, stop):
        def scores(i, h):
            grad_att = self.gatt[i, :, head(0, h, self.width)]
            return (
                dot_nt(self.cut(own, 3, h), self.cut(i, 2, h)),
                dot_nt(self.cut(own, 1, h), grad_att),
            )

        def finish(i, h, pair, mask):
            raw, grad_weights = pair
            value, slope = bent(raw, mask)
            grad_raw = grad_weights.astype(BF16) * slope
            self.join[:, head(3, h, self.width)] += dot(grad_raw, self.cut(i, 2, h))
            grad_att = self.gatt[i, :, head(0, h, self.width)]
            self.join[:, head(1, h, self.width)] += dot(value, grad_att)

        def mask_of(i):
            return visible(i, own, self.segc, self.segr, True)

        by_twos(start, stop, lambda chunks: pipelined(chunks, mask_of, scores, finish))


def early_kernel(index_ref, emb_ref, mate_ref, *refs):
    w_in_in, w_out_in, mixed_in, segc_in, segr_in, spread_in, side_in = refs[:7]
    proj_ref, att_ref, gatt_ref, join_ref, slope_ref, out_ref = refs[7:13]
    w_in_ref, w_out_ref, mixed_ref, segc_ref, segr_ref, spread_ref, side_ref, sems = refs[13:]
    width = emb_ref.shape[1]
    blocks = [pl.ds(block * width, width) for block in range(4)]
    pairs = [(w_in_in.at[:, block], w_in_ref.at[:, block]) for block in blocks]
    pairs += [(segc_in, segc_ref), (segr_in, segr_ref), (mixed_in, mixed_ref)]
    pairs += [(w_out_in, w_out_ref), (spread_in, spread_ref), (side_in, side_ref)]
    copies = start_copies(pairs, sems)
    own = index_ref[0]
    mate = index_ref[1]
    base = jnp.minimum(own, mate)
    last = jnp.maximum(own, mate)

    def write_to(place):
        def write(columns, value):
            proj_ref[place - base, :, columns] = value

        return write

    project(emb_ref[...], w_in_ref, write_to(own), slope_ref, copies[:4])
    project(mate_ref[...], w_in_ref, write_to(mate), None)
    for copy in copies[4:]:
        copy.wait()
    att_ref[...] = jnp.zeros_like(att_ref)
    join_ref[...] = jnp.zeros_like(join_ref)
    pair_rows = pl.ds(base, 2)
    chunks = Chunks(
        proj_ref, gatt_ref, segc_ref.at[pair_rows], segr_ref.at[pair_rows], join_ref
    )

    def forward(i, _):
        chunks.attend(i, 0, i + 1, att_ref.at[i])
        return 0

    lax.fori_loop(own - base, last - base + 1, forward, 0)

    @pl.when(base == 0)
    def _():
        def finish(i, _):
            chunks.finish(i, own, att_ref[i], mixed_ref[i], emb_ref, w_out_ref, out_ref)
            return 0

        lax.fori_loop(own, last + 1, finish, 0)
        chunks.query_side(own, 0, own + 1)
        chunks.key_side(own, own, last + 1)


def late_kernel(count, *refs):
    index_ref = refs[0]
    emb_refs = refs[1 : 1 + count]
    (
        proj_pair_ref,
        att_pair_ref,
        gatt_pair_ref,
        join_early_ref,
        slope_ref,
        out_early_ref,
        w_in_ref,
        w_out_ref,
        mixed_ref,
        segc_ref,
        segr_ref,
        spread_ref,
        side_ref,
        out_ref,
        grad_ref,
        proj_ref,
        att_ref,
        gatt_ref,
        join_ref,
        sems,
    ) = refs[1 + count :]
    own = index_ref[0]
    base = jnp.minimum(own, index_ref[1])
    last = jnp.maximum(own, index_ref[1])
    closed = base == 0

    pair_rows = pl.ds(base, 2)
    copies = start_copies(
        (
            (join_early_ref, join_ref),
            (proj_pair_ref, proj_ref.at[pair_rows]),
            (gatt_pair_ref, gatt_ref.at[pair_rows]),
        ),
        sems,
    )

    def write_to(place):
        def write(columns, value):
            proj_ref[place, :, columns] = value

        return write

    for t in range(2, count):
        project(emb_refs[t][...], w_in_ref, write_to(index_ref[t]), None)
    for copy in copies:
        copy.wait()
    chunks = Chunks(proj_ref, gatt_ref, segc_ref, segr_ref, join_ref)

    @pl.when(closed)
    def _():
        out_ref[...] = out_early_ref[...]

    def forward(i, _):
        begun = i <= last

        @pl.when(begun)
        def _():
            att_ref[...] = att_pair_ref[jnp.minimum(i - base, 1)]

        @pl.when(jnp.logical_not(begun))
        def _():
            att_ref[...] = jnp.zeros_like(att_ref)

        chunks.attend(i, 0, jnp.where(begun, base, i + 1), att_ref)
        chunks.finish(i, own, att_ref[...], mixed_ref[i], emb_refs[0], w_out_ref, out_ref)
        return 0

    lax.fori_loop(jnp.where(closed, last + 1, own), count, forward, 0)
    chunks.query_side(own, jnp.where(closed, own + 1, 0), own + 1)
    chunks.key_side(own, jnp.where(closed, last + 1, own), count)

    width = gatt_ref.shape[2]
    grad_normed = None
    for block in range(4):
        columns = slice(block * width, (block + 1) * width)
        joined = join_ref[:, columns] * slope_ref[:, columns]
        if block >= 2:
            joined = joined * (0.5 * SCALE)
        part = dot_nt(joined.astype(BF16), w_in_ref[:, columns])
        grad_normed = part if block == 0 else grad_normed + part
    normed, inverse = normalize(emb_refs[0][...].astype(F32))
    grad = norm_back(grad_normed, normed, inverse) + side_ref[0 : emb_refs[0].shape[0], :].astype(F32)
    grad_ref[...] = dot(spread_ref[...], grad.astype(BF16)).astype(BF16)


def in_hbm(*arrays):
    return [pltpu.with_memory_space_constraint(a, pltpu.HBM) for a in arrays]


def params(mebibytes=12):
    return pltpu.CompilerParams(vmem_limit_bytes=mebibytes * 1024 * 1024)


def flip(value, axis, offset):
    count = lax.axis_size(axis)
    return lax.ppermute(value, axis, [(i, i ^ offset) for i in range(count)])


def gather_blocks(value, axis, known):
    bit = lax.axis_size(axis)
    blocks = {0: value}
    while bit > 1:
        bit //= 2
        for t in list(blocks):
            blocks[t | bit] = known.get(t | bit)
            if blocks[t | bit] is None:
                blocks[t | bit] = flip(blocks[t], axis, bit)
    return [blocks[t] for t in range(lax.axis_size(axis))]


def after(value, earlier):
    return lax.optimization_barrier((value, earlier))[0]


def local(table, item_owner, item_row, segment_ids, w_in, w_out, cotangent):
    owners = lax.axis_size("table") * lax.axis_size("ctx")
    count = lax.axis_size("ctx")
    events, width = cotangent.shape
    id_count = events * NIDS
    capacity = 2 * ((id_count + owners - 1) // owners)
    slot_count = owners * capacity
    axes = ("table", "ctx")
    vmem = pl.BlockSpec(memory_space=pltpu.VMEM)
    smem = pl.BlockSpec(memory_space=pltpu.SMEM)

    def exchange(value):
        return lax.all_to_all(value, axes, split_axis=0, concat_axis=0, tiled=True)

    hbm = pl.BlockSpec(memory_space=pltpu.HBM)
    slots, wanted, side = pl.pallas_call(
        functools.partial(slots_kernel, capacity),
        out_shape=(
            jax.ShapeDtypeStruct((8, events), jnp.int32),
            jax.ShapeDtypeStruct((owners, capacity), jnp.int32),
            jax.ShapeDtypeStruct((events + EXTRA, width), BF16),
        ),
        in_specs=[hbm] * 4,
        out_specs=(vmem, vmem, vmem),
        scratch_shapes=[
            pltpu.VMEM((NIDS, events), jnp.int32),
            pltpu.VMEM((NIDS, events), jnp.int32),
            pltpu.VMEM((1, events), jnp.int32),
            pltpu.SemaphoreType.DMA((4,)),
        ],
        compiler_params=params(),
        name="slots",
    )(*in_hbm(item_owner.T, item_row.T, segment_ids.reshape(1, events), cotangent))
    asked = exchange(wanted)
    rows = pl.pallas_call(
        select_kernel,
        out_shape=pltpu.HBM((slot_count, width), BF16),
        in_specs=[vmem, hbm],
        out_specs=hbm,
        scratch_shapes=[
            pltpu.VMEM(table.shape, BF16),
            pltpu.VMEM((slot_count, width), BF16),
            pltpu.SemaphoreType.DMA((5,)),
        ],
        compiler_params=params(),
        name="select",
    )(asked, *in_hbm(table))
    fetched = exchange(rows.reshape(owners, capacity, width)).reshape(slot_count, width)
    side_far = flip(side, "ctx", count // 2)
    side_mate = flip(side, "ctx", 1)
    side_blocks = gather_blocks(side, "ctx", {1: side_mate, count // 2: after(side_far, rows)})
    index = lax.axis_index("ctx").astype(jnp.int32) ^ jnp.arange(count, dtype=jnp.int32)
    prep_shapes = (
        jax.ShapeDtypeStruct((count, events, width), F32),
        jax.ShapeDtypeStruct((count, events, 128), F32),
        jax.ShapeDtypeStruct((count, 8, events), F32),
        jax.ShapeDtypeStruct((slot_count, events), BF16),
    )
    *prepared, chosen = pl.pallas_call(
        functools.partial(prep_kernel, count),
        out_shape=tuple(pltpu.HBM(a.shape, a.dtype) for a in prep_shapes)
        + (jax.ShapeDtypeStruct((table.shape[0], slot_count), BF16),),
        in_specs=[smem] + [vmem] * (3 + count),
        out_specs=(vmem,) * 5,
        compiler_params=params(20),
        name="prep",
    )(index, slots, asked, w_out, *side_blocks)
    prepared = in_hbm(*prepared)
    fetched, prepared = lax.optimization_barrier((fetched, prepared))
    embedded = pl.pallas_call(
        embed_kernel,
        out_shape=jax.ShapeDtypeStruct((events, width), BF16),
        compiler_params=params(),
        name="embed",
    )(slots, fetched)
    emb_far = flip(embedded, "ctx", count // 2)
    emb_mate = flip(embedded, "ctx", 1)
    event_shape = jax.ShapeDtypeStruct((events, width), BF16)
    early = pl.pallas_call(
        early_kernel,
        out_shape=(
            jax.ShapeDtypeStruct((2, events, 4 * width), BF16),
            jax.ShapeDtypeStruct((2, events, width), F32),
            jax.ShapeDtypeStruct((2, events, width), BF16),
            jax.ShapeDtypeStruct((events, 4 * width), F32),
            jax.ShapeDtypeStruct((events, 4 * width), F32),
            event_shape,
        )
        + tuple(jax.ShapeDtypeStruct(a.shape, BF16) for a in (w_in, w_out))
        + prep_shapes
        + (jax.ShapeDtypeStruct(side.shape, BF16),),
        in_specs=[smem, vmem, vmem] + [hbm] * 7,
        out_specs=(vmem,) * 13,
        scratch_shapes=[pltpu.SemaphoreType.DMA((10,))],
        compiler_params=params(20),
        name="early",
    )(index, embedded, emb_mate, *in_hbm(w_in, w_out), *prepared, *in_hbm(side))
    emb_blocks = gather_blocks(embedded, "ctx", {1: emb_mate, count // 2: after(emb_far, early)})
    layer_out, slot_grad = pl.pallas_call(
        functools.partial(late_kernel, count),
        out_shape=(event_shape, jax.ShapeDtypeStruct((slot_count, width), BF16)),
        in_specs=[smem] + [vmem] * (13 + count),
        out_specs=(vmem, vmem),
        scratch_shapes=[
            pltpu.VMEM((count, events, 4 * width), BF16),
            pltpu.VMEM((events, width), F32),
            pltpu.VMEM((count, events, width), BF16),
            pltpu.VMEM((events, 4 * width), F32),
            pltpu.SemaphoreType.DMA((3,)),
        ],
        compiler_params=params(28),
        name="late",
    )(index, *emb_blocks, *early)
    returned = exchange(slot_grad.reshape(owners, capacity, width)).reshape(slot_count, width)
    row_grad = pl.pallas_call(
        collect_kernel,
        out_shape=pltpu.HBM(table.shape, F32),
        in_specs=[vmem, vmem],
        out_specs=hbm,
        scratch_shapes=[pltpu.VMEM(table.shape, F32), pltpu.SemaphoreType.DMA((4,))],
        compiler_params=params(),
        name="collect",
    )(chosen, returned)
    return layer_out, row_grad


def solution(mesh):
    rows = P(("table", "ctx"), None)
    return jax.shard_map(
        local,
        mesh=mesh,
        in_specs=(rows, rows, rows, P("table", "ctx"), P(), P(), rows),
        out_specs=(rows, rows),
        check_vma=False,
    )
```

```python
import functools

import jax
import jax.numpy as jnp
from jax import lax
from jax.experimental import pallas as pl
from jax.experimental.pallas import tpu as pltpu
from jax.sharding import PartitionSpec as P

HEADS = 4
HEAD_DIM = 128
NIDS = 2
EPS = 1e-06

F32 = jnp.float32
BF16 = jnp.bfloat16


def dot(a, b):
    return jnp.dot(a, b, preferred_element_type=F32)


def dot_nt(a, b):
    return lax.dot_general(a, b, (((1,), (1,)), ((), ())), preferred_element_type=F32)


def iota(shape, dim):
    return lax.broadcasted_iota(jnp.int32, shape, dim)


def normalize(values):
    centred = values - jnp.mean(values, -1, keepdims=True)
    inverse = lax.rsqrt(jnp.mean(centred * centred, -1, keepdims=True) + EPS)
    return centred * inverse, inverse


def norm_back(grad_norm, normed, inverse):
    mean_grad = jnp.mean(grad_norm, -1, keepdims=True)
    mean_cross = jnp.mean(grad_norm * normed, -1, keepdims=True)
    return (grad_norm - mean_grad - normed * mean_cross) * inverse


def split_exact(values):
    return (values >> 4).astype(F32).astype(BF16), (values & 15).astype(F32).astype(BF16)


def start_copies(pairs, sems):
    copies = [pltpu.make_async_copy(a, b, sems.at[i]) for i, (a, b) in enumerate(pairs)]
    for copy in copies:
        copy.start()
    return copies


EXTRA = 16


def slots_kernel(
    capacity,
    owner_in,
    row_in,
    seg_in,
    cot_in,
    slots_ref,
    wanted_ref,
    side_ref,
    owner_ref,
    row_ref,
    seg_ref,
    sems,
):
    events, width = cot_in.shape
    pairs = (
        (owner_in, owner_ref),
        (row_in, row_ref),
        (seg_in, seg_ref),
        (cot_in, side_ref.at[0:events]),
    )
    copies = start_copies(pairs, sems)
    for copy in copies[:3]:
        copy.wait()
    side_ref[events:, :] = jnp.zeros((EXTRA, width), BF16)
    segments = jnp.broadcast_to(seg_ref[...].astype(F32), (EXTRA, events))
    side_ref[events:, 0:events] = segments.astype(BF16)
    owners = wanted_ref.shape[0]
    owner = jnp.concatenate([owner_ref[k : k + 1, :] for k in range(NIDS)], 1)
    row = jnp.concatenate([row_ref[k : k + 1, :] for k in range(NIDS)], 1)
    ids = owner.shape[1]
    named = iota((owners, ids), 0) == owner
    named_f = jnp.where(named, 1.0, 0.0)
    before = jnp.where(iota((ids, ids), 0) < iota((ids, ids), 1), 1.0, 0.0).astype(BF16)
    earlier = dot(named_f.astype(BF16), before)
    rank = jnp.sum(earlier * named_f, 0, keepdims=True).astype(jnp.int32)
    slot = owner * capacity + rank
    slots_ref[...] = jnp.full(slots_ref.shape, -1, jnp.int32)
    for k in range(NIDS):
        slots_ref[k : k + 1, :] = slot[:, k * events : (k + 1) * events]
    ranked = jnp.where(iota((capacity, ids), 0) == rank, 1.0, 0.0).astype(BF16)
    high, low = (row >> 4).astype(F32), (row & 15).astype(F32)
    wanted = 16.0 * dot_nt((named_f * high).astype(BF16), ranked) + dot_nt(
        (named_f * low).astype(BF16), ranked
    )
    wanted_ref[...] = wanted.astype(jnp.int32)
    for copy in copies[3:]:
        copy.wait()


def select_kernel(asked_ref, table_in, out_ref, table_ref, rows_ref, sems):
    (table_copy,) = start_copies(((table_in, table_ref),), sems)
    owners, capacity = asked_ref.shape
    rows = table_ref.shape[0]
    parts = sems.shape[0] - 1
    step = owners // parts
    columns = jnp.transpose(asked_ref[...])
    lane = iota((capacity, rows), 1)
    copies = []
    for part in range(parts):
        sources = range(part * step, (part + 1) * step)
        chosen = [jnp.where(lane == columns[:, s : s + 1], 1.0, 0.0) for s in sources]
        chosen = jnp.concatenate(chosen, 0).astype(BF16)
        if part == 0:
            table_copy.wait()
        place = pl.ds(part * step * capacity, step * capacity)
        rows_ref[place, :] = dot(chosen, table_ref[...]).astype(BF16)
        copy = pltpu.make_async_copy(rows_ref.at[place], out_ref.at[place], sems.at[1 + part])
        copy.start()
        copies.append(copy)
    for copy in copies:
        copy.wait()


def embed_kernel(slots_ref, fetched_ref, out_ref):
    events = out_ref.shape[0]
    slots = fetched_ref.shape[0]
    column = jnp.transpose(slots_ref[...])
    lane = iota((events, slots), 1)
    hit = lane == column[:, 0:1]
    for k in range(1, NIDS):
        hit = hit | (lane == column[:, k : k + 1])
    picked = jnp.where(hit, 1.0, 0.0).astype(BF16)
    out_ref[...] = dot(picked, fetched_ref[...]).astype(BF16)


def collect_kernel(chosen_ref, returned_ref, out_ref, rows_ref, sems):
    parts = sems.shape[0]
    step = rows_ref.shape[0] // parts
    copies = []
    for part in range(parts):
        place = pl.ds(part * step, step)
        rows_ref[place, :] = dot(chosen_ref[place, :], returned_ref[...])
        copy = pltpu.make_async_copy(rows_ref.at[place], out_ref.at[place], sems.at[part])
        copy.start()
        copies.append(copy)
    for copy in copies:
        copy.wait()


SCALE = HEAD_DIM ** (-0.5)


def head(part, h, width):
    return slice(part * width + h * HEAD_DIM, part * width + (h + 1) * HEAD_DIM)


def visible(query_chunk, key_chunk, segc_ref, segr_ref, flip):
    events = segr_ref.shape[2]
    first, second = iota((events, events), 0), iota((events, events), 1)
    if flip:
        same = segc_ref[key_chunk][:, 0:1] == segr_ref[query_chunk][0:1, :]
        return same & (first <= second + (query_chunk - key_chunk) * events)
    same = segc_ref[query_chunk][:, 0:1] == segr_ref[key_chunk][0:1, :]
    return same & (first + (query_chunk - key_chunk) * events >= second)


def project(emb, w_in_ref, write, slope_ref):
    width = emb.shape[1]
    normed = (0.5 * normalize(emb.astype(F32))[0]).astype(BF16)
    for block in range(4):
        columns = slice(block * width, (block + 1) * width)
        half = dot(normed, w_in_ref[:, columns])
        bend = jnp.tanh(half)
        value = half + half * bend
        write(columns, value.astype(BF16))
        if slope_ref is not None:
            sigma = 0.5 + 0.5 * bend
            slope_ref[:, columns] = sigma + value - value * sigma


def prep_kernel(count, index_ref, slots_ref, asked_ref, w_out_ref, *refs):
    mixed_ref, segc_ref, segr_ref, spread_ref, chosen_ref = refs[count:]
    events = spread_ref.shape[1]
    for t in range(count):
        place = index_ref[t]
        mixed_ref[place] = dot_nt(refs[t][0:events, :], w_out_ref[...])
        seg = refs[t][events : events + EXTRA, 0:events].astype(F32)[0:8]
        segr_ref[place] = seg
        segc_ref[place] = jnp.broadcast_to(jnp.transpose(seg)[:, 0:1], segc_ref.shape[1:])
    slot = iota(spread_ref.shape, 0)
    hit = slot == slots_ref[0:1, :]
    for k in range(1, NIDS):
        hit = hit | (slot == slots_ref[k : k + 1, :])
    spread_ref[...] = jnp.where(hit, 1.0, 0.0).astype(BF16)
    owners, capacity = asked_ref.shape
    slots = owners * capacity
    high, low = split_exact(asked_ref[...])
    place = jnp.where(
        iota((capacity, slots), 1) % capacity == iota((capacity, slots), 0), 1.0, 0.0
    ).astype(BF16)
    values = 16.0 * dot(high, place) + dot(low, place)
    mine = iota((owners, slots), 1) // capacity == iota((owners, slots), 0)
    asked = jnp.sum(jnp.where(mine, values, 0.0), 0, keepdims=True).astype(jnp.int32)
    chosen_ref[...] = jnp.where(iota(chosen_ref.shape, 0) == asked, 1.0, 0.0).astype(BF16)


HIDDEN = -1e4


def bent(raw, mask):
    half = jnp.where(mask, raw * (0.5 * SCALE), HIDDEN)
    raised = (1.0 + jnp.tanh(half)).astype(BF16)
    half = half.astype(BF16)
    one, two = BF16(1.0), BF16(2.0)
    return half * raised, raised * (one + half * (two - raised))


def by_twos(start, stop, work):
    twos = (stop - start) // 2

    def step(k, _):
        work([start + 2 * k, start + 2 * k + 1])
        return 0

    lax.fori_loop(0, twos, step, 0)

    @pl.when(stop - start > 2 * twos)
    def _():
        work([stop - 1])


def pipelined(numbers, mask_of, scores, finish):
    masks = {}
    items = [(n, h) for n in range(len(numbers)) for h in range(HEADS)]
    ready = scores(numbers[0], 0)
    for at, (n, h) in enumerate(items):
        now = ready
        if at + 1 < len(items):
            later, later_head = items[at + 1]
            ready = scores(numbers[later], later_head)
        if n not in masks:
            masks[n] = mask_of(numbers[n])
        finish(numbers[n], h, now, masks[n])


class Chunks:
    def __init__(self, proj_ref, gatt_ref, segc_ref, segr_ref, join_ref):
        self.proj, self.gatt = proj_ref, gatt_ref
        self.segc, self.segr, self.join = segc_ref, segr_ref, join_ref
        self.width = gatt_ref.shape[2]

    def cut(self, chunk, part, h):
        return self.proj[chunk, :, head(part, h, self.width)]

    def attend(self, i, start, stop, att_ref):
        def scores(j, h):
            return dot_nt(self.cut(i, 2, h), self.cut(j, 3, h))

        def finish(j, h, raw, mask):
            half = jnp.where(mask, raw * (0.5 * SCALE), HIDDEN)
            weights = (half + half * jnp.tanh(half)).astype(BF16)
            att_ref[:, head(0, h, self.width)] += dot(weights, self.cut(j, 1, h))

        def mask_of(j):
            return visible(i, j, self.segc, self.segr, False)

        by_twos(start, stop, lambda js: pipelined(js, mask_of, scores, finish))

    def finish(self, i, own, att, grad_mixed, emb_ref, w_out_ref, out_ref):
        att_norm, att_inverse = normalize(att)
        gate = self.proj[i, :, 0 : self.width].astype(F32)
        grad_att = norm_back(grad_mixed * gate, att_norm, att_inverse)
        self.gatt[i] = grad_att.astype(BF16)

        @pl.when(i == own)
        def _():
            mixed = (att_norm * gate).astype(BF16)
            out = emb_ref[...].astype(F32) + dot(mixed, w_out_ref[...])
            out_ref[...] = out.astype(BF16)
            self.join[:, 0 : self.width] = grad_mixed * att_norm

    def query_side(self, own, start, stop):
        def scores(j, h):
            grad_att = self.gatt[own, :, head(0, h, self.width)]
            return (
                dot_nt(self.cut(own, 2, h), self.cut(j, 3, h)),
                dot_nt(grad_att, self.cut(j, 1, h)),
            )

        def finish(j, h, pair, mask):
            raw, grad_weights = pair
            _, slope = bent(raw, mask)
            grad_raw = grad_weights.astype(BF16) * slope
            self.join[:, head(2, h, self.width)] += dot(grad_raw, self.cut(j, 3, h))

        def mask_of(j):
            return visible(own, j, self.segc, self.segr, False)

        by_twos(start, stop, lambda js: pipelined(js, mask_of, scores, finish))

    def key_side(self, own, start, stop):
        def scores(i, h):
            grad_att = self.gatt[i, :, head(0, h, self.width)]
            return (
                dot_nt(self.cut(own, 3, h), self.cut(i, 2, h)),
                dot_nt(self.cut(own, 1, h), grad_att),
            )

        def finish(i, h, pair, mask):
            raw, grad_weights = pair
            value, slope = bent(raw, mask)
            grad_raw = grad_weights.astype(BF16) * slope
            self.join[:, head(3, h, self.width)] += dot(grad_raw, self.cut(i, 2, h))
            grad_att = self.gatt[i, :, head(0, h, self.width)]
            self.join[:, head(1, h, self.width)] += dot(value, grad_att)

        def mask_of(i):
            return visible(i, own, self.segc, self.segr, True)

        by_twos(start, stop, lambda chunks: pipelined(chunks, mask_of, scores, finish))


def early_kernel(index_ref, emb_ref, mate_ref, *refs):
    w_in_in, w_out_in, mixed_in, segc_in, segr_in, spread_in, side_in = refs[:7]
    proj_ref, att_ref, gatt_ref, join_ref, slope_ref, out_ref = refs[7:13]
    w_in_ref, w_out_ref, mixed_ref, segc_ref, segr_ref, spread_ref, side_ref, sems = refs[13:]
    pairs = [(segc_in, segc_ref), (segr_in, segr_ref), (mixed_in, mixed_ref)]
    pairs += [(w_out_in, w_out_ref), (spread_in, spread_ref), (side_in, side_ref)]
    pairs += [(w_in_in, w_in_ref)]
    copies = start_copies(pairs, sems)
    own = index_ref[0]
    mate = index_ref[1]
    base = jnp.minimum(own, mate)
    last = jnp.maximum(own, mate)

    def write_to(place):
        def write(columns, value):
            proj_ref[place - base, :, columns] = value

        return write

    project(emb_ref[...], w_in_in, write_to(own), slope_ref)
    project(mate_ref[...], w_in_in, write_to(mate), None)
    for copy in copies:
        copy.wait()
    att_ref[...] = jnp.zeros_like(att_ref)
    join_ref[...] = jnp.zeros_like(join_ref)
    pair_rows = pl.ds(base, 2)
    chunks = Chunks(
        proj_ref, gatt_ref, segc_ref.at[pair_rows], segr_ref.at[pair_rows], join_ref
    )

    def forward(i, _):
        chunks.attend(i, 0, i + 1, att_ref.at[i])
        return 0

    lax.fori_loop(own - base, last - base + 1, forward, 0)

    @pl.when(base == 0)
    def _():
        def finish(i, _):
            chunks.finish(i, own, att_ref[i], mixed_ref[i], emb_ref, w_out_ref, out_ref)
            return 0

        lax.fori_loop(own, last + 1, finish, 0)
        chunks.query_side(own, 0, own + 1)
        chunks.key_side(own, own, last + 1)


def project_kernel(emb_ref, w_in_ref, proj_ref):
    def write(columns, value):
        proj_ref[:, columns] = value

    project(emb_ref[...], w_in_ref, write, None)


def late_kernel(count, *refs):
    index_ref = refs[0]
    emb_refs = refs[1 : 1 + count]
    proj_far_ref = refs[1 + count]
    (
        proj_pair_ref,
        att_pair_ref,
        gatt_pair_ref,
        join_early_ref,
        slope_ref,
        out_early_ref,
        w_in_ref,
        w_out_ref,
        mixed_ref,
        segc_ref,
        segr_ref,
        spread_ref,
        side_ref,
        out_ref,
        grad_ref,
        proj_ref,
        att_ref,
        gatt_ref,
        join_ref,
        sems,
    ) = refs[2 + count :]
    own = index_ref[0]
    base = jnp.minimum(own, index_ref[1])
    last = jnp.maximum(own, index_ref[1])
    closed = base == 0

    pair_rows = pl.ds(base, 2)
    copies = start_copies(
        (
            (join_early_ref, join_ref),
            (proj_pair_ref, proj_ref.at[pair_rows]),
            (gatt_pair_ref, gatt_ref.at[pair_rows]),
            (proj_far_ref, proj_ref.at[index_ref[count // 2]]),
        ),
        sems,
    )

    def write_to(place):
        def write(columns, value):
            proj_ref[place, :, columns] = value

        return write

    for t in range(2, count):
        if t == count // 2:
            continue
        project(emb_refs[t][...], w_in_ref, write_to(index_ref[t]), None)
    for copy in copies:
        copy.wait()
    chunks = Chunks(proj_ref, gatt_ref, segc_ref, segr_ref, join_ref)

    @pl.when(closed)
    def _():
        out_ref[...] = out_early_ref[...]

    def forward(i, _):
        begun = i <= last

        @pl.when(begun)
        def _():
            att_ref[...] = att_pair_ref[jnp.minimum(i - base, 1)]

        @pl.when(jnp.logical_not(begun))
        def _():
            att_ref[...] = jnp.zeros_like(att_ref)

        chunks.attend(i, 0, jnp.where(begun, base, i + 1), att_ref)
        chunks.finish(i, own, att_ref[...], mixed_ref[i], emb_refs[0], w_out_ref, out_ref)
        return 0

    lax.fori_loop(jnp.where(closed, last + 1, own), count, forward, 0)
    chunks.query_side(own, jnp.where(closed, own + 1, 0), own + 1)
    chunks.key_side(own, jnp.where(closed, last + 1, own), count)

    width = gatt_ref.shape[2]
    grad_normed = None
    for block in range(4):
        columns = slice(block * width, (block + 1) * width)
        joined = join_ref[:, columns] * slope_ref[:, columns]
        if block >= 2:
            joined = joined * (0.5 * SCALE)
        part = dot_nt(joined.astype(BF16), w_in_ref[:, columns])
        grad_normed = part if block == 0 else grad_normed + part
    normed, inverse = normalize(emb_refs[0][...].astype(F32))
    grad = norm_back(grad_normed, normed, inverse) + side_ref[0 : emb_refs[0].shape[0], :].astype(F32)
    grad_ref[...] = dot(spread_ref[...], grad.astype(BF16)).astype(BF16)


def in_hbm(*arrays):
    return [pltpu.with_memory_space_constraint(a, pltpu.HBM) for a in arrays]


def params(mebibytes=12):
    return pltpu.CompilerParams(vmem_limit_bytes=mebibytes * 1024 * 1024)


def flip(value, axis, offset):
    count = lax.axis_size(axis)
    return lax.ppermute(value, axis, [(i, i ^ offset) for i in range(count)])


def gather_blocks(value, axis, known):
    bit = lax.axis_size(axis)
    blocks = {0: value}
    while bit > 1:
        bit //= 2
        for t in list(blocks):
            blocks[t | bit] = known.get(t | bit)
            if blocks[t | bit] is None:
                blocks[t | bit] = flip(blocks[t], axis, bit)
    return [blocks[t] for t in range(lax.axis_size(axis))]


def after(value, earlier):
    return lax.optimization_barrier((value, earlier))[0]


def local(table, item_owner, item_row, segment_ids, w_in, w_out, cotangent):
    owners = lax.axis_size("table") * lax.axis_size("ctx")
    count = lax.axis_size("ctx")
    events, width = cotangent.shape
    id_count = events * NIDS
    capacity = 2 * ((id_count + owners - 1) // owners)
    slot_count = owners * capacity
    axes = ("table", "ctx")
    vmem = pl.BlockSpec(memory_space=pltpu.VMEM)
    smem = pl.BlockSpec(memory_space=pltpu.SMEM)

    def exchange(value):
        return lax.all_to_all(value, axes, split_axis=0, concat_axis=0, tiled=True)

    hbm = pl.BlockSpec(memory_space=pltpu.HBM)
    slots, wanted, side = pl.pallas_call(
        functools.partial(slots_kernel, capacity),
        out_shape=(
            jax.ShapeDtypeStruct((8, events), jnp.int32),
            jax.ShapeDtypeStruct((owners, capacity), jnp.int32),
            jax.ShapeDtypeStruct((events + EXTRA, width), BF16),
        ),
        in_specs=[hbm] * 4,
        out_specs=(vmem, vmem, vmem),
        scratch_shapes=[
            pltpu.VMEM((NIDS, events), jnp.int32),
            pltpu.VMEM((NIDS, events), jnp.int32),
            pltpu.VMEM((1, events), jnp.int32),
            pltpu.SemaphoreType.DMA((4,)),
        ],
        compiler_params=params(),
        name="slots",
    )(*in_hbm(item_owner.T, item_row.T, segment_ids.reshape(1, events), cotangent))
    asked = exchange(wanted)
    rows = pl.pallas_call(
        select_kernel,
        out_shape=pltpu.HBM((slot_count, width), BF16),
        in_specs=[vmem, hbm],
        out_specs=hbm,
        scratch_shapes=[
            pltpu.VMEM(table.shape, BF16),
            pltpu.VMEM((slot_count, width), BF16),
            pltpu.SemaphoreType.DMA((5,)),
        ],
        compiler_params=params(),
        name="select",
    )(asked, *in_hbm(table))
    fetched = exchange(rows.reshape(owners, capacity, width)).reshape(slot_count, width)
    side_far = flip(side, "ctx", count // 2)
    side_mate = flip(side, "ctx", 1)
    side_blocks = gather_blocks(side, "ctx", {1: side_mate, count // 2: after(side_far, rows)})
    index = lax.axis_index("ctx").astype(jnp.int32) ^ jnp.arange(count, dtype=jnp.int32)
    prep_shapes = (
        jax.ShapeDtypeStruct((count, events, width), F32),
        jax.ShapeDtypeStruct((count, events, 128), F32),
        jax.ShapeDtypeStruct((count, 8, events), F32),
        jax.ShapeDtypeStruct((slot_count, events), BF16),
    )
    *prepared, chosen = pl.pallas_call(
        functools.partial(prep_kernel, count),
        out_shape=tuple(pltpu.HBM(a.shape, a.dtype) for a in prep_shapes)
        + (jax.ShapeDtypeStruct((table.shape[0], slot_count), BF16),),
        in_specs=[smem] + [vmem] * (3 + count),
        out_specs=(vmem,) * 5,
        compiler_params=params(20),
        name="prep",
    )(index, slots, asked, w_out, *side_blocks)
    prepared = in_hbm(*prepared)
    fetched, prepared = lax.optimization_barrier((fetched, prepared))
    embedded = pl.pallas_call(
        embed_kernel,
        out_shape=jax.ShapeDtypeStruct((events, width), BF16),
        compiler_params=params(),
        name="embed",
    )(slots, fetched)
    emb_far = flip(embedded, "ctx", count // 2)
    emb_mate = flip(embedded, "ctx", 1)
    event_shape = jax.ShapeDtypeStruct((events, width), BF16)
    early = pl.pallas_call(
        early_kernel,
        out_shape=(
            jax.ShapeDtypeStruct((2, events, 4 * width), BF16),
            jax.ShapeDtypeStruct((2, events, width), F32),
            jax.ShapeDtypeStruct((2, events, width), BF16),
            jax.ShapeDtypeStruct((events, 4 * width), F32),
            jax.ShapeDtypeStruct((events, 4 * width), F32),
            event_shape,
        )
        + tuple(jax.ShapeDtypeStruct(a.shape, BF16) for a in (w_in, w_out))
        + prep_shapes
        + (jax.ShapeDtypeStruct(side.shape, BF16),),
        in_specs=[smem, vmem, vmem, vmem] + [hbm] * 6,
        out_specs=(vmem,) * 13,
        scratch_shapes=[pltpu.SemaphoreType.DMA((7,))],
        compiler_params=params(20),
        name="early",
    )(index, embedded, emb_mate, w_in, *in_hbm(w_out), *prepared, *in_hbm(side))
    emb_far = after(emb_far, early[0])
    proj_far = pl.pallas_call(
        project_kernel,
        out_shape=jax.ShapeDtypeStruct((events, 4 * width), BF16),
        compiler_params=params(),
        name="project_far",
    )(emb_far, early[6])
    emb_blocks = gather_blocks(embedded, "ctx", {1: emb_mate, count // 2: emb_far})
    layer_out, slot_grad = pl.pallas_call(
        functools.partial(late_kernel, count),
        out_shape=(event_shape, jax.ShapeDtypeStruct((slot_count, width), BF16)),
        in_specs=[smem] + [vmem] * (14 + count),
        out_specs=(vmem, vmem),
        scratch_shapes=[
            pltpu.VMEM((count, events, 4 * width), BF16),
            pltpu.VMEM((events, width), F32),
            pltpu.VMEM((count, events, width), BF16),
            pltpu.VMEM((events, 4 * width), F32),
            pltpu.SemaphoreType.DMA((4,)),
        ],
        compiler_params=params(28),
        name="late",
    )(index, *emb_blocks, proj_far, *early)
    returned = exchange(slot_grad.reshape(owners, capacity, width)).reshape(slot_count, width)
    row_grad = pl.pallas_call(
        collect_kernel,
        out_shape=pltpu.HBM(table.shape, F32),
        in_specs=[vmem, vmem],
        out_specs=hbm,
        scratch_shapes=[pltpu.VMEM(table.shape, F32), pltpu.SemaphoreType.DMA((4,))],
        compiler_params=params(),
        name="collect",
    )(chosen, returned)
    return layer_out, row_grad


def solution(mesh):
    rows = P(("table", "ctx"), None)
    return jax.shard_map(
        local,
        mesh=mesh,
        in_specs=(rows, rows, rows, P("table", "ctx"), P(), P(), rows),
        out_specs=(rows, rows),
        check_vma=False,
    )
```

```python
import functools

import jax
import jax.numpy as jnp
from jax import lax
from jax.experimental import pallas as pl
from jax.experimental.pallas import tpu as pltpu
from jax.sharding import PartitionSpec as P

HEADS = 4
HEAD_DIM = 128
NIDS = 2
EPS = 1e-06

F32 = jnp.float32
BF16 = jnp.bfloat16


def dot(a, b):
    return jnp.dot(a, b, preferred_element_type=F32)


def dot_nt(a, b):
    return lax.dot_general(a, b, (((1,), (1,)), ((), ())), preferred_element_type=F32)


def iota(shape, dim):
    return lax.broadcasted_iota(jnp.int32, shape, dim)


def normalize(values):
    centred = values - jnp.mean(values, -1, keepdims=True)
    inverse = lax.rsqrt(jnp.mean(centred * centred, -1, keepdims=True) + EPS)
    return centred * inverse, inverse


def norm_back(grad_norm, normed, inverse):
    mean_grad = jnp.mean(grad_norm, -1, keepdims=True)
    mean_cross = jnp.mean(grad_norm * normed, -1, keepdims=True)
    return (grad_norm - mean_grad - normed * mean_cross) * inverse


def split_exact(values):
    return (values >> 4).astype(F32).astype(BF16), (values & 15).astype(F32).astype(BF16)


def start_copies(pairs, sems):
    copies = [pltpu.make_async_copy(a, b, sems.at[i]) for i, (a, b) in enumerate(pairs)]
    for copy in copies:
        copy.start()
    return copies


EXTRA = 16


def slots_kernel(
    capacity,
    owner_in,
    row_in,
    seg_in,
    cot_in,
    slots_ref,
    wanted_ref,
    side_ref,
    owner_ref,
    row_ref,
    seg_ref,
    sems,
):
    events, width = cot_in.shape
    pairs = (
        (owner_in, owner_ref),
        (row_in, row_ref),
        (seg_in, seg_ref),
        (cot_in, side_ref.at[0:events]),
    )
    copies = start_copies(pairs, sems)
    for copy in copies[:3]:
        copy.wait()
    side_ref[events:, :] = jnp.zeros((EXTRA, width), BF16)
    segments = jnp.broadcast_to(seg_ref[...].astype(F32), (EXTRA, events))
    side_ref[events:, 0:events] = segments.astype(BF16)
    owners = wanted_ref.shape[0]
    owner = jnp.concatenate([owner_ref[k : k + 1, :] for k in range(NIDS)], 1)
    row = jnp.concatenate([row_ref[k : k + 1, :] for k in range(NIDS)], 1)
    ids = owner.shape[1]
    named = iota((owners, ids), 0) == owner
    named_f = jnp.where(named, 1.0, 0.0)
    before = jnp.where(iota((ids, ids), 0) < iota((ids, ids), 1), 1.0, 0.0).astype(BF16)
    earlier = dot(named_f.astype(BF16), before)
    rank = jnp.sum(earlier * named_f, 0, keepdims=True).astype(jnp.int32)
    slot = owner * capacity + rank
    slots_ref[...] = jnp.full(slots_ref.shape, -1, jnp.int32)
    for k in range(NIDS):
        slots_ref[k : k + 1, :] = slot[:, k * events : (k + 1) * events]
    ranked = jnp.where(iota((capacity, ids), 0) == rank, 1.0, 0.0).astype(BF16)
    high, low = (row >> 4).astype(F32), (row & 15).astype(F32)
    wanted = 16.0 * dot_nt((named_f * high).astype(BF16), ranked) + dot_nt(
        (named_f * low).astype(BF16), ranked
    )
    wanted_ref[...] = wanted.astype(jnp.int32)
    for copy in copies[3:]:
        copy.wait()


def select_kernel(asked_ref, table_in, out_ref, table_ref, rows_ref, sems):
    (table_copy,) = start_copies(((table_in, table_ref),), sems)
    owners, capacity = asked_ref.shape
    rows = table_ref.shape[0]
    parts = sems.shape[0] - 1
    step = owners // parts
    columns = jnp.transpose(asked_ref[...])
    lane = iota((capacity, rows), 1)
    copies = []
    for part in range(parts):
        sources = range(part * step, (part + 1) * step)
        chosen = [jnp.where(lane == columns[:, s : s + 1], 1.0, 0.0) for s in sources]
        chosen = jnp.concatenate(chosen, 0).astype(BF16)
        if part == 0:
            table_copy.wait()
        place = pl.ds(part * step * capacity, step * capacity)
        rows_ref[place, :] = dot(chosen, table_ref[...]).astype(BF16)
        copy = pltpu.make_async_copy(rows_ref.at[place], out_ref.at[place], sems.at[1 + part])
        copy.start()
        copies.append(copy)
    for copy in copies:
        copy.wait()


def embed_kernel(slots_ref, fetched_ref, out_ref):
    events = out_ref.shape[0]
    slots = fetched_ref.shape[0]
    column = jnp.transpose(slots_ref[...])
    lane = iota((events, slots), 1)
    hit = lane == column[:, 0:1]
    for k in range(1, NIDS):
        hit = hit | (lane == column[:, k : k + 1])
    picked = jnp.where(hit, 1.0, 0.0).astype(BF16)
    out_ref[...] = dot(picked, fetched_ref[...]).astype(BF16)


def collect_kernel(chosen_ref, returned_ref, out_ref, rows_ref, sems):
    parts = sems.shape[0]
    step = rows_ref.shape[0] // parts
    copies = []
    for part in range(parts):
        place = pl.ds(part * step, step)
        rows_ref[place, :] = dot(chosen_ref[place, :], returned_ref[...])
        copy = pltpu.make_async_copy(rows_ref.at[place], out_ref.at[place], sems.at[part])
        copy.start()
        copies.append(copy)
    for copy in copies:
        copy.wait()


SCALE = HEAD_DIM ** (-0.5)


def head(part, h, width):
    return slice(part * width + h * HEAD_DIM, part * width + (h + 1) * HEAD_DIM)


def visible(query_chunk, key_chunk, segc_ref, segr_ref, flip):
    events = segr_ref.shape[2]
    first, second = iota((events, events), 0), iota((events, events), 1)
    if flip:
        same = segc_ref[key_chunk][:, 0:1] == segr_ref[query_chunk][0:1, :]
        return same & (first <= second + (query_chunk - key_chunk) * events)
    same = segc_ref[query_chunk][:, 0:1] == segr_ref[key_chunk][0:1, :]
    return same & (first + (query_chunk - key_chunk) * events >= second)


def project(emb, w_in_ref, write, slope_ref):
    width = emb.shape[1]
    normed = (0.5 * normalize(emb.astype(F32))[0]).astype(BF16)
    for block in range(4):
        columns = slice(block * width, (block + 1) * width)
        half = dot(normed, w_in_ref[:, columns])
        bend = jnp.tanh(half)
        value = half + half * bend
        write(columns, value.astype(BF16))
        if slope_ref is not None:
            sigma = 0.5 + 0.5 * bend
            slope_ref[:, columns] = sigma + value - value * sigma


def prep_kernel(count, index_ref, w_out_in, *refs):
    mixed_ref, segc_ref, segr_ref, w_out_ref, sems = refs[count:]
    (copy,) = start_copies(((w_out_in, w_out_ref),), sems)
    events = mixed_ref.shape[1]
    for t in range(count):
        place = index_ref[t]
        seg = refs[t][events : events + EXTRA, 0:events].astype(F32)[0:8]
        segr_ref[place] = seg
        segc_ref[place] = jnp.broadcast_to(jnp.transpose(seg)[:, 0:1], segc_ref.shape[1:])
    copy.wait()
    for t in range(count):
        mixed_ref[index_ref[t]] = dot_nt(refs[t][0:events, :], w_out_ref[...])


def places_kernel(slots_ref, asked_ref, spread_ref, chosen_ref):
    slot = iota(spread_ref.shape, 0)
    hit = slot == slots_ref[0:1, :]
    for k in range(1, NIDS):
        hit = hit | (slot == slots_ref[k : k + 1, :])
    spread_ref[...] = jnp.where(hit, 1.0, 0.0).astype(BF16)
    owners, capacity = asked_ref.shape
    slots = owners * capacity
    high, low = split_exact(asked_ref[...])
    place = jnp.where(
        iota((capacity, slots), 1) % capacity == iota((capacity, slots), 0), 1.0, 0.0
    ).astype(BF16)
    values = 16.0 * dot(high, place) + dot(low, place)
    mine = iota((owners, slots), 1) // capacity == iota((owners, slots), 0)
    asked = jnp.sum(jnp.where(mine, values, 0.0), 0, keepdims=True).astype(jnp.int32)
    chosen_ref[...] = jnp.where(iota(chosen_ref.shape, 0) == asked, 1.0, 0.0).astype(BF16)


HIDDEN = -1e4


def bent(raw, mask):
    half = jnp.where(mask, raw * (0.5 * SCALE), HIDDEN)
    raised = (1.0 + jnp.tanh(half)).astype(BF16)
    half = half.astype(BF16)
    one, two = BF16(1.0), BF16(2.0)
    return half * raised, raised * (one + half * (two - raised))


def by_twos(start, stop, work):
    twos = (stop - start) // 2

    def step(k, _):
        work([start + 2 * k, start + 2 * k + 1])
        return 0

    lax.fori_loop(0, twos, step, 0)

    @pl.when(stop - start > 2 * twos)
    def _():
        work([stop - 1])


def pipelined(numbers, mask_of, scores, finish):
    masks = {}
    items = [(n, h) for n in range(len(numbers)) for h in range(HEADS)]
    ready = scores(numbers[0], 0)
    for at, (n, h) in enumerate(items):
        now = ready
        if at + 1 < len(items):
            later, later_head = items[at + 1]
            ready = scores(numbers[later], later_head)
        if n not in masks:
            masks[n] = mask_of(numbers[n])
        finish(numbers[n], h, now, masks[n])


class Chunks:
    def __init__(self, proj_ref, gatt_ref, segc_ref, segr_ref, join_ref):
        self.proj, self.gatt = proj_ref, gatt_ref
        self.segc, self.segr, self.join = segc_ref, segr_ref, join_ref
        self.width = gatt_ref.shape[2]

    def cut(self, chunk, part, h):
        return self.proj[chunk, :, head(part, h, self.width)]

    def attend(self, i, start, stop, att_ref):
        def scores(j, h):
            return dot_nt(self.cut(i, 2, h), self.cut(j, 3, h))

        def finish(j, h, raw, mask):
            half = jnp.where(mask, raw * (0.5 * SCALE), HIDDEN)
            weights = (half + half * jnp.tanh(half)).astype(BF16)
            att_ref[:, head(0, h, self.width)] += dot(weights, self.cut(j, 1, h))

        def mask_of(j):
            return visible(i, j, self.segc, self.segr, False)

        by_twos(start, stop, lambda js: pipelined(js, mask_of, scores, finish))

    def finish(self, i, own, att, grad_mixed, emb_ref, w_out_ref, out_ref):
        att_norm, att_inverse = normalize(att)
        gate = self.proj[i, :, 0 : self.width].astype(F32)
        grad_att = norm_back(grad_mixed * gate, att_norm, att_inverse)
        self.gatt[i] = grad_att.astype(BF16)

        @pl.when(i == own)
        def _():
            mixed = (att_norm * gate).astype(BF16)
            out = emb_ref[...].astype(F32) + dot(mixed, w_out_ref[...])
            out_ref[...] = out.astype(BF16)
            self.join[:, 0 : self.width] = grad_mixed * att_norm

    def query_side(self, own, start, stop):
        def scores(j, h):
            grad_att = self.gatt[own, :, head(0, h, self.width)]
            return (
                dot_nt(self.cut(own, 2, h), self.cut(j, 3, h)),
                dot_nt(grad_att, self.cut(j, 1, h)),
            )

        def finish(j, h, pair, mask):
            raw, grad_weights = pair
            _, slope = bent(raw, mask)
            grad_raw = grad_weights.astype(BF16) * slope
            self.join[:, head(2, h, self.width)] += dot(grad_raw, self.cut(j, 3, h))

        def mask_of(j):
            return visible(own, j, self.segc, self.segr, False)

        by_twos(start, stop, lambda js: pipelined(js, mask_of, scores, finish))

    def key_side(self, own, start, stop):
        def scores(i, h):
            grad_att = self.gatt[i, :, head(0, h, self.width)]
            return (
                dot_nt(self.cut(own, 3, h), self.cut(i, 2, h)),
                dot_nt(self.cut(own, 1, h), grad_att),
            )

        def finish(i, h, pair, mask):
            raw, grad_weights = pair
            value, slope = bent(raw, mask)
            grad_raw = grad_weights.astype(BF16) * slope
            self.join[:, head(3, h, self.width)] += dot(grad_raw, self.cut(i, 2, h))
            grad_att = self.gatt[i, :, head(0, h, self.width)]
            self.join[:, head(1, h, self.width)] += dot(value, grad_att)

        def mask_of(i):
            return visible(i, own, self.segc, self.segr, True)

        by_twos(start, stop, lambda chunks: pipelined(chunks, mask_of, scores, finish))


def early_kernel(index_ref, emb_ref, mate_ref, *refs):
    w_in_in, w_out_in, mixed_in, segc_in, segr_in, spread_in, side_in = refs[:7]
    proj_ref, att_ref, gatt_ref, join_ref, slope_ref, out_ref = refs[7:13]
    w_in_ref, w_out_ref, mixed_ref, segc_ref, segr_ref, spread_ref, side_ref, sems = refs[13:]
    pairs = [(segc_in, segc_ref), (segr_in, segr_ref), (mixed_in, mixed_ref)]
    pairs += [(w_out_in, w_out_ref), (spread_in, spread_ref), (side_in, side_ref)]
    pairs += [(w_in_in, w_in_ref)]
    copies = start_copies(pairs, sems)
    own = index_ref[0]
    mate = index_ref[1]
    base = jnp.minimum(own, mate)
    last = jnp.maximum(own, mate)

    def write_to(place):
        def write(columns, value):
            proj_ref[place - base, :, columns] = value

        return write

    project(emb_ref[...], w_in_in, write_to(own), slope_ref)
    project(mate_ref[...], w_in_in, write_to(mate), None)
    for copy in copies:
        copy.wait()
    att_ref[...] = jnp.zeros_like(att_ref)
    join_ref[...] = jnp.zeros_like(join_ref)
    pair_rows = pl.ds(base, 2)
    chunks = Chunks(
        proj_ref, gatt_ref, segc_ref.at[pair_rows], segr_ref.at[pair_rows], join_ref
    )

    def forward(i, _):
        chunks.attend(i, 0, i + 1, att_ref.at[i])
        return 0

    lax.fori_loop(own - base, last - base + 1, forward, 0)

    @pl.when(base == 0)
    def _():
        def finish(i, _):
            chunks.finish(i, own, att_ref[i], mixed_ref[i], emb_ref, w_out_ref, out_ref)
            return 0

        lax.fori_loop(own, last + 1, finish, 0)
        chunks.query_side(own, 0, own + 1)
        chunks.key_side(own, own, last + 1)


def project_kernel(emb_ref, w_in_ref, proj_ref):
    def write(columns, value):
        proj_ref[:, columns] = value

    project(emb_ref[...], w_in_ref, write, None)


def late_kernel(count, *refs):
    index_ref = refs[0]
    emb_refs = refs[1 : 1 + count]
    proj_far_ref = refs[1 + count]
    (
        proj_pair_ref,
        att_pair_ref,
        gatt_pair_ref,
        join_early_ref,
        slope_ref,
        out_early_ref,
        w_in_ref,
        w_out_ref,
        mixed_ref,
        segc_ref,
        segr_ref,
        spread_ref,
        side_ref,
        out_ref,
        grad_ref,
        proj_ref,
        att_ref,
        gatt_ref,
        join_ref,
        sems,
    ) = refs[2 + count :]
    own = index_ref[0]
    base = jnp.minimum(own, index_ref[1])
    last = jnp.maximum(own, index_ref[1])
    closed = base == 0

    pair_rows = pl.ds(base, 2)
    copies = start_copies(
        (
            (join_early_ref, join_ref),
            (proj_pair_ref, proj_ref.at[pair_rows]),
            (gatt_pair_ref, gatt_ref.at[pair_rows]),
            (proj_far_ref, proj_ref.at[index_ref[count // 2]]),
        ),
        sems,
    )

    def write_to(place):
        def write(columns, value):
            proj_ref[place, :, columns] = value

        return write

    for t in range(2, count):
        if t == count // 2:
            continue
        project(emb_refs[t][...], w_in_ref, write_to(index_ref[t]), None)
    for copy in copies:
        copy.wait()
    chunks = Chunks(proj_ref, gatt_ref, segc_ref, segr_ref, join_ref)

    @pl.when(closed)
    def _():
        out_ref[...] = out_early_ref[...]

    def forward(i, _):
        begun = i <= last

        @pl.when(begun)
        def _():
            att_ref[...] = att_pair_ref[jnp.minimum(i - base, 1)]

        @pl.when(jnp.logical_not(begun))
        def _():
            att_ref[...] = jnp.zeros_like(att_ref)

        chunks.attend(i, 0, jnp.where(begun, base, i + 1), att_ref)
        chunks.finish(i, own, att_ref[...], mixed_ref[i], emb_refs[0], w_out_ref, out_ref)
        return 0

    lax.fori_loop(jnp.where(closed, last + 1, own), count, forward, 0)
    chunks.query_side(own, jnp.where(closed, own + 1, 0), own + 1)
    chunks.key_side(own, jnp.where(closed, last + 1, own), count)

    width = gatt_ref.shape[2]
    grad_normed = None
    for block in range(4):
        columns = slice(block * width, (block + 1) * width)
        joined = join_ref[:, columns] * slope_ref[:, columns]
        if block >= 2:
            joined = joined * (0.5 * SCALE)
        part = dot_nt(joined.astype(BF16), w_in_ref[:, columns])
        grad_normed = part if block == 0 else grad_normed + part
    normed, inverse = normalize(emb_refs[0][...].astype(F32))
    grad = norm_back(grad_normed, normed, inverse) + side_ref[0 : emb_refs[0].shape[0], :].astype(F32)
    grad_ref[...] = dot(spread_ref[...], grad.astype(BF16)).astype(BF16)


def in_hbm(*arrays):
    return [pltpu.with_memory_space_constraint(a, pltpu.HBM) for a in arrays]


def params(mebibytes=12):
    return pltpu.CompilerParams(vmem_limit_bytes=mebibytes * 1024 * 1024)


def flip(value, axis, offset):
    count = lax.axis_size(axis)
    return lax.ppermute(value, axis, [(i, i ^ offset) for i in range(count)])


def gather_blocks(value, axis, known):
    bit = lax.axis_size(axis)
    blocks = {0: value}
    while bit > 1:
        bit //= 2
        for t in list(blocks):
            blocks[t | bit] = known.get(t | bit)
            if blocks[t | bit] is None:
                blocks[t | bit] = flip(blocks[t], axis, bit)
    return [blocks[t] for t in range(lax.axis_size(axis))]


def after(value, earlier):
    return lax.optimization_barrier((value, earlier))[0]


def local(table, item_owner, item_row, segment_ids, w_in, w_out, cotangent):
    owners = lax.axis_size("table") * lax.axis_size("ctx")
    count = lax.axis_size("ctx")
    events, width = cotangent.shape
    id_count = events * NIDS
    capacity = 2 * ((id_count + owners - 1) // owners)
    slot_count = owners * capacity
    axes = ("table", "ctx")
    vmem = pl.BlockSpec(memory_space=pltpu.VMEM)
    smem = pl.BlockSpec(memory_space=pltpu.SMEM)

    def exchange(value):
        return lax.all_to_all(value, axes, split_axis=0, concat_axis=0, tiled=True)

    hbm = pl.BlockSpec(memory_space=pltpu.HBM)
    slots, wanted, side = pl.pallas_call(
        functools.partial(slots_kernel, capacity),
        out_shape=(
            jax.ShapeDtypeStruct((8, events), jnp.int32),
            jax.ShapeDtypeStruct((owners, capacity), jnp.int32),
            jax.ShapeDtypeStruct((events + EXTRA, width), BF16),
        ),
        in_specs=[hbm] * 4,
        out_specs=(vmem, vmem, vmem),
        scratch_shapes=[
            pltpu.VMEM((NIDS, events), jnp.int32),
            pltpu.VMEM((NIDS, events), jnp.int32),
            pltpu.VMEM((1, events), jnp.int32),
            pltpu.SemaphoreType.DMA((4,)),
        ],
        compiler_params=params(),
        name="slots",
    )(*in_hbm(item_owner.T, item_row.T, segment_ids.reshape(1, events), cotangent))
    asked = exchange(wanted)
    rows = pl.pallas_call(
        select_kernel,
        out_shape=pltpu.HBM((slot_count, width), BF16),
        in_specs=[vmem, hbm],
        out_specs=hbm,
        scratch_shapes=[
            pltpu.VMEM(table.shape, BF16),
            pltpu.VMEM((slot_count, width), BF16),
            pltpu.SemaphoreType.DMA((5,)),
        ],
        compiler_params=params(),
        name="select",
    )(asked, *in_hbm(table))
    fetched = exchange(rows.reshape(owners, capacity, width)).reshape(slot_count, width)
    side_far = flip(side, "ctx", count // 2)
    side_mate = flip(side, "ctx", 1)
    side_blocks = gather_blocks(side, "ctx", {1: side_mate, count // 2: after(side_far, rows)})
    index = lax.axis_index("ctx").astype(jnp.int32) ^ jnp.arange(count, dtype=jnp.int32)
    prep_shapes = (
        jax.ShapeDtypeStruct((count, events, width), F32),
        jax.ShapeDtypeStruct((count, events, 128), F32),
        jax.ShapeDtypeStruct((count, 8, events), F32),
        jax.ShapeDtypeStruct((slot_count, events), BF16),
    )
    pinned = [pltpu.HBM(a.shape, a.dtype) for a in prep_shapes]
    spread, chosen = pl.pallas_call(
        places_kernel,
        out_shape=(pinned[3], pltpu.HBM((table.shape[0], slot_count), BF16)),
        in_specs=[vmem, vmem],
        out_specs=(vmem, vmem),
        compiler_params=params(),
        name="places",
    )(slots, after(asked, rows))
    prepared = pl.pallas_call(
        functools.partial(prep_kernel, count),
        out_shape=tuple(pinned[:3]),
        in_specs=[smem, hbm] + [vmem] * count,
        out_specs=(vmem,) * 3,
        scratch_shapes=[pltpu.VMEM(w_out.shape, BF16), pltpu.SemaphoreType.DMA((1,))],
        compiler_params=params(20),
        name="prep",
    )(index, *in_hbm(w_out), *side_blocks)
    prepared = in_hbm(*prepared, spread)
    fetched, prepared = lax.optimization_barrier((fetched, prepared))
    embedded = pl.pallas_call(
        embed_kernel,
        out_shape=jax.ShapeDtypeStruct((events, width), BF16),
        compiler_params=params(),
        name="embed",
    )(slots, fetched)
    emb_far = flip(embedded, "ctx", count // 2)
    emb_mate = flip(embedded, "ctx", 1)
    event_shape = jax.ShapeDtypeStruct((events, width), BF16)
    early = pl.pallas_call(
        early_kernel,
        out_shape=(
            jax.ShapeDtypeStruct((2, events, 4 * width), BF16),
            jax.ShapeDtypeStruct((2, events, width), F32),
            jax.ShapeDtypeStruct((2, events, width), BF16),
            jax.ShapeDtypeStruct((events, 4 * width), F32),
            jax.ShapeDtypeStruct((events, 4 * width), F32),
            event_shape,
        )
        + tuple(jax.ShapeDtypeStruct(a.shape, BF16) for a in (w_in, w_out))
        + prep_shapes
        + (jax.ShapeDtypeStruct(side.shape, BF16),),
        in_specs=[smem, vmem, vmem, vmem] + [hbm] * 6,
        out_specs=(vmem,) * 13,
        scratch_shapes=[pltpu.SemaphoreType.DMA((7,))],
        compiler_params=params(20),
        name="early",
    )(index, embedded, emb_mate, w_in, *in_hbm(w_out), *prepared, *in_hbm(side))
    emb_far = after(emb_far, early[0])
    proj_far = pl.pallas_call(
        project_kernel,
        out_shape=jax.ShapeDtypeStruct((events, 4 * width), BF16),
        compiler_params=params(),
        name="project_far",
    )(emb_far, early[6])
    emb_blocks = gather_blocks(embedded, "ctx", {1: emb_mate, count // 2: emb_far})
    layer_out, slot_grad = pl.pallas_call(
        functools.partial(late_kernel, count),
        out_shape=(event_shape, jax.ShapeDtypeStruct((slot_count, width), BF16)),
        in_specs=[smem] + [vmem] * (14 + count),
        out_specs=(vmem, vmem),
        scratch_shapes=[
            pltpu.VMEM((count, events, 4 * width), BF16),
            pltpu.VMEM((events, width), F32),
            pltpu.VMEM((count, events, width), BF16),
            pltpu.VMEM((events, 4 * width), F32),
            pltpu.SemaphoreType.DMA((4,)),
        ],
        compiler_params=params(28),
        name="late",
    )(index, *emb_blocks, proj_far, *early)
    returned = exchange(slot_grad.reshape(owners, capacity, width)).reshape(slot_count, width)
    row_grad = pl.pallas_call(
        collect_kernel,
        out_shape=pltpu.HBM(table.shape, F32),
        in_specs=[vmem, vmem],
        out_specs=hbm,
        scratch_shapes=[pltpu.VMEM(table.shape, F32), pltpu.SemaphoreType.DMA((4,))],
        compiler_params=params(),
        name="collect",
    )(chosen, returned)
    return layer_out, row_grad


def solution(mesh):
    rows = P(("table", "ctx"), None)
    return jax.shard_map(
        local,
        mesh=mesh,
        in_specs=(rows, rows, rows, P("table", "ctx"), P(), P(), rows),
        out_specs=(rows, rows),
        check_vma=False,
    )
```

```python
import functools

import jax
import jax.numpy as jnp
from jax import lax
from jax.experimental import pallas as pl
from jax.experimental.pallas import tpu as pltpu
from jax.sharding import PartitionSpec as P

HEADS = 4
HEAD_DIM = 128
NIDS = 2
EPS = 1e-06

F32 = jnp.float32
BF16 = jnp.bfloat16


def dot(a, b):
    return jnp.dot(a, b, preferred_element_type=F32)


def dot_nt(a, b):
    return lax.dot_general(a, b, (((1,), (1,)), ((), ())), preferred_element_type=F32)


def iota(shape, dim):
    return lax.broadcasted_iota(jnp.int32, shape, dim)


def normalize(values):
    centred = values - jnp.mean(values, -1, keepdims=True)
    inverse = lax.rsqrt(jnp.mean(centred * centred, -1, keepdims=True) + EPS)
    return centred * inverse, inverse


def norm_back(grad_norm, normed, inverse):
    mean_grad = jnp.mean(grad_norm, -1, keepdims=True)
    mean_cross = jnp.mean(grad_norm * normed, -1, keepdims=True)
    return (grad_norm - mean_grad - normed * mean_cross) * inverse


def split_exact(values):
    return (values >> 4).astype(F32).astype(BF16), (values & 15).astype(F32).astype(BF16)


def start_copies(pairs, sems):
    copies = [pltpu.make_async_copy(a, b, sems.at[i]) for i, (a, b) in enumerate(pairs)]
    for copy in copies:
        copy.start()
    return copies


EXTRA = 16


def slots_kernel(
    capacity,
    owner_in,
    row_in,
    seg_in,
    cot_in,
    slots_ref,
    wanted_ref,
    side_ref,
    owner_ref,
    row_ref,
    seg_ref,
    sems,
):
    events, width = cot_in.shape
    pairs = (
        (owner_in, owner_ref),
        (row_in, row_ref),
        (seg_in, seg_ref),
        (cot_in, side_ref.at[0:events]),
    )
    copies = start_copies(pairs, sems)
    for copy in copies[:3]:
        copy.wait()
    side_ref[events:, :] = jnp.zeros((EXTRA, width), BF16)
    segments = jnp.broadcast_to(seg_ref[...].astype(F32), (EXTRA, events))
    side_ref[events:, 0:events] = segments.astype(BF16)
    owners = wanted_ref.shape[0]
    owner = jnp.concatenate([owner_ref[k : k + 1, :] for k in range(NIDS)], 1)
    row = jnp.concatenate([row_ref[k : k + 1, :] for k in range(NIDS)], 1)
    ids = owner.shape[1]
    named = iota((owners, ids), 0) == owner
    named_f = jnp.where(named, 1.0, 0.0)
    before = jnp.where(iota((ids, ids), 0) < iota((ids, ids), 1), 1.0, 0.0).astype(BF16)
    earlier = dot(named_f.astype(BF16), before)
    rank = jnp.sum(earlier * named_f, 0, keepdims=True).astype(jnp.int32)
    slot = owner * capacity + rank
    slots_ref[...] = jnp.full(slots_ref.shape, -1, jnp.int32)
    for k in range(NIDS):
        slots_ref[k : k + 1, :] = slot[:, k * events : (k + 1) * events]
    ranked = jnp.where(iota((capacity, ids), 0) == rank, 1.0, 0.0).astype(BF16)
    high, low = (row >> 4).astype(F32), (row & 15).astype(F32)
    wanted = 16.0 * dot_nt((named_f * high).astype(BF16), ranked) + dot_nt(
        (named_f * low).astype(BF16), ranked
    )
    wanted_ref[...] = wanted.astype(jnp.int32)
    for copy in copies[3:]:
        copy.wait()


def select_kernel(asked_ref, table_in, out_ref, table_ref, rows_ref, sems):
    (table_copy,) = start_copies(((table_in, table_ref),), sems)
    owners, capacity = asked_ref.shape
    rows = table_ref.shape[0]
    parts = sems.shape[0] - 1
    step = owners // parts
    columns = jnp.transpose(asked_ref[...])
    lane = iota((capacity, rows), 1)
    chosen = []
    for part in range(parts):
        sources = range(part * step, (part + 1) * step)
        hits = [jnp.where(lane == columns[:, s : s + 1], 1.0, 0.0) for s in sources]
        chosen.append(jnp.concatenate(hits, 0).astype(BF16))
    table_copy.wait()
    copies = []
    for part in range(parts):
        place = pl.ds(part * step * capacity, step * capacity)
        rows_ref[place, :] = dot(chosen[part], table_ref[...]).astype(BF16)
        copy = pltpu.make_async_copy(rows_ref.at[place], out_ref.at[place], sems.at[1 + part])
        copy.start()
        copies.append(copy)
    for copy in copies:
        copy.wait()


def embed_kernel(slots_ref, fetched_ref, out_ref):
    events = out_ref.shape[0]
    slots = fetched_ref.shape[0]
    column = jnp.transpose(slots_ref[...])
    lane = iota((events, slots), 1)
    hit = lane == column[:, 0:1]
    for k in range(1, NIDS):
        hit = hit | (lane == column[:, k : k + 1])
    picked = jnp.where(hit, 1.0, 0.0).astype(BF16)
    out_ref[...] = dot(picked, fetched_ref[...]).astype(BF16)


def collect_kernel(chosen_ref, returned_ref, out_ref, rows_ref, sems):
    parts = sems.shape[0]
    step = rows_ref.shape[1] // parts
    copies = []
    for part in range(parts):
        place = pl.ds(part * step, step)
        rows_ref[:, place] = dot(chosen_ref[...], returned_ref[:, place])
        copy = pltpu.make_async_copy(rows_ref.at[:, place], out_ref.at[:, place], sems.at[part])
        copy.start()
        copies.append(copy)
    for copy in copies:
        copy.wait()


SCALE = HEAD_DIM ** (-0.5)


def head(part, h, width):
    return slice(part * width + h * HEAD_DIM, part * width + (h + 1) * HEAD_DIM)


def visible(query_chunk, key_chunk, segc_ref, segr_ref, flip):
    events = segr_ref.shape[2]
    first, second = iota((events, events), 0), iota((events, events), 1)
    if flip:
        same = segc_ref[key_chunk][:, 0:1] == segr_ref[query_chunk][0:1, :]
        return same & (first <= second + (query_chunk - key_chunk) * events)
    same = segc_ref[query_chunk][:, 0:1] == segr_ref[key_chunk][0:1, :]
    return same & (first + (query_chunk - key_chunk) * events >= second)


def project(emb, w_in_ref, write, slope_ref):
    width = emb.shape[1]
    normed = (0.5 * normalize(emb.astype(F32))[0]).astype(BF16)
    for block in range(4):
        columns = slice(block * width, (block + 1) * width)
        half = dot(normed, w_in_ref[:, columns])
        bend = jnp.tanh(half)
        value = half + half * bend
        kept = value * (0.5 * SCALE) if block == 2 else value
        write(columns, kept.astype(BF16))
        if slope_ref is not None:
            sigma = 0.5 + 0.5 * bend
            slope_ref[:, columns] = sigma + value - value * sigma


def prep_kernel(count, index_ref, w_out_in, *refs):
    mixed_ref, segc_ref, segr_ref, w_out_ref, sems = refs[count:]
    (copy,) = start_copies(((w_out_in, w_out_ref),), sems)
    events = mixed_ref.shape[1]
    for t in range(count):
        place = index_ref[t]
        seg = refs[t][events : events + EXTRA, 0:events].astype(F32)[0:8]
        segr_ref[place] = seg
        segc_ref[place] = jnp.broadcast_to(jnp.transpose(seg)[:, 0:1], segc_ref.shape[1:])
    copy.wait()
    for t in range(count):
        mixed_ref[index_ref[t]] = dot_nt(refs[t][0:events, :], w_out_ref[...])


def places_kernel(slots_ref, asked_ref, spread_ref, chosen_ref):
    slot = iota(spread_ref.shape, 0)
    hit = slot == slots_ref[0:1, :]
    for k in range(1, NIDS):
        hit = hit | (slot == slots_ref[k : k + 1, :])
    spread_ref[...] = jnp.where(hit, 1.0, 0.0).astype(BF16)
    owners, capacity = asked_ref.shape
    slots = owners * capacity
    high, low = split_exact(asked_ref[...])
    place = jnp.where(
        iota((capacity, slots), 1) % capacity == iota((capacity, slots), 0), 1.0, 0.0
    ).astype(BF16)
    values = 16.0 * dot(high, place) + dot(low, place)
    mine = iota((owners, slots), 1) // capacity == iota((owners, slots), 0)
    asked = jnp.sum(jnp.where(mine, values, 0.0), 0, keepdims=True).astype(jnp.int32)
    chosen_ref[...] = jnp.where(iota(chosen_ref.shape, 0) == asked, 1.0, 0.0).astype(BF16)


HIDDEN = -1e4


def bent(raw, mask):
    half = jnp.where(mask, raw, HIDDEN)
    raised = (1.0 + jnp.tanh(half)).astype(BF16)
    half = half.astype(BF16)
    one, two = BF16(1.0), BF16(2.0)
    return half * raised, raised * (one + half * (two - raised))


def by_twos(start, stop, work):
    twos = (stop - start) // 2

    def step(k, _):
        work([start + 2 * k, start + 2 * k + 1])
        return 0

    lax.fori_loop(0, twos, step, 0)

    @pl.when(stop - start > 2 * twos)
    def _():
        work([stop - 1])


def pipelined(numbers, mask_of, scores, finish):
    masks = {}
    items = [(n, h) for n in range(len(numbers)) for h in range(HEADS)]
    ready = scores(numbers[0], 0)
    for at, (n, h) in enumerate(items):
        now = ready
        if at + 1 < len(items):
            later, later_head = items[at + 1]
            ready = scores(numbers[later], later_head)
        if n not in masks:
            masks[n] = mask_of(numbers[n])
        finish(numbers[n], h, now, masks[n])


class Chunks:
    def __init__(self, proj_ref, gatt_ref, segc_ref, segr_ref, join_ref):
        self.proj, self.gatt = proj_ref, gatt_ref
        self.segc, self.segr, self.join = segc_ref, segr_ref, join_ref
        self.width = gatt_ref.shape[2]

    def cut(self, chunk, part, h):
        return self.proj[chunk, :, head(part, h, self.width)]

    def attend(self, i, start, stop, att_ref):
        def scores(j, h):
            return dot_nt(self.cut(i, 2, h), self.cut(j, 3, h))

        def finish(j, h, raw, mask):
            half = jnp.where(mask, raw, HIDDEN)
            weights = (half + half * jnp.tanh(half)).astype(BF16)
            att_ref[:, head(0, h, self.width)] += dot(weights, self.cut(j, 1, h))

        def mask_of(j):
            return visible(i, j, self.segc, self.segr, False)

        by_twos(start, stop, lambda js: pipelined(js, mask_of, scores, finish))

    def finish(self, i, own, att, grad_mixed, emb_ref, w_out_ref, out_ref):
        att_norm, att_inverse = normalize(att)
        gate = self.proj[i, :, 0 : self.width].astype(F32)
        grad_att = norm_back(grad_mixed * gate, att_norm, att_inverse)
        self.gatt[i] = grad_att.astype(BF16)

        @pl.when(i == own)
        def _():
            mixed = (att_norm * gate).astype(BF16)
            out = emb_ref[...].astype(F32) + dot(mixed, w_out_ref[...])
            out_ref[...] = out.astype(BF16)
            self.join[:, 0 : self.width] = grad_mixed * att_norm

    def query_side(self, own, start, stop):
        def scores(j, h):
            grad_att = self.gatt[own, :, head(0, h, self.width)]
            return (
                dot_nt(self.cut(own, 2, h), self.cut(j, 3, h)),
                dot_nt(grad_att, self.cut(j, 1, h)),
            )

        def finish(j, h, pair, mask):
            raw, grad_weights = pair
            _, slope = bent(raw, mask)
            grad_raw = grad_weights.astype(BF16) * slope
            self.join[:, head(2, h, self.width)] += dot(grad_raw, self.cut(j, 3, h))

        def mask_of(j):
            return visible(own, j, self.segc, self.segr, False)

        by_twos(start, stop, lambda js: pipelined(js, mask_of, scores, finish))

    def key_side(self, own, start, stop):
        def scores(i, h):
            grad_att = self.gatt[i, :, head(0, h, self.width)]
            return (
                dot_nt(self.cut(own, 3, h), self.cut(i, 2, h)),
                dot_nt(self.cut(own, 1, h), grad_att),
            )

        def finish(i, h, pair, mask):
            raw, grad_weights = pair
            value, slope = bent(raw, mask)
            grad_raw = grad_weights.astype(BF16) * slope
            self.join[:, head(3, h, self.width)] += dot(grad_raw, self.cut(i, 2, h))
            grad_att = self.gatt[i, :, head(0, h, self.width)]
            self.join[:, head(1, h, self.width)] += dot(value, grad_att)

        def mask_of(i):
            return visible(i, own, self.segc, self.segr, True)

        by_twos(start, stop, lambda chunks: pipelined(chunks, mask_of, scores, finish))


def early_kernel(index_ref, emb_ref, mate_ref, *refs):
    w_in_in, w_out_in, mixed_in, segc_in, segr_in, spread_in, side_in = refs[:7]
    proj_ref, att_ref, gatt_ref, join_ref, slope_ref, out_ref = refs[7:13]
    w_in_ref, w_out_ref, mixed_ref, segc_ref, segr_ref, spread_ref, side_ref, sems = refs[13:]
    pairs = [(segc_in, segc_ref), (segr_in, segr_ref), (mixed_in, mixed_ref)]
    pairs += [(w_out_in, w_out_ref), (spread_in, spread_ref), (side_in, side_ref)]
    pairs += [(w_in_in, w_in_ref)]
    copies = start_copies(pairs, sems)
    own = index_ref[0]
    mate = index_ref[1]
    base = jnp.minimum(own, mate)
    last = jnp.maximum(own, mate)

    def write_to(place):
        def write(columns, value):
            proj_ref[place - base, :, columns] = value

        return write

    project(emb_ref[...], w_in_in, write_to(own), slope_ref)
    project(mate_ref[...], w_in_in, write_to(mate), None)
    for copy in copies:
        copy.wait()
    att_ref[...] = jnp.zeros_like(att_ref)
    join_ref[...] = jnp.zeros_like(join_ref)
    pair_rows = pl.ds(base, 2)
    chunks = Chunks(
        proj_ref, gatt_ref, segc_ref.at[pair_rows], segr_ref.at[pair_rows], join_ref
    )

    def forward(i, _):
        chunks.attend(i, 0, i + 1, att_ref.at[i])
        return 0

    lax.fori_loop(own - base, last - base + 1, forward, 0)

    @pl.when(base == 0)
    def _():
        def finish(i, _):
            chunks.finish(i, own, att_ref[i], mixed_ref[i], emb_ref, w_out_ref, out_ref)
            return 0

        lax.fori_loop(own, last + 1, finish, 0)
        chunks.query_side(own, 0, own + 1)
        chunks.key_side(own, own, last + 1)


def project_kernel(emb_ref, w_in_ref, proj_ref):
    def write(columns, value):
        proj_ref[:, columns] = value

    project(emb_ref[...], w_in_ref, write, None)


def late_kernel(count, *refs):
    index_ref = refs[0]
    emb_refs = refs[1 : 1 + count]
    proj_far_ref = refs[1 + count]
    (
        proj_pair_ref,
        att_pair_ref,
        gatt_pair_ref,
        join_early_ref,
        slope_ref,
        out_early_ref,
        w_in_ref,
        w_out_ref,
        mixed_ref,
        segc_ref,
        segr_ref,
        spread_ref,
        side_ref,
        out_ref,
        grad_ref,
        proj_ref,
        att_ref,
        gatt_ref,
        join_ref,
        sems,
    ) = refs[2 + count :]
    own = index_ref[0]
    base = jnp.minimum(own, index_ref[1])
    last = jnp.maximum(own, index_ref[1])
    closed = base == 0

    pair_rows = pl.ds(base, 2)
    copies = start_copies(
        (
            (join_early_ref, join_ref),
            (proj_pair_ref, proj_ref.at[pair_rows]),
            (gatt_pair_ref, gatt_ref.at[pair_rows]),
            (proj_far_ref, proj_ref.at[index_ref[count // 2]]),
        ),
        sems,
    )

    def write_to(place):
        def write(columns, value):
            proj_ref[place, :, columns] = value

        return write

    for t in range(2, count):
        if t == count // 2:
            continue
        project(emb_refs[t][...], w_in_ref, write_to(index_ref[t]), None)
    for copy in copies:
        copy.wait()
    chunks = Chunks(proj_ref, gatt_ref, segc_ref, segr_ref, join_ref)

    @pl.when(closed)
    def _():
        out_ref[...] = out_early_ref[...]

    def forward(i, _):
        begun = i <= last

        @pl.when(begun)
        def _():
            att_ref[...] = att_pair_ref[jnp.minimum(i - base, 1)]

        @pl.when(jnp.logical_not(begun))
        def _():
            att_ref[...] = jnp.zeros_like(att_ref)

        chunks.attend(i, 0, jnp.where(begun, base, i + 1), att_ref)
        chunks.finish(i, own, att_ref[...], mixed_ref[i], emb_refs[0], w_out_ref, out_ref)
        return 0

    lax.fori_loop(jnp.where(closed, last + 1, own), count, forward, 0)
    chunks.query_side(own, jnp.where(closed, own + 1, 0), own + 1)
    chunks.key_side(own, jnp.where(closed, last + 1, own), count)

    width = gatt_ref.shape[2]
    grad_normed = None
    for block in range(4):
        columns = slice(block * width, (block + 1) * width)
        joined = join_ref[:, columns] * slope_ref[:, columns]
        if block == 2:
            joined = joined * (0.5 * SCALE)
        part = dot_nt(joined.astype(BF16), w_in_ref[:, columns])
        grad_normed = part if block == 0 else grad_normed + part
    normed, inverse = normalize(emb_refs[0][...].astype(F32))
    grad = norm_back(grad_normed, normed, inverse) + side_ref[0 : emb_refs[0].shape[0], :].astype(F32)
    grad_ref[...] = dot(spread_ref[...], grad.astype(BF16)).astype(BF16)


def in_hbm(*arrays):
    return [pltpu.with_memory_space_constraint(a, pltpu.HBM) for a in arrays]


def params(mebibytes=12):
    return pltpu.CompilerParams(vmem_limit_bytes=mebibytes * 1024 * 1024)


def flip(value, axis, offset):
    count = lax.axis_size(axis)
    return lax.ppermute(value, axis, [(i, i ^ offset) for i in range(count)])


def gather_blocks(value, axis, known):
    bit = lax.axis_size(axis)
    blocks = {0: value}
    while bit > 1:
        bit //= 2
        for t in list(blocks):
            blocks[t | bit] = known.get(t | bit)
            if blocks[t | bit] is None:
                blocks[t | bit] = flip(blocks[t], axis, bit)
    return [blocks[t] for t in range(lax.axis_size(axis))]


def after(value, earlier):
    return lax.optimization_barrier((value, earlier))[0]


def local(table, item_owner, item_row, segment_ids, w_in, w_out, cotangent):
    owners = lax.axis_size("table") * lax.axis_size("ctx")
    count = lax.axis_size("ctx")
    events, width = cotangent.shape
    id_count = events * NIDS
    capacity = 2 * ((id_count + owners - 1) // owners)
    slot_count = owners * capacity
    axes = ("table", "ctx")
    vmem = pl.BlockSpec(memory_space=pltpu.VMEM)
    smem = pl.BlockSpec(memory_space=pltpu.SMEM)

    def exchange(value):
        return lax.all_to_all(value, axes, split_axis=0, concat_axis=0, tiled=True)

    hbm = pl.BlockSpec(memory_space=pltpu.HBM)
    slots, wanted, side = pl.pallas_call(
        functools.partial(slots_kernel, capacity),
        out_shape=(
            jax.ShapeDtypeStruct((8, events), jnp.int32),
            jax.ShapeDtypeStruct((owners, capacity), jnp.int32),
            jax.ShapeDtypeStruct((events + EXTRA, width), BF16),
        ),
        in_specs=[hbm] * 4,
        out_specs=(vmem, vmem, vmem),
        scratch_shapes=[
            pltpu.VMEM((NIDS, events), jnp.int32),
            pltpu.VMEM((NIDS, events), jnp.int32),
            pltpu.VMEM((1, events), jnp.int32),
            pltpu.SemaphoreType.DMA((4,)),
        ],
        compiler_params=params(),
        name="slots",
    )(*in_hbm(item_owner.T, item_row.T, segment_ids.reshape(1, events), cotangent))
    asked = exchange(wanted)
    rows = pl.pallas_call(
        select_kernel,
        out_shape=pltpu.HBM((slot_count, width), BF16),
        in_specs=[vmem, hbm],
        out_specs=hbm,
        scratch_shapes=[
            pltpu.VMEM(table.shape, BF16),
            pltpu.VMEM((slot_count, width), BF16),
            pltpu.SemaphoreType.DMA((5,)),
        ],
        compiler_params=params(),
        name="select",
    )(asked, *in_hbm(table))
    fetched = exchange(rows.reshape(owners, capacity, width)).reshape(slot_count, width)
    side_far = flip(side, "ctx", count // 2)
    side_mate = flip(side, "ctx", 1)
    side_blocks = gather_blocks(side, "ctx", {1: side_mate, count // 2: after(side_far, rows)})
    index = lax.axis_index("ctx").astype(jnp.int32) ^ jnp.arange(count, dtype=jnp.int32)
    prep_shapes = (
        jax.ShapeDtypeStruct((count, events, width), F32),
        jax.ShapeDtypeStruct((count, events, 128), F32),
        jax.ShapeDtypeStruct((count, 8, events), F32),
        jax.ShapeDtypeStruct((slot_count, events), BF16),
    )
    pinned = [pltpu.HBM(a.shape, a.dtype) for a in prep_shapes]
    spread, chosen = pl.pallas_call(
        places_kernel,
        out_shape=(pinned[3], pltpu.HBM((table.shape[0], slot_count), BF16)),
        in_specs=[vmem, vmem],
        out_specs=(vmem, vmem),
        compiler_params=params(),
        name="places",
    )(slots, after(asked, rows))
    prepared = pl.pallas_call(
        functools.partial(prep_kernel, count),
        out_shape=tuple(pinned[:3]),
        in_specs=[smem, hbm] + [vmem] * count,
        out_specs=(vmem,) * 3,
        scratch_shapes=[pltpu.VMEM(w_out.shape, BF16), pltpu.SemaphoreType.DMA((1,))],
        compiler_params=params(20),
        name="prep",
    )(index, *in_hbm(w_out), *side_blocks)
    prepared = in_hbm(*prepared, spread)
    fetched, prepared = lax.optimization_barrier((fetched, prepared))
    embedded = pl.pallas_call(
        embed_kernel,
        out_shape=jax.ShapeDtypeStruct((events, width), BF16),
        compiler_params=params(),
        name="embed",
    )(slots, fetched)
    emb_far = flip(embedded, "ctx", count // 2)
    emb_mate = flip(embedded, "ctx", 1)
    event_shape = jax.ShapeDtypeStruct((events, width), BF16)
    early = pl.pallas_call(
        early_kernel,
        out_shape=(
            jax.ShapeDtypeStruct((2, events, 4 * width), BF16),
            jax.ShapeDtypeStruct((2, events, width), F32),
            jax.ShapeDtypeStruct((2, events, width), BF16),
            jax.ShapeDtypeStruct((events, 4 * width), F32),
            jax.ShapeDtypeStruct((events, 4 * width), F32),
            event_shape,
        )
        + tuple(jax.ShapeDtypeStruct(a.shape, BF16) for a in (w_in, w_out))
        + prep_shapes
        + (jax.ShapeDtypeStruct(side.shape, BF16),),
        in_specs=[smem, vmem, vmem, vmem] + [hbm] * 6,
        out_specs=(vmem,) * 13,
        scratch_shapes=[pltpu.SemaphoreType.DMA((7,))],
        compiler_params=params(20),
        name="early",
    )(index, embedded, emb_mate, w_in, *in_hbm(w_out), *prepared, *in_hbm(side))
    emb_far = after(emb_far, early[0])
    proj_far = pl.pallas_call(
        project_kernel,
        out_shape=jax.ShapeDtypeStruct((events, 4 * width), BF16),
        compiler_params=params(),
        name="project_far",
    )(emb_far, early[6])
    emb_blocks = gather_blocks(embedded, "ctx", {1: emb_mate, count // 2: emb_far})
    layer_out, slot_grad = pl.pallas_call(
        functools.partial(late_kernel, count),
        out_shape=(event_shape, jax.ShapeDtypeStruct((slot_count, width), BF16)),
        in_specs=[smem] + [vmem] * (14 + count),
        out_specs=(vmem, vmem),
        scratch_shapes=[
            pltpu.VMEM((count, events, 4 * width), BF16),
            pltpu.VMEM((events, width), F32),
            pltpu.VMEM((count, events, width), BF16),
            pltpu.VMEM((events, 4 * width), F32),
            pltpu.SemaphoreType.DMA((4,)),
        ],
        compiler_params=params(28),
        name="late",
    )(index, *emb_blocks, proj_far, *early)
    returned = exchange(slot_grad.reshape(owners, capacity, width)).reshape(slot_count, width)
    row_grad = pl.pallas_call(
        collect_kernel,
        out_shape=pltpu.HBM(table.shape, F32),
        in_specs=[vmem, vmem],
        out_specs=hbm,
        scratch_shapes=[pltpu.VMEM(table.shape, F32), pltpu.SemaphoreType.DMA((2,))],
        compiler_params=params(),
        name="collect",
    )(chosen, returned)
    return layer_out, row_grad


def solution(mesh):
    rows = P(("table", "ctx"), None)
    return jax.shard_map(
        local,
        mesh=mesh,
        in_specs=(rows, rows, rows, P("table", "ctx"), P(), P(), rows),
        out_specs=(rows, rows),
        check_vma=False,
    )
```

```python
import functools

import jax
import jax.numpy as jnp
from jax import lax
from jax.experimental import pallas as pl
from jax.experimental.pallas import tpu as pltpu
from jax.sharding import PartitionSpec as P

HEADS = 4
HEAD_DIM = 128
NIDS = 2
EPS = 1e-06

F32 = jnp.float32
BF16 = jnp.bfloat16


def dot(a, b):
    return jnp.dot(a, b, preferred_element_type=F32)


def dot_nt(a, b):
    return lax.dot_general(a, b, (((1,), (1,)), ((), ())), preferred_element_type=F32)


def iota(shape, dim):
    return lax.broadcasted_iota(jnp.int32, shape, dim)


def normalize(values):
    centred = values - jnp.mean(values, -1, keepdims=True)
    inverse = lax.rsqrt(jnp.mean(centred * centred, -1, keepdims=True) + EPS)
    return centred * inverse, inverse


def norm_back(grad_norm, normed, inverse):
    mean_grad = jnp.mean(grad_norm, -1, keepdims=True)
    mean_cross = jnp.mean(grad_norm * normed, -1, keepdims=True)
    return (grad_norm - mean_grad - normed * mean_cross) * inverse


def split_exact(values):
    return (values >> 4).astype(F32).astype(BF16), (values & 15).astype(F32).astype(BF16)


def start_copies(pairs, sems):
    copies = [pltpu.make_async_copy(a, b, sems.at[i]) for i, (a, b) in enumerate(pairs)]
    for copy in copies:
        copy.start()
    return copies


EXTRA = 16


def slots_kernel(
    capacity,
    owner_in,
    row_in,
    seg_in,
    cot_in,
    slots_ref,
    wanted_ref,
    side_ref,
    owner_ref,
    row_ref,
    seg_ref,
    sems,
):
    events, width = cot_in.shape
    pairs = (
        (owner_in, owner_ref),
        (row_in, row_ref),
        (seg_in, seg_ref),
        (cot_in, side_ref.at[0:events]),
    )
    copies = start_copies(pairs, sems)
    for copy in copies[:3]:
        copy.wait()
    side_ref[events:, :] = jnp.zeros((EXTRA, width), BF16)
    segments = jnp.broadcast_to(seg_ref[...].astype(F32), (EXTRA, events))
    side_ref[events:, 0:events] = segments.astype(BF16)
    owners = wanted_ref.shape[0]
    owner = jnp.concatenate([owner_ref[k : k + 1, :] for k in range(NIDS)], 1)
    row = jnp.concatenate([row_ref[k : k + 1, :] for k in range(NIDS)], 1)
    ids = owner.shape[1]
    named = iota((owners, ids), 0) == owner
    named_f = jnp.where(named, 1.0, 0.0)
    before = jnp.where(iota((ids, ids), 0) < iota((ids, ids), 1), 1.0, 0.0).astype(BF16)
    earlier = dot(named_f.astype(BF16), before)
    rank = jnp.sum(earlier * named_f, 0, keepdims=True).astype(jnp.int32)
    slot = owner * capacity + rank
    slots_ref[...] = jnp.full(slots_ref.shape, -1, jnp.int32)
    for k in range(NIDS):
        slots_ref[k : k + 1, :] = slot[:, k * events : (k + 1) * events]
    ranked = jnp.where(iota((capacity, ids), 0) == rank, 1.0, 0.0).astype(BF16)
    high, low = (row >> 4).astype(F32), (row & 15).astype(F32)
    wanted = 16.0 * dot_nt((named_f * high).astype(BF16), ranked) + dot_nt(
        (named_f * low).astype(BF16), ranked
    )
    wanted_ref[...] = wanted.astype(jnp.int32)
    for copy in copies[3:]:
        copy.wait()


def select_kernel(asked_ref, table_in, out_ref, table_ref, rows_ref, sems):
    (table_copy,) = start_copies(((table_in, table_ref),), sems)
    owners, capacity = asked_ref.shape
    rows = table_ref.shape[0]
    parts = sems.shape[0] - 1
    step = owners // parts
    columns = jnp.transpose(asked_ref[...])
    lane = iota((capacity, rows), 1)
    copies = []
    for part in range(parts):
        sources = range(part * step, (part + 1) * step)
        chosen = [jnp.where(lane == columns[:, s : s + 1], 1.0, 0.0) for s in sources]
        chosen = jnp.concatenate(chosen, 0).astype(BF16)
        if part == 0:
            table_copy.wait()
        place = pl.ds(part * step * capacity, step * capacity)
        rows_ref[place, :] = dot(chosen, table_ref[...]).astype(BF16)
        copy = pltpu.make_async_copy(rows_ref.at[place], out_ref.at[place], sems.at[1 + part])
        copy.start()
        copies.append(copy)
    for copy in copies:
        copy.wait()


def embed_kernel(slots_ref, fetched_ref, out_ref):
    events = out_ref.shape[0]
    slots = fetched_ref.shape[0]
    column = jnp.transpose(slots_ref[...])
    lane = iota((events, slots), 1)
    hit = lane == column[:, 0:1]
    for k in range(1, NIDS):
        hit = hit | (lane == column[:, k : k + 1])
    picked = jnp.where(hit, 1.0, 0.0).astype(BF16)
    out_ref[...] = dot(picked, fetched_ref[...]).astype(BF16)


def collect_kernel(chosen_ref, returned_ref, out_ref, rows_ref, sems):
    parts = sems.shape[0]
    step = rows_ref.shape[0] // parts
    copies = []
    for part in range(parts):
        place = pl.ds(part * step, step)
        rows_ref[place, :] = dot(chosen_ref[place, :], returned_ref[...])
        copy = pltpu.make_async_copy(rows_ref.at[place], out_ref.at[place], sems.at[part])
        copy.start()
        copies.append(copy)
    for copy in copies:
        copy.wait()


SCALE = HEAD_DIM ** (-0.5)


def head(part, h, width):
    return slice(part * width + h * HEAD_DIM, part * width + (h + 1) * HEAD_DIM)


def visible(query_chunk, key_chunk, segc_ref, segr_ref, flip):
    events = segr_ref.shape[2]
    first, second = iota((events, events), 0), iota((events, events), 1)
    if flip:
        same = segc_ref[key_chunk][:, 0:1] == segr_ref[query_chunk][0:1, :]
        return same & (first <= second + (query_chunk - key_chunk) * events)
    same = segc_ref[query_chunk][:, 0:1] == segr_ref[key_chunk][0:1, :]
    return same & (first + (query_chunk - key_chunk) * events >= second)


def project(emb, w_in_ref, write, slope_ref):
    width = emb.shape[1]
    normed = (0.5 * normalize(emb.astype(F32))[0]).astype(BF16)
    for block in range(4):
        columns = slice(block * width, (block + 1) * width)
        half = dot(normed, w_in_ref[:, columns])
        bend = jnp.tanh(half)
        value = half + half * bend
        write(columns, value.astype(BF16))
        if slope_ref is not None:
            sigma = 0.5 + 0.5 * bend
            slope_ref[:, columns] = sigma + value - value * sigma


def prep_kernel(count, index_ref, w_out_in, *refs):
    mixed_ref, segc_ref, segr_ref, w_out_ref, sems = refs[count:]
    (copy,) = start_copies(((w_out_in, w_out_ref),), sems)
    events = mixed_ref.shape[1]
    for t in range(count):
        place = index_ref[t]
        seg = refs[t][events : events + EXTRA, 0:events].astype(F32)[0:8]
        segr_ref[place] = seg
        segc_ref[place] = jnp.broadcast_to(jnp.transpose(seg)[:, 0:1], segc_ref.shape[1:])
    copy.wait()
    for t in range(count):
        mixed_ref[index_ref[t]] = dot_nt(refs[t][0:events, :], w_out_ref[...])


def places_kernel(slots_ref, asked_ref, spread_ref, chosen_ref):
    slot = iota(spread_ref.shape, 0)
    hit = slot == slots_ref[0:1, :]
    for k in range(1, NIDS):
        hit = hit | (slot == slots_ref[k : k + 1, :])
    spread_ref[...] = jnp.where(hit, 1.0, 0.0).astype(BF16)
    owners, capacity = asked_ref.shape
    slots = owners * capacity
    high, low = split_exact(asked_ref[...])
    place = jnp.where(
        iota((capacity, slots), 1) % capacity == iota((capacity, slots), 0), 1.0, 0.0
    ).astype(BF16)
    values = 16.0 * dot(high, place) + dot(low, place)
    mine = iota((owners, slots), 1) // capacity == iota((owners, slots), 0)
    asked = jnp.sum(jnp.where(mine, values, 0.0), 0, keepdims=True).astype(jnp.int32)
    chosen_ref[...] = jnp.where(iota(chosen_ref.shape, 0) == asked, 1.0, 0.0).astype(BF16)


HIDDEN = -1e4


def bent(raw, mask):
    half = jnp.where(mask, raw * (0.5 * SCALE), HIDDEN)
    raised = (1.0 + jnp.tanh(half)).astype(BF16)
    half = half.astype(BF16)
    one, two = BF16(1.0), BF16(2.0)
    return half * raised, raised * (one + half * (two - raised))


def by_twos(start, stop, work):
    twos = (stop - start) // 2

    def step(k, _):
        work([start + 2 * k, start + 2 * k + 1])
        return 0

    lax.fori_loop(0, twos, step, 0)

    @pl.when(stop - start > 2 * twos)
    def _():
        work([stop - 1])


def pipelined(numbers, mask_of, scores, finish):
    masks = {}
    items = [(n, h) for n in range(len(numbers)) for h in range(HEADS)]
    ready = scores(numbers[0], 0)
    for at, (n, h) in enumerate(items):
        now = ready
        if at + 1 < len(items):
            later, later_head = items[at + 1]
            ready = scores(numbers[later], later_head)
        if n not in masks:
            masks[n] = mask_of(numbers[n])
        finish(numbers[n], h, now, masks[n])


class Chunks:
    def __init__(self, proj_ref, gatt_ref, segc_ref, segr_ref, join_ref):
        self.proj, self.gatt = proj_ref, gatt_ref
        self.segc, self.segr, self.join = segc_ref, segr_ref, join_ref
        self.width = gatt_ref.shape[2]

    def cut(self, chunk, part, h):
        return self.proj[chunk, :, head(part, h, self.width)]

    def attend(self, i, start, stop, att_ref):
        def scores(j, h):
            return dot_nt(self.cut(i, 2, h), self.cut(j, 3, h))

        def finish(j, h, raw, mask):
            half = jnp.where(mask, raw * (0.5 * SCALE), HIDDEN)
            weights = (half + half * jnp.tanh(half)).astype(BF16)
            att_ref[:, head(0, h, self.width)] += dot(weights, self.cut(j, 1, h))

        def mask_of(j):
            return visible(i, j, self.segc, self.segr, False)

        by_twos(start, stop, lambda js: pipelined(js, mask_of, scores, finish))

    def finish(self, i, own, att, grad_mixed, emb_ref, w_out_ref, out_ref):
        att_norm, att_inverse = normalize(att)
        gate = self.proj[i, :, 0 : self.width].astype(F32)
        grad_att = norm_back(grad_mixed * gate, att_norm, att_inverse)
        self.gatt[i] = grad_att.astype(BF16)

        @pl.when(i == own)
        def _():
            mixed = (att_norm * gate).astype(BF16)
            out = emb_ref[...].astype(F32) + dot(mixed, w_out_ref[...])
            out_ref[...] = out.astype(BF16)
            self.join[:, 0 : self.width] = grad_mixed * att_norm

    def query_side(self, own, start, stop):
        def scores(j, h):
            grad_att = self.gatt[own, :, head(0, h, self.width)]
            return (
                dot_nt(self.cut(own, 2, h), self.cut(j, 3, h)),
                dot_nt(grad_att, self.cut(j, 1, h)),
            )

        def finish(j, h, pair, mask):
            raw, grad_weights = pair
            _, slope = bent(raw, mask)
            grad_raw = grad_weights.astype(BF16) * slope
            self.join[:, head(2, h, self.width)] += dot(grad_raw, self.cut(j, 3, h))

        def mask_of(j):
            return visible(own, j, self.segc, self.segr, False)

        by_twos(start, stop, lambda js: pipelined(js, mask_of, scores, finish))

    def key_side(self, own, start, stop):
        def scores(i, h):
            grad_att = self.gatt[i, :, head(0, h, self.width)]
            return (
                dot_nt(self.cut(own, 3, h), self.cut(i, 2, h)),
                dot_nt(self.cut(own, 1, h), grad_att),
            )

        def finish(i, h, pair, mask):
            raw, grad_weights = pair
            value, slope = bent(raw, mask)
            grad_raw = grad_weights.astype(BF16) * slope
            self.join[:, head(3, h, self.width)] += dot(grad_raw, self.cut(i, 2, h))
            grad_att = self.gatt[i, :, head(0, h, self.width)]
            self.join[:, head(1, h, self.width)] += dot(value, grad_att)

        def mask_of(i):
            return visible(i, own, self.segc, self.segr, True)

        by_twos(start, stop, lambda chunks: pipelined(chunks, mask_of, scores, finish))


def early_kernel(index_ref, emb_ref, mate_ref, *refs):
    w_in_in, w_out_in, mixed_in, segc_in, segr_in, spread_in, side_in = refs[:7]
    proj_ref, att_ref, gatt_ref, join_ref, slope_ref, out_ref = refs[7:13]
    w_in_ref, w_out_ref, mixed_ref, segc_ref, segr_ref, spread_ref, side_ref, sems = refs[13:]
    pairs = [(segc_in, segc_ref), (segr_in, segr_ref), (mixed_in, mixed_ref)]
    pairs += [(w_out_in, w_out_ref), (spread_in, spread_ref), (side_in, side_ref)]
    pairs += [(w_in_in, w_in_ref)]
    copies = start_copies(pairs, sems)
    own = index_ref[0]
    mate = index_ref[1]
    base = jnp.minimum(own, mate)
    last = jnp.maximum(own, mate)

    def write_to(place):
        def write(columns, value):
            proj_ref[place - base, :, columns] = value

        return write

    project(emb_ref[...], w_in_in, write_to(own), slope_ref)
    project(mate_ref[...], w_in_in, write_to(mate), None)
    for copy in copies[:2]:
        copy.wait()
    att_ref[...] = jnp.zeros_like(att_ref)
    join_ref[...] = jnp.zeros_like(join_ref)
    pair_rows = pl.ds(base, 2)
    chunks = Chunks(
        proj_ref, gatt_ref, segc_ref.at[pair_rows], segr_ref.at[pair_rows], join_ref
    )

    def forward(i, _):
        chunks.attend(i, 0, i + 1, att_ref.at[i])
        return 0

    lax.fori_loop(own - base, last - base + 1, forward, 0)
    for copy in copies[2:]:
        copy.wait()

    @pl.when(base == 0)
    def _():
        def finish(i, _):
            chunks.finish(i, own, att_ref[i], mixed_ref[i], emb_ref, w_out_ref, out_ref)
            return 0

        lax.fori_loop(own, last + 1, finish, 0)
        chunks.query_side(own, 0, own + 1)
        chunks.key_side(own, own, last + 1)


def project_kernel(emb_ref, w_in_ref, proj_ref):
    def write(columns, value):
        proj_ref[:, columns] = value

    project(emb_ref[...], w_in_ref, write, None)


def late_kernel(count, *refs):
    index_ref = refs[0]
    emb_refs = refs[1 : 1 + count]
    proj_far_ref = refs[1 + count]
    (
        proj_pair_ref,
        att_pair_ref,
        gatt_pair_ref,
        join_early_ref,
        slope_ref,
        out_early_ref,
        w_in_ref,
        w_out_ref,
        mixed_ref,
        segc_ref,
        segr_ref,
        spread_ref,
        side_ref,
        out_ref,
        grad_ref,
        proj_ref,
        att_ref,
        gatt_ref,
        join_ref,
        sems,
    ) = refs[2 + count :]
    own = index_ref[0]
    base = jnp.minimum(own, index_ref[1])
    last = jnp.maximum(own, index_ref[1])
    closed = base == 0

    pair_rows = pl.ds(base, 2)
    copies = start_copies(
        (
            (join_early_ref, join_ref),
            (proj_pair_ref, proj_ref.at[pair_rows]),
            (gatt_pair_ref, gatt_ref.at[pair_rows]),
            (proj_far_ref, proj_ref.at[index_ref[count // 2]]),
        ),
        sems,
    )

    def write_to(place):
        def write(columns, value):
            proj_ref[place, :, columns] = value

        return write

    for t in range(2, count):
        if t == count // 2:
            continue
        project(emb_refs[t][...], w_in_ref, write_to(index_ref[t]), None)
    for copy in copies:
        copy.wait()
    chunks = Chunks(proj_ref, gatt_ref, segc_ref, segr_ref, join_ref)

    @pl.when(closed)
    def _():
        out_ref[...] = out_early_ref[...]

    def forward(i, _):
        begun = i <= last

        @pl.when(begun)
        def _():
            att_ref[...] = att_pair_ref[jnp.minimum(i - base, 1)]

        @pl.when(jnp.logical_not(begun))
        def _():
            att_ref[...] = jnp.zeros_like(att_ref)

        chunks.attend(i, 0, jnp.where(begun, base, i + 1), att_ref)
        chunks.finish(i, own, att_ref[...], mixed_ref[i], emb_refs[0], w_out_ref, out_ref)
        return 0

    lax.fori_loop(jnp.where(closed, last + 1, own), count, forward, 0)
    chunks.query_side(own, jnp.where(closed, own + 1, 0), own + 1)
    chunks.key_side(own, jnp.where(closed, last + 1, own), count)

    width = gatt_ref.shape[2]
    grad_normed = None
    for block in range(4):
        columns = slice(block * width, (block + 1) * width)
        joined = join_ref[:, columns] * slope_ref[:, columns]
        if block >= 2:
            joined = joined * (0.5 * SCALE)
        part = dot_nt(joined.astype(BF16), w_in_ref[:, columns])
        grad_normed = part if block == 0 else grad_normed + part
    normed, inverse = normalize(emb_refs[0][...].astype(F32))
    grad = norm_back(grad_normed, normed, inverse) + side_ref[0 : emb_refs[0].shape[0], :].astype(F32)
    grad_ref[...] = dot(spread_ref[...], grad.astype(BF16)).astype(BF16)


def in_hbm(*arrays):
    return [pltpu.with_memory_space_constraint(a, pltpu.HBM) for a in arrays]


def params(mebibytes=12):
    return pltpu.CompilerParams(vmem_limit_bytes=mebibytes * 1024 * 1024)


def flip(value, axis, offset):
    count = lax.axis_size(axis)
    return lax.ppermute(value, axis, [(i, i ^ offset) for i in range(count)])


def gather_blocks(value, axis, known):
    bit = lax.axis_size(axis)
    blocks = {0: value}
    while bit > 1:
        bit //= 2
        for t in list(blocks):
            blocks[t | bit] = known.get(t | bit)
            if blocks[t | bit] is None:
                blocks[t | bit] = flip(blocks[t], axis, bit)
    return [blocks[t] for t in range(lax.axis_size(axis))]


def after(value, earlier):
    return lax.optimization_barrier((value, earlier))[0]


def local(table, item_owner, item_row, segment_ids, w_in, w_out, cotangent):
    owners = lax.axis_size("table") * lax.axis_size("ctx")
    count = lax.axis_size("ctx")
    events, width = cotangent.shape
    id_count = events * NIDS
    capacity = 2 * ((id_count + owners - 1) // owners)
    slot_count = owners * capacity
    axes = ("table", "ctx")
    vmem = pl.BlockSpec(memory_space=pltpu.VMEM)
    smem = pl.BlockSpec(memory_space=pltpu.SMEM)

    def exchange(value):
        return lax.all_to_all(value, axes, split_axis=0, concat_axis=0, tiled=True)

    hbm = pl.BlockSpec(memory_space=pltpu.HBM)
    slots, wanted, side = pl.pallas_call(
        functools.partial(slots_kernel, capacity),
        out_shape=(
            jax.ShapeDtypeStruct((8, events), jnp.int32),
            jax.ShapeDtypeStruct((owners, capacity), jnp.int32),
            jax.ShapeDtypeStruct((events + EXTRA, width), BF16),
        ),
        in_specs=[hbm] * 4,
        out_specs=(vmem, vmem, vmem),
        scratch_shapes=[
            pltpu.VMEM((NIDS, events), jnp.int32),
            pltpu.VMEM((NIDS, events), jnp.int32),
            pltpu.VMEM((1, events), jnp.int32),
            pltpu.SemaphoreType.DMA((4,)),
        ],
        compiler_params=params(),
        name="slots",
    )(*in_hbm(item_owner.T, item_row.T, segment_ids.reshape(1, events), cotangent))
    asked = exchange(wanted)
    rows = pl.pallas_call(
        select_kernel,
        out_shape=pltpu.HBM((slot_count, width), BF16),
        in_specs=[vmem, hbm],
        out_specs=hbm,
        scratch_shapes=[
            pltpu.VMEM(table.shape, BF16),
            pltpu.VMEM((slot_count, width), BF16),
            pltpu.SemaphoreType.DMA((5,)),
        ],
        compiler_params=params(),
        name="select",
    )(asked, *in_hbm(table))
    fetched = exchange(rows.reshape(owners, capacity, width)).reshape(slot_count, width)
    side_far = flip(side, "ctx", count // 2)
    side_mate = flip(side, "ctx", 1)
    side_blocks = gather_blocks(side, "ctx", {1: side_mate, count // 2: after(side_far, rows)})
    index = lax.axis_index("ctx").astype(jnp.int32) ^ jnp.arange(count, dtype=jnp.int32)
    prep_shapes = (
        jax.ShapeDtypeStruct((count, events, width), F32),
        jax.ShapeDtypeStruct((count, events, 128), F32),
        jax.ShapeDtypeStruct((count, 8, events), F32),
        jax.ShapeDtypeStruct((slot_count, events), BF16),
    )
    pinned = [pltpu.HBM(a.shape, a.dtype) for a in prep_shapes]
    spread, chosen = pl.pallas_call(
        places_kernel,
        out_shape=(pinned[3], pltpu.HBM((table.shape[0], slot_count), BF16)),
        in_specs=[vmem, vmem],
        out_specs=(vmem, vmem),
        compiler_params=params(),
        name="places",
    )(slots, after(asked, rows))
    prepared = pl.pallas_call(
        functools.partial(prep_kernel, count),
        out_shape=tuple(pinned[:3]),
        in_specs=[smem, hbm] + [vmem] * count,
        out_specs=(vmem,) * 3,
        scratch_shapes=[pltpu.VMEM(w_out.shape, BF16), pltpu.SemaphoreType.DMA((1,))],
        compiler_params=params(20),
        name="prep",
    )(index, *in_hbm(w_out), *side_blocks)
    prepared = in_hbm(*prepared, spread)
    fetched, prepared = lax.optimization_barrier((fetched, prepared))
    embedded = pl.pallas_call(
        embed_kernel,
        out_shape=jax.ShapeDtypeStruct((events, width), BF16),
        compiler_params=params(),
        name="embed",
    )(slots, fetched)
    emb_far = flip(embedded, "ctx", count // 2)
    emb_mate = flip(embedded, "ctx", 1)
    event_shape = jax.ShapeDtypeStruct((events, width), BF16)
    early = pl.pallas_call(
        early_kernel,
        out_shape=(
            jax.ShapeDtypeStruct((2, events, 4 * width), BF16),
            jax.ShapeDtypeStruct((2, events, width), F32),
            jax.ShapeDtypeStruct((2, events, width), BF16),
            jax.ShapeDtypeStruct((events, 4 * width), F32),
            jax.ShapeDtypeStruct((events, 4 * width), F32),
            event_shape,
        )
        + tuple(jax.ShapeDtypeStruct(a.shape, BF16) for a in (w_in, w_out))
        + prep_shapes
        + (jax.ShapeDtypeStruct(side.shape, BF16),),
        in_specs=[smem, vmem, vmem, vmem] + [hbm] * 6,
        out_specs=(vmem,) * 13,
        scratch_shapes=[pltpu.SemaphoreType.DMA((7,))],
        compiler_params=params(20),
        name="early",
    )(index, embedded, emb_mate, w_in, *in_hbm(w_out), *prepared, *in_hbm(side))
    emb_far = after(emb_far, early[0])
    proj_far = pl.pallas_call(
        project_kernel,
        out_shape=jax.ShapeDtypeStruct((events, 4 * width), BF16),
        compiler_params=params(),
        name="project_far",
    )(emb_far, early[6])
    emb_blocks = gather_blocks(embedded, "ctx", {1: emb_mate, count // 2: emb_far})
    layer_out, slot_grad = pl.pallas_call(
        functools.partial(late_kernel, count),
        out_shape=(event_shape, jax.ShapeDtypeStruct((slot_count, width), BF16)),
        in_specs=[smem] + [vmem] * (14 + count),
        out_specs=(vmem, vmem),
        scratch_shapes=[
            pltpu.VMEM((count, events, 4 * width), BF16),
            pltpu.VMEM((events, width), F32),
            pltpu.VMEM((count, events, width), BF16),
            pltpu.VMEM((events, 4 * width), F32),
            pltpu.SemaphoreType.DMA((4,)),
        ],
        compiler_params=params(28),
        name="late",
    )(index, *emb_blocks, proj_far, *early)
    returned = exchange(slot_grad.reshape(owners, capacity, width)).reshape(slot_count, width)
    row_grad = pl.pallas_call(
        collect_kernel,
        out_shape=pltpu.HBM(table.shape, F32),
        in_specs=[vmem, vmem],
        out_specs=hbm,
        scratch_shapes=[pltpu.VMEM(table.shape, F32), pltpu.SemaphoreType.DMA((2,))],
        compiler_params=params(),
        name="collect",
    )(chosen, returned)
    return layer_out, row_grad


def solution(mesh):
    rows = P(("table", "ctx"), None)
    return jax.shard_map(
        local,
        mesh=mesh,
        in_specs=(rows, rows, rows, P("table", "ctx"), P(), P(), rows),
        out_specs=(rows, rows),
        check_vma=False,
    )
```

```python
import functools

import jax
import jax.numpy as jnp
from jax import lax
from jax.experimental import pallas as pl
from jax.experimental.pallas import tpu as pltpu
from jax.sharding import PartitionSpec as P

HEADS = 4
HEAD_DIM = 128
NIDS = 2
EPS = 1e-06

F32 = jnp.float32
BF16 = jnp.bfloat16


def dot(a, b):
    return jnp.dot(a, b, preferred_element_type=F32)


def dot_nt(a, b):
    return lax.dot_general(a, b, (((1,), (1,)), ((), ())), preferred_element_type=F32)


def iota(shape, dim):
    return lax.broadcasted_iota(jnp.int32, shape, dim)


def normalize(values):
    centred = values - jnp.mean(values, -1, keepdims=True)
    inverse = lax.rsqrt(jnp.mean(centred * centred, -1, keepdims=True) + EPS)
    return centred * inverse, inverse


def norm_back(grad_norm, normed, inverse):
    mean_grad = jnp.mean(grad_norm, -1, keepdims=True)
    mean_cross = jnp.mean(grad_norm * normed, -1, keepdims=True)
    return (grad_norm - mean_grad - normed * mean_cross) * inverse


def split_exact(values):
    return (values >> 4).astype(F32).astype(BF16), (values & 15).astype(F32).astype(BF16)


def start_copies(pairs, sems):
    copies = [pltpu.make_async_copy(a, b, sems.at[i]) for i, (a, b) in enumerate(pairs)]
    for copy in copies:
        copy.start()
    return copies


EXTRA = 16


def slots_kernel(
    capacity,
    owner_in,
    row_in,
    seg_in,
    cot_in,
    slots_ref,
    wanted_ref,
    side_ref,
    owner_ref,
    row_ref,
    seg_ref,
    sems,
):
    events, width = cot_in.shape
    pairs = (
        (owner_in, owner_ref),
        (row_in, row_ref),
        (seg_in, seg_ref),
        (cot_in, side_ref.at[0:events]),
    )
    copies = start_copies(pairs, sems)
    for copy in copies[:3]:
        copy.wait()
    side_ref[events:, :] = jnp.zeros((EXTRA, width), BF16)
    segments = jnp.broadcast_to(seg_ref[...].astype(F32), (EXTRA, events))
    side_ref[events:, 0:events] = segments.astype(BF16)
    owners = wanted_ref.shape[0]
    owner = jnp.concatenate([owner_ref[k : k + 1, :] for k in range(NIDS)], 1)
    row = jnp.concatenate([row_ref[k : k + 1, :] for k in range(NIDS)], 1)
    ids = owner.shape[1]
    named = iota((owners, ids), 0) == owner
    named_f = jnp.where(named, 1.0, 0.0)
    before = jnp.where(iota((ids, ids), 0) < iota((ids, ids), 1), 1.0, 0.0).astype(BF16)
    earlier = dot(named_f.astype(BF16), before)
    rank = jnp.sum(earlier * named_f, 0, keepdims=True).astype(jnp.int32)
    slot = owner * capacity + rank
    slots_ref[...] = jnp.full(slots_ref.shape, -1, jnp.int32)
    for k in range(NIDS):
        slots_ref[k : k + 1, :] = slot[:, k * events : (k + 1) * events]
    ranked = jnp.where(iota((capacity, ids), 0) == rank, 1.0, 0.0).astype(BF16)
    high, low = (row >> 4).astype(F32), (row & 15).astype(F32)
    wanted = 16.0 * dot_nt((named_f * high).astype(BF16), ranked) + dot_nt(
        (named_f * low).astype(BF16), ranked
    )
    wanted_ref[...] = wanted.astype(jnp.int32)
    for copy in copies[3:]:
        copy.wait()


def select_kernel(asked_ref, table_in, out_ref, table_ref, rows_ref, sems):
    (table_copy,) = start_copies(((table_in, table_ref),), sems)
    owners, capacity = asked_ref.shape
    rows = table_ref.shape[0]
    parts = sems.shape[0] - 1
    step = owners // parts
    columns = jnp.transpose(asked_ref[...])
    lane = iota((capacity, rows), 1)
    copies = []
    for part in range(parts):
        sources = range(part * step, (part + 1) * step)
        chosen = [jnp.where(lane == columns[:, s : s + 1], 1.0, 0.0) for s in sources]
        chosen = jnp.concatenate(chosen, 0).astype(BF16)
        if part == 0:
            table_copy.wait()
        place = pl.ds(part * step * capacity, step * capacity)
        rows_ref[place, :] = dot(chosen, table_ref[...]).astype(BF16)
        copy = pltpu.make_async_copy(rows_ref.at[place], out_ref.at[place], sems.at[1 + part])
        copy.start()
        copies.append(copy)
    for copy in copies:
        copy.wait()


def embed_kernel(slots_ref, fetched_ref, out_ref):
    events = out_ref.shape[0]
    slots = fetched_ref.shape[0]
    column = jnp.transpose(slots_ref[...])
    lane = iota((events, slots), 1)
    hit = lane == column[:, 0:1]
    for k in range(1, NIDS):
        hit = hit | (lane == column[:, k : k + 1])
    picked = jnp.where(hit, 1.0, 0.0).astype(BF16)
    out_ref[...] = dot(picked, fetched_ref[...]).astype(BF16)


def collect_kernel(chosen_ref, returned_ref, out_ref, rows_ref, sems):
    parts = sems.shape[0]
    step = rows_ref.shape[0] // parts
    copies = []
    for part in range(parts):
        place = pl.ds(part * step, step)
        rows_ref[place, :] = dot(chosen_ref[place, :], returned_ref[...])
        copy = pltpu.make_async_copy(rows_ref.at[place], out_ref.at[place], sems.at[part])
        copy.start()
        copies.append(copy)
    for copy in copies:
        copy.wait()


SCALE = HEAD_DIM ** (-0.5)


def head(part, h, width):
    return slice(part * width + h * HEAD_DIM, part * width + (h + 1) * HEAD_DIM)


def visible(query_chunk, key_chunk, segc_ref, segr_ref, flip):
    events = segr_ref.shape[2]
    first, second = iota((events, events), 0), iota((events, events), 1)
    if flip:
        same = segc_ref[key_chunk][:, 0:1] == segr_ref[query_chunk][0:1, :]
        return same & (first <= second + (query_chunk - key_chunk) * events)
    same = segc_ref[query_chunk][:, 0:1] == segr_ref[key_chunk][0:1, :]
    return same & (first + (query_chunk - key_chunk) * events >= second)


def project(emb, w_in_ref, write, slope_ref):
    width = emb.shape[1]
    normed = (0.5 * normalize(emb.astype(F32))[0]).astype(BF16)
    for block in range(4):
        columns = slice(block * width, (block + 1) * width)
        half = dot(normed, w_in_ref[:, columns])
        bend = jnp.tanh(half)
        value = half + half * bend
        write(columns, value.astype(BF16))
        if slope_ref is not None:
            sigma = 0.5 + 0.5 * bend
            slope_ref[:, columns] = sigma + value - value * sigma


def prep_kernel(count, index_ref, w_out_in, *refs):
    mixed_ref, segc_ref, segr_ref, w_out_ref, sems = refs[count:]
    (copy,) = start_copies(((w_out_in, w_out_ref),), sems)
    events = mixed_ref.shape[1]
    for t in range(count):
        place = index_ref[t]
        seg = refs[t][events : events + EXTRA, 0:events].astype(F32)[0:8]
        segr_ref[place] = seg
        segc_ref[place] = jnp.broadcast_to(jnp.transpose(seg)[:, 0:1], segc_ref.shape[1:])
    copy.wait()
    for t in range(count):
        mixed_ref[index_ref[t]] = dot_nt(refs[t][0:events, :], w_out_ref[...])


def places_kernel(slots_ref, asked_ref, spread_ref, chosen_ref):
    slot = iota(spread_ref.shape, 0)
    hit = slot == slots_ref[0:1, :]
    for k in range(1, NIDS):
        hit = hit | (slot == slots_ref[k : k + 1, :])
    spread_ref[...] = jnp.where(hit, 1.0, 0.0).astype(BF16)
    owners, capacity = asked_ref.shape
    slots = owners * capacity
    high, low = split_exact(asked_ref[...])
    place = jnp.where(
        iota((capacity, slots), 1) % capacity == iota((capacity, slots), 0), 1.0, 0.0
    ).astype(BF16)
    values = 16.0 * dot(high, place) + dot(low, place)
    mine = iota((owners, slots), 1) // capacity == iota((owners, slots), 0)
    asked = jnp.sum(jnp.where(mine, values, 0.0), 0, keepdims=True).astype(jnp.int32)
    chosen_ref[...] = jnp.where(iota(chosen_ref.shape, 0) == asked, 1.0, 0.0).astype(BF16)


HIDDEN = -1e4


def bent(raw, mask):
    half = jnp.where(mask, raw * (0.5 * SCALE), HIDDEN)
    raised = (1.0 + jnp.tanh(half)).astype(BF16)
    half = half.astype(BF16)
    one, two = BF16(1.0), BF16(2.0)
    return half * raised, raised * (one + half * (two - raised))


def by_twos(start, stop, work):
    twos = (stop - start) // 2

    def step(k, _):
        work([start + 2 * k, start + 2 * k + 1])
        return 0

    lax.fori_loop(0, twos, step, 0)

    @pl.when(stop - start > 2 * twos)
    def _():
        work([stop - 1])


def pipelined(numbers, mask_of, scores, finish):
    masks = {}
    items = [(n, h) for n in range(len(numbers)) for h in range(HEADS)]
    ready = scores(numbers[0], 0)
    for at, (n, h) in enumerate(items):
        now = ready
        if at + 1 < len(items):
            later, later_head = items[at + 1]
            ready = scores(numbers[later], later_head)
        if n not in masks:
            masks[n] = mask_of(numbers[n])
        finish(numbers[n], h, now, masks[n])


class Chunks:
    def __init__(self, proj_ref, gatt_ref, segc_ref, segr_ref, join_ref):
        self.proj, self.gatt = proj_ref, gatt_ref
        self.segc, self.segr, self.join = segc_ref, segr_ref, join_ref
        self.width = gatt_ref.shape[2]

    def cut(self, chunk, part, h):
        return self.proj[chunk, :, head(part, h, self.width)]

    def attend(self, i, start, stop, att_ref):
        def scores(j, h):
            return dot_nt(self.cut(i, 2, h), self.cut(j, 3, h))

        def finish(j, h, raw, mask):
            half = jnp.where(mask, raw * (0.5 * SCALE), HIDDEN)
            weights = (half + half * jnp.tanh(half)).astype(BF16)
            att_ref[:, head(0, h, self.width)] += dot(weights, self.cut(j, 1, h))

        def mask_of(j):
            return visible(i, j, self.segc, self.segr, False)

        by_twos(start, stop, lambda js: pipelined(js, mask_of, scores, finish))

    def finish(self, i, own, att, grad_mixed, emb_ref, w_out_ref, out_ref):
        att_norm, att_inverse = normalize(att)
        gate = self.proj[i, :, 0 : self.width].astype(F32)
        grad_att = norm_back(grad_mixed * gate, att_norm, att_inverse)
        self.gatt[i] = grad_att.astype(BF16)

        @pl.when(i == own)
        def _():
            mixed = (att_norm * gate).astype(BF16)
            out = emb_ref[...].astype(F32) + dot(mixed, w_out_ref[...])
            out_ref[...] = out.astype(BF16)
            self.join[:, 0 : self.width] = grad_mixed * att_norm

    def query_side(self, own, start, stop):
        def scores(j, h):
            grad_att = self.gatt[own, :, head(0, h, self.width)]
            return (
                dot_nt(self.cut(own, 2, h), self.cut(j, 3, h)),
                dot_nt(grad_att, self.cut(j, 1, h)),
            )

        def finish(j, h, pair, mask):
            raw, grad_weights = pair
            _, slope = bent(raw, mask)
            grad_raw = grad_weights.astype(BF16) * slope
            self.join[:, head(2, h, self.width)] += dot(grad_raw, self.cut(j, 3, h))

        def mask_of(j):
            return visible(own, j, self.segc, self.segr, False)

        by_twos(start, stop, lambda js: pipelined(js, mask_of, scores, finish))

    def key_side(self, own, start, stop):
        def scores(i, h):
            grad_att = self.gatt[i, :, head(0, h, self.width)]
            return (
                dot_nt(self.cut(own, 3, h), self.cut(i, 2, h)),
                dot_nt(self.cut(own, 1, h), grad_att),
            )

        def finish(i, h, pair, mask):
            raw, grad_weights = pair
            value, slope = bent(raw, mask)
            grad_raw = grad_weights.astype(BF16) * slope
            self.join[:, head(3, h, self.width)] += dot(grad_raw, self.cut(i, 2, h))
            grad_att = self.gatt[i, :, head(0, h, self.width)]
            self.join[:, head(1, h, self.width)] += dot(value, grad_att)

        def mask_of(i):
            return visible(i, own, self.segc, self.segr, True)

        by_twos(start, stop, lambda chunks: pipelined(chunks, mask_of, scores, finish))


def early_kernel(index_ref, emb_ref, mate_ref, *refs):
    w_in_in, w_out_in, mixed_in, segc_in, segr_in, spread_in, side_in = refs[:7]
    proj_ref, att_ref, gatt_ref, join_ref, slope_ref, out_ref = refs[7:13]
    w_in_ref, w_out_ref, mixed_ref, segc_ref, segr_ref, spread_ref, side_ref, sems = refs[13:]
    pairs = [(segc_in, segc_ref), (segr_in, segr_ref), (mixed_in, mixed_ref)]
    pairs += [(w_out_in, w_out_ref), (spread_in, spread_ref), (side_in, side_ref)]
    pairs += [(w_in_in, w_in_ref)]
    copies = start_copies(pairs, sems)
    own = index_ref[0]
    mate = index_ref[1]
    base = jnp.minimum(own, mate)
    last = jnp.maximum(own, mate)

    def write_to(place):
        def write(columns, value):
            proj_ref[place - base, :, columns] = value

        return write

    project(emb_ref[...], w_in_in, write_to(own), slope_ref)
    project(mate_ref[...], w_in_in, write_to(mate), None)
    for copy in copies[:2]:
        copy.wait()
    att_ref[...] = jnp.zeros_like(att_ref)
    join_ref[...] = jnp.zeros_like(join_ref)
    pair_rows = pl.ds(base, 2)
    chunks = Chunks(
        proj_ref, gatt_ref, segc_ref.at[pair_rows], segr_ref.at[pair_rows], join_ref
    )

    def forward(i, _):
        chunks.attend(i, 0, i + 1, att_ref.at[i])
        return 0

    lax.fori_loop(own - base, last - base + 1, forward, 0)
    for copy in copies[2:]:
        copy.wait()

    @pl.when(base == 0)
    def _():
        def finish(i, _):
            chunks.finish(i, own, att_ref[i], mixed_ref[i], emb_ref, w_out_ref, out_ref)
            return 0

        lax.fori_loop(own, last + 1, finish, 0)
        chunks.query_side(own, 0, own + 1)
        chunks.key_side(own, own, last + 1)


def project_kernel(emb_ref, w_in_ref, proj_ref):
    def write(columns, value):
        proj_ref[:, columns] = value

    project(emb_ref[...], w_in_ref, write, None)


def late_kernel(count, *refs):
    index_ref = refs[0]
    emb_refs = refs[1 : 1 + count]
    proj_far_ref = refs[1 + count]
    (
        proj_pair_ref,
        att_pair_ref,
        gatt_pair_ref,
        join_early_ref,
        slope_ref,
        out_early_ref,
        w_in_ref,
        w_out_ref,
        mixed_ref,
        segc_ref,
        segr_ref,
        spread_ref,
        side_ref,
        out_ref,
        grad_ref,
        proj_ref,
        att_ref,
        gatt_ref,
        join_ref,
        sems,
    ) = refs[2 + count :]
    own = index_ref[0]
    base = jnp.minimum(own, index_ref[1])
    last = jnp.maximum(own, index_ref[1])
    closed = base == 0

    pair_rows = pl.ds(base, 2)
    width = gatt_ref.shape[2]
    gate_part, other_parts = pl.ds(0, width), pl.ds(width, 3 * width)
    copies = start_copies(
        (
            (proj_pair_ref, proj_ref.at[pair_rows]),
            (proj_far_ref, proj_ref.at[index_ref[count // 2]]),
            (gatt_pair_ref, gatt_ref.at[pair_rows]),
            (join_early_ref.at[:, gate_part], join_ref.at[:, gate_part]),
            (join_early_ref.at[:, other_parts], join_ref.at[:, other_parts]),
        ),
        sems,
    )

    def write_to(place):
        def write(columns, value):
            proj_ref[place, :, columns] = value

        return write

    for t in range(2, count):
        if t == count // 2:
            continue
        project(emb_refs[t][...], w_in_ref, write_to(index_ref[t]), None)
    for copy in copies[:4]:
        copy.wait()
    chunks = Chunks(proj_ref, gatt_ref, segc_ref, segr_ref, join_ref)

    @pl.when(closed)
    def _():
        out_ref[...] = out_early_ref[...]

    def forward(i, _):
        begun = i <= last

        @pl.when(begun)
        def _():
            att_ref[...] = att_pair_ref[jnp.minimum(i - base, 1)]

        @pl.when(jnp.logical_not(begun))
        def _():
            att_ref[...] = jnp.zeros_like(att_ref)

        chunks.attend(i, 0, jnp.where(begun, base, i + 1), att_ref)
        chunks.finish(i, own, att_ref[...], mixed_ref[i], emb_refs[0], w_out_ref, out_ref)
        return 0

    lax.fori_loop(jnp.where(closed, last + 1, own), count, forward, 0)
    copies[4].wait()
    chunks.query_side(own, jnp.where(closed, own + 1, 0), own + 1)
    chunks.key_side(own, jnp.where(closed, last + 1, own), count)

    width = gatt_ref.shape[2]
    grad_normed = None
    for block in range(4):
        columns = slice(block * width, (block + 1) * width)
        joined = join_ref[:, columns] * slope_ref[:, columns]
        if block >= 2:
            joined = joined * (0.5 * SCALE)
        part = dot_nt(joined.astype(BF16), w_in_ref[:, columns])
        grad_normed = part if block == 0 else grad_normed + part
    normed, inverse = normalize(emb_refs[0][...].astype(F32))
    grad = norm_back(grad_normed, normed, inverse) + side_ref[0 : emb_refs[0].shape[0], :].astype(F32)
    grad_ref[...] = dot(spread_ref[...], grad.astype(BF16)).astype(BF16)


def in_hbm(*arrays):
    return [pltpu.with_memory_space_constraint(a, pltpu.HBM) for a in arrays]


def params(mebibytes=12):
    return pltpu.CompilerParams(vmem_limit_bytes=mebibytes * 1024 * 1024)


def flip(value, axis, offset):
    count = lax.axis_size(axis)
    return lax.ppermute(value, axis, [(i, i ^ offset) for i in range(count)])


def gather_blocks(value, axis, known):
    bit = lax.axis_size(axis)
    blocks = {0: value}
    while bit > 1:
        bit //= 2
        for t in list(blocks):
            blocks[t | bit] = known.get(t | bit)
            if blocks[t | bit] is None:
                blocks[t | bit] = flip(blocks[t], axis, bit)
    return [blocks[t] for t in range(lax.axis_size(axis))]


def after(value, earlier):
    return lax.optimization_barrier((value, earlier))[0]


def local(table, item_owner, item_row, segment_ids, w_in, w_out, cotangent):
    owners = lax.axis_size("table") * lax.axis_size("ctx")
    count = lax.axis_size("ctx")
    events, width = cotangent.shape
    id_count = events * NIDS
    capacity = 2 * ((id_count + owners - 1) // owners)
    slot_count = owners * capacity
    axes = ("table", "ctx")
    vmem = pl.BlockSpec(memory_space=pltpu.VMEM)
    smem = pl.BlockSpec(memory_space=pltpu.SMEM)

    def exchange(value):
        return lax.all_to_all(value, axes, split_axis=0, concat_axis=0, tiled=True)

    hbm = pl.BlockSpec(memory_space=pltpu.HBM)
    slots, wanted, side = pl.pallas_call(
        functools.partial(slots_kernel, capacity),
        out_shape=(
            jax.ShapeDtypeStruct((8, events), jnp.int32),
            jax.ShapeDtypeStruct((owners, capacity), jnp.int32),
            jax.ShapeDtypeStruct((events + EXTRA, width), BF16),
        ),
        in_specs=[hbm] * 4,
        out_specs=(vmem, vmem, vmem),
        scratch_shapes=[
            pltpu.VMEM((NIDS, events), jnp.int32),
            pltpu.VMEM((NIDS, events), jnp.int32),
            pltpu.VMEM((1, events), jnp.int32),
            pltpu.SemaphoreType.DMA((4,)),
        ],
        compiler_params=params(),
        name="slots",
    )(*in_hbm(item_owner.T, item_row.T, segment_ids.reshape(1, events), cotangent))
    asked = exchange(wanted)
    rows = pl.pallas_call(
        select_kernel,
        out_shape=pltpu.HBM((slot_count, width), BF16),
        in_specs=[vmem, hbm],
        out_specs=hbm,
        scratch_shapes=[
            pltpu.VMEM(table.shape, BF16),
            pltpu.VMEM((slot_count, width), BF16),
            pltpu.SemaphoreType.DMA((5,)),
        ],
        compiler_params=params(),
        name="select",
    )(asked, *in_hbm(table))
    fetched = exchange(rows.reshape(owners, capacity, width)).reshape(slot_count, width)
    side_far = flip(side, "ctx", count // 2)
    side_mate = flip(side, "ctx", 1)
    side_blocks = gather_blocks(side, "ctx", {1: side_mate, count // 2: after(side_far, rows)})
    index = lax.axis_index("ctx").astype(jnp.int32) ^ jnp.arange(count, dtype=jnp.int32)
    prep_shapes = (
        jax.ShapeDtypeStruct((count, events, width), F32),
        jax.ShapeDtypeStruct((count, events, 128), F32),
        jax.ShapeDtypeStruct((count, 8, events), F32),
        jax.ShapeDtypeStruct((slot_count, events), BF16),
    )
    pinned = [pltpu.HBM(a.shape, a.dtype) for a in prep_shapes]
    spread, chosen = pl.pallas_call(
        places_kernel,
        out_shape=(pinned[3], pltpu.HBM((table.shape[0], slot_count), BF16)),
        in_specs=[vmem, vmem],
        out_specs=(vmem, vmem),
        compiler_params=params(),
        name="places",
    )(slots, after(asked, rows))
    prepared = pl.pallas_call(
        functools.partial(prep_kernel, count),
        out_shape=tuple(pinned[:3]),
        in_specs=[smem, hbm] + [vmem] * count,
        out_specs=(vmem,) * 3,
        scratch_shapes=[pltpu.VMEM(w_out.shape, BF16), pltpu.SemaphoreType.DMA((1,))],
        compiler_params=params(20),
        name="prep",
    )(index, *in_hbm(w_out), *side_blocks)
    prepared = in_hbm(*prepared, spread)
    fetched, prepared = lax.optimization_barrier((fetched, prepared))
    embedded = pl.pallas_call(
        embed_kernel,
        out_shape=jax.ShapeDtypeStruct((events, width), BF16),
        compiler_params=params(),
        name="embed",
    )(slots, fetched)
    emb_far = flip(embedded, "ctx", count // 2)
    emb_mate = flip(embedded, "ctx", 1)
    event_shape = jax.ShapeDtypeStruct((events, width), BF16)
    early = pl.pallas_call(
        early_kernel,
        out_shape=(
            jax.ShapeDtypeStruct((2, events, 4 * width), BF16),
            jax.ShapeDtypeStruct((2, events, width), F32),
            jax.ShapeDtypeStruct((2, events, width), BF16),
            jax.ShapeDtypeStruct((events, 4 * width), F32),
            jax.ShapeDtypeStruct((events, 4 * width), F32),
            event_shape,
        )
        + tuple(jax.ShapeDtypeStruct(a.shape, BF16) for a in (w_in, w_out))
        + prep_shapes
        + (jax.ShapeDtypeStruct(side.shape, BF16),),
        in_specs=[smem, vmem, vmem, vmem] + [hbm] * 6,
        out_specs=(vmem,) * 13,
        scratch_shapes=[pltpu.SemaphoreType.DMA((7,))],
        compiler_params=params(20),
        name="early",
    )(index, embedded, emb_mate, w_in, *in_hbm(w_out), *prepared, *in_hbm(side))
    emb_far = after(emb_far, early[0])
    proj_far = pl.pallas_call(
        project_kernel,
        out_shape=jax.ShapeDtypeStruct((events, 4 * width), BF16),
        compiler_params=params(),
        name="project_far",
    )(emb_far, early[6])
    emb_blocks = gather_blocks(embedded, "ctx", {1: emb_mate, count // 2: emb_far})
    layer_out, slot_grad = pl.pallas_call(
        functools.partial(late_kernel, count),
        out_shape=(event_shape, jax.ShapeDtypeStruct((slot_count, width), BF16)),
        in_specs=[smem] + [vmem] * (14 + count),
        out_specs=(vmem, vmem),
        scratch_shapes=[
            pltpu.VMEM((count, events, 4 * width), BF16),
            pltpu.VMEM((events, width), F32),
            pltpu.VMEM((count, events, width), BF16),
            pltpu.VMEM((events, 4 * width), F32),
            pltpu.SemaphoreType.DMA((5,)),
        ],
        compiler_params=params(28),
        name="late",
    )(index, *emb_blocks, proj_far, *early)
    returned = exchange(slot_grad.reshape(owners, capacity, width)).reshape(slot_count, width)
    row_grad = pl.pallas_call(
        collect_kernel,
        out_shape=pltpu.HBM(table.shape, F32),
        in_specs=[vmem, vmem],
        out_specs=hbm,
        scratch_shapes=[pltpu.VMEM(table.shape, F32), pltpu.SemaphoreType.DMA((2,))],
        compiler_params=params(),
        name="collect",
    )(chosen, returned)
    return layer_out, row_grad


def solution(mesh):
    rows = P(("table", "ctx"), None)
    return jax.shard_map(
        local,
        mesh=mesh,
        in_specs=(rows, rows, rows, P("table", "ctx"), P(), P(), rows),
        out_specs=(rows, rows),
        check_vma=False,
    )
```
